32 devices in a mesh: dp: 16 (over z, y, x), outer: 2 (over core).
Axes of the slice: x: 2, y: 2, z: 4, core: 2. Of those that a mesh axis runs over, the one named last changes fastest.
Arguments:
- tokens: bfloat16 [64, 128, 2048], P(('dp', 'outer')), may hold values from -6 to 6
- starts: int32 [64, 128], P(('dp', 'outer')), may hold values 0 or 1
- w_query: bfloat16 [2048, 2048], P(('dp', 'outer')), may hold values from -0.125 to 0.125
- w_key: bfloat16 [2048, 2048], P(('dp', 'outer')), may hold values from -0.125 to 0.125
- w_value: bfloat16 [2048, 2048], P(('dp', 'outer')), may hold values from -0.125 to 0.125
- w_gate_out: bfloat16 [2048, 2048], P(('dp', 'outer')), may hold values from -0.125 to 0.125
- w_out: bfloat16 [2048, 2048], P(('dp', 'outer')), may hold values from -0.25 to 0.25
- w_forget_down: bfloat16 [2048, 16], P(('dp', 'outer')), may hold values from -0.125 to 0.125
- w_forget_up: bfloat16 [16, 256], P(None, ('dp', 'outer')), may hold values from -3 to 3
- norm_attn: bfloat16 [2048], P(('dp', 'outer')), may hold values from 0.5 to 1.5
- norm_head: bfloat16 [512], P(('dp', 'outer')), may hold values from 0.5 to 1.5
- norm_mlp: bfloat16 [2048], P(('dp', 'outer')), may hold values from 0.5 to 1.5
- w_gate: bfloat16 [2048, 5632], P(('dp', 'outer')), may hold values from -0.125 to 0.125
- w_up: bfloat16 [2048, 5632], P(('dp', 'outer')), may hold values from -0.125 to 0.125
- w_down: bfloat16 [5632, 2048], P(('dp', 'outer')), may hold values from -0.15625 to 0.15625
- cotangent: bfloat16 [64, 128, 2048], P(('dp', 'outer')), may hold values from -6 to 6
Outputs:
- mixed: bfloat16 [64, 128, 2048], P(('dp', 'outer'))
- tokens_grad: bfloat16 [64, 128, 2048], P(('dp', 'outer'))
- grad_query: float32 [2048, 2048], P(('dp', 'outer'))
- grad_key: float32 [2048, 2048], P(('dp', 'outer'))
- grad_value: float32 [2048, 2048], P(('dp', 'outer'))
- grad_gate_out: float32 [2048, 2048], P(('dp', 'outer'))
- grad_out: float32 [2048, 2048], P(('dp', 'outer'))
- grad_forget_down: float32 [2048, 16], P(('dp', 'outer'))
- grad_forget_up: float32 [16, 256], P(None, ('dp', 'outer'))
- grad_norm_attn: float32 [2048], P(('dp', 'outer'))
- grad_norm_head: float32 [512], P(('dp', 'outer'))
- grad_norm_mlp: float32 [2048], P(('dp', 'outer'))
- grad_gate: float32 [2048, 5632], P(('dp', 'outer'))
- grad_up: float32 [2048, 5632], P(('dp', 'outer'))
- grad_down: float32 [5632, 2048], P(('dp', 'outer'))
The draws below stay inside these ranges and needn't reach their ends.
All inputs are finite; a program needn't handle non-finite values. No bound on the sum of `starts` on one device may be relied on, other than what follows from the above.
Results may differ from the reference program's by a relative error of at most 0.015.
Values may be sent and summed in bfloat16 or wider, within the bound.
A program may use at most 512 MiB of HBM per device.

```python
import jax
import jax.numpy as jnp
from jax import lax

HEADS = 4
HEAD = 512
D = 2048
SLOTS = 64
RANK = 16
FF = 5632
SEQ = 128
SEQUENCES = 64


def set_ends(entries, key, least, largest):
    spot = [jax.random.randint(jax.random.fold_in(key, axis), (), 0, length) for axis, length in enumerate(entries.shape)]
    main_axis = entries.shape.index(max(entries.shape))
    neighbour = spot[:main_axis] + [(spot[main_axis] + 1) % entries.shape[main_axis]] + spot[main_axis + 1:]
    return entries.at[tuple(spot)].set(least).at[tuple(neighbour)].set(largest)


def block_levels(rng, extent, cuts, least, top_value):
    factor_of, own = 1.0, jax.random.fold_in(rng, 6)
    for dim, blocks in cuts:
        heights = jnp.exp(jax.random.uniform(jax.random.fold_in(own, dim), (blocks,), jnp.float32, least / len(cuts), top_value / len(cuts)))
        factor_of = factor_of * jnp.repeat(heights, extent[dim] // blocks).reshape([-1 if axis == dim else 1 for axis in range(len(extent))])
    return factor_of


def centred(own_key, extent, scale, reach, split=(), kind=jnp.bfloat16):
    values = scale * jax.random.normal(own_key, extent, jnp.float32)
    if split:
        values = values * block_levels(own_key, extent, split, -0.22, 0.18)
    return jnp.clip(values, -reach, reach).astype(kind)


def setup_inputs(seed: int = 0) -> dict:
    seeds = jax.random.split(jax.random.key(seed), 17)
    tokens = centred(seeds[0], (SEQUENCES, SEQ, D), 1.0, 6.0, ((0, 32),))
    starts = set_ends((jax.random.randint(seeds[1], (SEQUENCES, SEQ), 0, 32) < 1).astype(jnp.int32), jax.random.fold_in(seeds[1], 1), 0, 1)
    w_query = centred(seeds[2], (D, D), D ** -0.5, 0.125, ((0, 32),))
    w_key = centred(seeds[3], (D, D), D ** -0.5, 0.125, ((0, 32),))
    w_value = centred(seeds[4], (D, D), D ** -0.5, 0.125, ((0, 32),))
    w_gate_out = centred(seeds[5], (D, D), D ** -0.5, 0.125, ((0, 32),))
    w_out = centred(seeds[6], (D, D), (D // 4) ** -0.5, 0.25, ((0, 32),))
    w_forget_down = centred(seeds[7], (D, RANK), D ** -0.5, 0.125, ((0, 32),))
    w_forget_up = centred(seeds[8], (RANK, HEADS * SLOTS), (RANK // 4) ** -0.5, 3.0, ((1, 32),))
    norm_attn = jnp.clip(1.0 + 0.1 * jax.random.normal(seeds[9], (D,), jnp.float32), 0.5, 1.5).astype(jnp.bfloat16)
    norm_head = jnp.clip(1.0 + 0.1 * jax.random.normal(seeds[10], (HEAD,), jnp.float32), 0.5, 1.5).astype(jnp.bfloat16)
    norm_mlp = jnp.clip(1.0 + 0.1 * jax.random.normal(seeds[11], (D,), jnp.float32), 0.5, 1.5).astype(jnp.bfloat16)
    w_gate = centred(seeds[12], (D, FF), D ** -0.5, 0.125, ((0, 32),))
    w_up = centred(seeds[13], (D, FF), D ** -0.5, 0.125, ((0, 32),))
    w_down = centred(seeds[14], (FF, D), (FF // 4) ** -0.5, 0.15625, ((0, 32),))
    cotangent = centred(seeds[15], (SEQUENCES, SEQ, D), 1.0, 6.0, ((0, 32),))
    return {"tokens": tokens, "starts": starts, "w_query": w_query, "w_key": w_key, "w_value": w_value, "w_gate_out": w_gate_out, "w_out": w_out, "w_forget_down": w_forget_down, "w_forget_up": w_forget_up, "norm_attn": norm_attn, "norm_head": norm_head, "norm_mlp": norm_mlp, "w_gate": w_gate, "w_up": w_up, "w_down": w_down, "cotangent": cotangent}


@jax.custom_vjp
def low(v):
    return lax.optimization_barrier(v.astype(jnp.bfloat16)).astype(jnp.float32)

@jax.custom_vjp
def low_back(v):
    return v

def low_keep(v):
    return (low(v), None)

def low_pass(kept, grad):
    return (grad,)

def back_keep(v):
    return (v, None)

def back_low(kept, grad):
    return (low(grad),)
low.defvjp(low_keep, low_pass)
low_back.defvjp(back_keep, back_low)

def swish_fn(values_in):
    return values_in * jax.nn.sigmoid(values_in)

def rms_norm(values_in, gain_vec):
    return values_in * lax.rsqrt(lax.optimization_barrier(jnp.mean(values_in * values_in, axis=-1, keepdims=True)) + 1e-06) * gain_vec

def mixer_seq(query_pre, key_pre, value_pre, forget_pre, doc_starts):
    seq_len = query_pre.shape[0]
    highest = lax.Precision.HIGHEST
    query_feat = low(swish_fn(query_pre)).reshape(seq_len, HEADS, HEAD)
    key_feat = low(swish_fn(key_pre)).reshape(seq_len, HEADS, HEAD)
    value_feat = low(value_pre).reshape(seq_len, HEADS, HEAD)
    log_forget = jax.nn.log_sigmoid(forget_pre.reshape(seq_len, HEADS, SLOTS)) / 8.0
    log_total = jnp.cumsum(log_forget, axis=0)
    doc_ids = jnp.cumsum(doc_starts)
    position = jnp.arange(seq_len)
    same_doc = (doc_ids[:, None] == doc_ids[None, :]) & (position[None, :] <= position[:, None])
    same_doc = same_doc[:, :, None, None]
    log_gap = log_total[:, None] - log_total[None, :]
    weight = jnp.where(same_doc, jnp.exp(jnp.where(same_doc, log_gap, 0.0)), 0.0) * (1.0 - jnp.exp(log_forget))[None]
    inner_prod = low_back(jnp.einsum('thd,jhd->htj', query_feat, key_feat, precision=highest) * HEAD ** (-0.5))
    scores = jnp.einsum('tjhm,htj->thm', weight, inner_prod, precision=highest)
    slot_probs = jax.nn.softmax(scores, axis=-1)
    mixing = low(jnp.einsum('thm,tjhm->htj', slot_probs, weight, precision=highest))
    output = jnp.einsum('htj,jhd->thd', mixing, value_feat, precision=highest)
    return low_back(output.reshape(seq_len, HEADS * HEAD))

def head_gate(head_out, gate_pre, gain_vec):
    token_count = head_out.shape[0]
    normed = rms_norm(head_out.reshape(token_count, HEADS, HEAD), gain_vec).reshape(token_count, HEADS * HEAD)
    return normed * swish_fn(gate_pre)

def matmul_hi(left, right):
    return jnp.dot(left, right, precision=lax.Precision.HIGHEST, preferred_element_type=jnp.float32)

def reference(tokens, starts, w_query, w_key, w_value, w_gate_out, w_out, w_forget_down, w_forget_up, norm_attn, norm_head, norm_mlp, w_gate, w_up, w_down, cotangent):
    seq_count, seq_len, model_width = tokens.shape

    def layer_fn(inputs, wq_full, wk_full, wv_full, wg_full, wo_full, wfd_full, wfu_full, gain_attn, gain_head, gain_mlp, wgate_full, wup_full, wdown_full):
        flat_rows = inputs.reshape(seq_count * seq_len, model_width)
        normed_in = low(rms_norm(flat_rows, gain_attn))
        query_pre = low_back(matmul_hi(normed_in, wq_full))
        key_pre = low_back(matmul_hi(normed_in, wk_full))
        value_pre = low_back(matmul_hi(normed_in, wv_full))
        gate_pre = low_back(matmul_hi(normed_in, wg_full))
        forget_low = low(low_back(matmul_hi(normed_in, wfd_full)))
        forget_pre = low_back(matmul_hi(forget_low, wfu_full))

        def one_seq(pieces):
            return mixer_seq(*pieces)
        head_out = lax.map(jax.checkpoint(one_seq), (query_pre.reshape(seq_count, seq_len, -1), key_pre.reshape(seq_count, seq_len, -1), value_pre.reshape(seq_count, seq_len, -1), forget_pre.reshape(seq_count, seq_len, -1), starts))
        head_out = head_out.reshape(seq_count * seq_len, -1)
        attn_act = low(head_gate(head_out, gate_pre, gain_head))
        resid = flat_rows + low_back(matmul_hi(attn_act, wo_full))
        normed_mlp = low(rms_norm(resid, gain_mlp))
        gate_val = low_back(matmul_hi(normed_mlp, wgate_full))
        up_val = low_back(matmul_hi(normed_mlp, wup_full))
        hidden = low(jax.nn.silu(gate_val) * up_val)
        result = resid + low_back(matmul_hi(hidden, wdown_full))
        return result.reshape(seq_count, seq_len, model_width)
    floats = [a.astype(jnp.float32) for a in (tokens, w_query, w_key, w_value, w_gate_out, w_out, w_forget_down, w_forget_up, norm_attn, norm_head, norm_mlp, w_gate, w_up, w_down)]
    result, back_fn = jax.vjp(layer_fn, *floats)
    gradients = back_fn(cotangent.astype(jnp.float32))
    return (result.astype(jnp.bfloat16), gradients[0].astype(jnp.bfloat16), gradients[1], gradients[2], gradients[3], gradients[4], gradients[5], gradients[6], gradients[7], gradients[8], gradients[9], gradients[10], gradients[11], gradients[12], gradients[13])
```

```python
import jax
import jax.numpy as jnp
from jax import lax
from jax.sharding import Mesh, PartitionSpec as P

HEADS = 4
HEAD = 512
SLOTS = 64
TP = 4
ALL = ("z", "t", "c")
ZC = ("z", "c")
F32 = jnp.float32
BF16 = jnp.bfloat16


def swish_fn(v):
    return v * jax.nn.sigmoid(v)


def rms_norm(v, gain):
    return v * lax.rsqrt(jnp.mean(v * v, axis=-1, keepdims=True) + 1e-06) * gain


def slot_seq(inner_prod, forget_pre, doc_ids):
    seq_len = forget_pre.shape[0]
    highest = lax.Precision.HIGHEST
    log_forget = jax.nn.log_sigmoid(forget_pre) / 8.0
    log_total = jnp.cumsum(log_forget, axis=0)
    position = jnp.arange(seq_len)
    same_doc = (doc_ids[:, None] == doc_ids[None, :]) & (position[None, :] <= position[:, None])
    same_doc = same_doc[:, :, None]
    log_gap = log_total[:, None] - log_total[None, :]
    weight = (
        jnp.where(same_doc, jnp.exp(jnp.where(same_doc, log_gap, 0.0)), 0.0)
        * (1.0 - jnp.exp(log_forget))[None]
    )
    scores = jnp.einsum("tjm,tj->tm", weight, inner_prod, precision=highest)
    probs = jax.nn.softmax(scores, axis=-1)
    return jnp.einsum("tm,tjm->tj", probs, weight, precision=highest)


def head_gate(head_out, gate_pre, gain):
    return rms_norm(head_out, gain) * swish_fn(gate_pre)


def swiglu(gate_val, up_val):
    return jax.nn.silu(gate_val) * up_val


def dot(left, right):
    return lax.dot_general(left, right, (((1,), (0,)), ((), ())), preferred_element_type=F32)


def dot_nt(left, right):
    return lax.dot_general(left, right, (((1,), (1,)), ((), ())), preferred_element_type=F32)


def dot_tn(left, right):
    return lax.dot_general(left, right, (((0,), (0,)), ((), ())), preferred_element_type=F32)


def send_t(x, step):
    return lax.ppermute(x, "t", [(i, i ^ step) for i in range(TP)])


def gather_t(x):
    return jnp.concatenate([x] + [send_t(x, k) for k in (1, 2, 3)], axis=0)


def scatter_t(x):
    parts = x.reshape(TP, x.shape[0] // TP, x.shape[1])
    total = parts[0]
    for k in (1, 2, 3):
        total = total + send_t(parts[k].astype(BF16), k).astype(F32)
    return total


def per_device(zs, cs, tokens, starts, w_query, w_key, w_value, w_gate_out, w_out, w_forget_down,
               w_forget_up, norm_attn, norm_head, norm_mlp, w_gate, w_up, w_down, cotangent):
    seqs, seq_len, D = tokens.shape
    n = zs * TP * cs
    rows = w_query.shape[0]
    ff_rows = w_down.shape[0]
    rank = w_forget_down.shape[1]
    fu_cols = w_forget_up.shape[1]
    mine = seqs * seq_len
    group = TP * mine
    t_idx = lax.axis_index("t")

    def to_k(v):
        return v.reshape(-1, zs, TP, cs, rows).transpose(0, 1, 3, 2, 4).reshape(-1, D)

    def from_k(v):
        return v.reshape(-1, zs, cs, TP, rows).transpose(0, 1, 3, 2, 4).reshape(-1, D)

    small = jnp.concatenate([w_forget_down.reshape(-1), w_forget_up.reshape(-1), norm_attn, norm_head, norm_mlp])
    small = lax.all_gather(small, ALL, axis=0, tiled=False).reshape(n, -1)
    cuts = [rows * rank, rank * fu_cols, norm_attn.shape[0], norm_head.shape[0], norm_mlp.shape[0]]
    at, pieces = 0, []
    for size in cuts:
        pieces.append(small[:, at:at + size])
        at += size
    wfd = to_k(pieces[0].reshape(D, rank).T).T
    wfu = pieces[1].reshape(n, rank, fu_cols).transpose(1, 0, 2).reshape(rank, n * fu_cols)
    wfu = lax.dynamic_slice_in_dim(wfu, t_idx * SLOTS, SLOTS, axis=1)
    gain_attn = pieces[2].reshape(-1).astype(F32)
    gain_head = pieces[3].reshape(-1).astype(F32)
    gain_mlp = pieces[4].reshape(-1).astype(F32)

    w4 = jnp.stack([w_query, w_key, w_value, w_gate_out]).reshape(4, rows, HEADS, HEAD)
    w4 = w4.transpose(2, 1, 0, 3)
    w4 = lax.all_to_all(w4, "t", 0, 0, tiled=True).reshape(TP * rows, 4 * HEAD)
    w4 = lax.all_gather(w4, ZC, axis=0, tiled=True)
    wo = lax.all_gather(w_out, ZC, axis=0, tiled=True)
    wo = lax.all_to_all(wo.reshape(TP, -1, D), "t", 0, 0, tiled=True)
    wo = wo.reshape(TP, zs // TP, cs, rows, D).transpose(1, 0, 2, 3, 4).reshape(HEAD, D)
    ff_cols = zs * cs * ff_rows

    def split_ff(w):
        w = w.reshape(rows, zs, TP, cs * ff_rows).transpose(2, 0, 1, 3)
        return w.reshape(TP, rows, ff_cols)

    w_gu = jnp.stack([split_ff(w_gate), split_ff(w_up)], axis=1)
    w_gu = lax.all_to_all(w_gu, "t", 0, 0, tiled=True)
    wg = lax.all_gather(w_gu[:, 0].reshape(TP * rows, ff_cols), ZC, axis=0, tiled=True)
    wu = lax.all_gather(w_gu[:, 1].reshape(TP * rows, ff_cols), ZC, axis=0, tiled=True)
    wd = lax.all_gather(w_down, ZC, axis=0, tiled=True)

    x = tokens.reshape(mine, D).astype(F32)
    normed_in, norm_in_back = jax.vjp(rms_norm, x, gain_attn)
    h = gather_t(to_k(normed_in.astype(BF16)))
    d_branch = gather_t(cotangent.reshape(mine, D))
    docs = gather_t(jnp.cumsum(starts, axis=1).astype(F32))
    pre = dot(h, w4)
    q_pre, k_pre, v_pre, g_pre = (pre[:, i * HEAD:(i + 1) * HEAD] for i in range(4))
    f_low = dot(h, wfd).astype(BF16)
    f_pre = dot(f_low, wfu)
    q, q_back = jax.vjp(swish_fn, q_pre)
    k, k_back = jax.vjp(swish_fn, k_pre)
    q = q.astype(BF16).reshape(-1, seq_len, HEAD)
    k = k.astype(BF16).reshape(-1, seq_len, HEAD)
    v = v_pre.astype(BF16).reshape(-1, seq_len, HEAD)
    inner = jnp.einsum("sth,sjh->stj", q, k, preferred_element_type=F32) * HEAD ** -0.5

    def slots(inner_in, forget_in):
        return jax.vmap(slot_seq)(inner_in, forget_in, docs)

    mixing, slot_back = jax.vjp(slots, inner, f_pre.reshape(-1, seq_len, SLOTS))
    mixing = mixing.astype(BF16)
    head_out = jnp.einsum("stj,sjh->sth", mixing, v, preferred_element_type=F32).reshape(group, HEAD)
    act, gate_back = jax.vjp(head_gate, head_out, g_pre, gain_head)
    act = act.astype(BF16)
    resid = x + scatter_t(dot(act, wo))
    normed_mlp, norm_mlp_back = jax.vjp(rms_norm, resid, gain_mlp)
    hm = gather_t(to_k(normed_mlp.astype(BF16)))
    gate_val = dot(hm, wg)
    up_val = dot(hm, wu)
    hidden, swiglu_back = jax.vjp(swiglu, gate_val, up_val)
    hidden = hidden.astype(BF16)
    mixed = (resid + scatter_t(dot(hidden, wd))).astype(BF16)

    g_down = dot_tn(hidden, d_branch).astype(BF16)
    d_gate, d_up = swiglu_back(dot_nt(d_branch, wd))
    d_gate = d_gate.astype(BF16)
    d_up = d_up.astype(BF16)
    g_gate = dot_tn(hm, d_gate).astype(BF16)
    g_up = dot_tn(hm, d_up).astype(BF16)

    def sum_zc(v):
        return lax.psum_scatter(v, ZC, scatter_dimension=0, tiled=True)

    g_down = sum_zc(g_down).astype(F32)
    g_gate = sum_zc(g_gate).reshape(TP, rows, ff_cols)
    g_up = sum_zc(g_up).reshape(TP, rows, ff_cols)
    d_hm = from_k(scatter_t(dot_nt(d_gate, wg) + dot_nt(d_up, wu)))
    d_resid, g_norm_mlp = norm_mlp_back(d_hm)
    d_resid = d_resid + cotangent.reshape(mine, D).astype(F32)

    d_attn = gather_t(d_resid.astype(BF16))
    g_out = dot_tn(act, d_attn).astype(BF16)
    d_head, d_g, g_norm_head = gate_back(dot_nt(d_attn, wo))
    d_head = d_head.astype(BF16).reshape(-1, seq_len, HEAD)
    d_mixing = jnp.einsum("sth,sjh->stj", d_head, v, preferred_element_type=F32)
    d_v = jnp.einsum("stj,sth->sjh", mixing, d_head, preferred_element_type=F32).reshape(group, HEAD)
    d_inner, d_f = slot_back(d_mixing)
    d_inner = d_inner.astype(BF16)
    d_q = jnp.einsum("stj,sjh->sth", d_inner, k, preferred_element_type=F32) * HEAD ** -0.5
    d_k = jnp.einsum("stj,sth->sjh", d_inner, q, preferred_element_type=F32) * HEAD ** -0.5
    (d_q,) = q_back(d_q.reshape(group, HEAD))
    (d_k,) = k_back(d_k.reshape(group, HEAD))
    d_pre = jnp.concatenate([d_q.astype(BF16), d_k.astype(BF16), d_v.astype(BF16), d_g.astype(BF16)], axis=1)
    d_f = d_f.reshape(group, SLOTS).astype(BF16)
    g4 = dot_tn(h, d_pre).astype(BF16)
    g_fu = dot_tn(f_low, d_f)
    d_low = dot_nt(d_f, wfu).astype(BF16)
    g_fd = dot_tn(h, d_low)
    g4 = sum_zc(g4)
    d_h = from_k(scatter_t(dot_nt(d_pre, w4) + dot_nt(d_low, wfd)))
    d_x, g_norm_attn = norm_in_back(d_h)
    tokens_grad = (d_resid + d_x).astype(BF16)

    g_out = g_out.reshape(zs // TP, TP, cs * rows, D).transpose(1, 0, 2, 3)
    g_out = lax.all_to_all(g_out, "t", 0, 0, tiled=True)
    g_out = sum_zc(g_out.reshape(zs * cs * rows, D)).astype(F32)
    g4 = lax.all_to_all(g4.reshape(TP, rows, 4, HEAD), "t", 0, 0, tiled=True)
    g4 = g4.transpose(2, 1, 0, 3).reshape(4, rows, D).astype(F32)
    g_gu = lax.all_to_all(jnp.stack([g_gate, g_up], axis=1), "t", 0, 0, tiled=True)
    g_gu = g_gu.reshape(TP, 2, rows, zs, cs * ff_rows).transpose(1, 2, 3, 0, 4)
    g_gu = g_gu.reshape(2, rows, n * ff_rows).astype(F32)

    fu_full = lax.dynamic_update_slice_in_dim(jnp.zeros((rank, n * fu_cols), F32), g_fu, t_idx * SLOTS, axis=1)
    flat = jnp.concatenate([
        from_k(g_fd.T).T.reshape(n, -1),
        fu_full.reshape(rank, n, fu_cols).transpose(1, 0, 2).reshape(n, -1),
        g_norm_attn.reshape(n, -1),
        g_norm_head.reshape(n, -1),
        g_norm_mlp.reshape(n, -1),
    ], axis=1)
    flat = lax.psum_scatter(flat, ALL, scatter_dimension=0, tiled=False)
    at, pieces = 0, []
    for size in cuts:
        pieces.append(flat[at:at + size])
        at += size
    return (
        mixed.reshape(tokens.shape),
        tokens_grad.reshape(tokens.shape),
        g4[0], g4[1], g4[2], g4[3],
        g_out,
        pieces[0].reshape(rows, rank),
        pieces[1].reshape(rank, fu_cols),
        pieces[2],
        pieces[3],
        pieces[4],
        g_gu[0], g_gu[1],
        g_down,
    )


def solution(mesh):
    cs = mesh.shape["outer"]
    zs = mesh.shape["dp"] // TP
    grid = Mesh(mesh.devices.reshape(zs, TP, cs), ALL)
    whole, row, vec = P(ALL, None, None), P(ALL, None), P(ALL)
    cols = P(None, ALL)

    def body(*args):
        return per_device(zs, cs, *args)

    return jax.shard_map(
        body,
        mesh=grid,
        in_specs=(whole, row, row, row, row, row, row, row, cols, vec, vec, vec, row, row, row, whole),
        out_specs=(whole, whole, row, row, row, row, row, row, cols, vec, vec, vec, row, row, row),
        check_vma=False,
    )
```

```python
import functools

import jax
import jax.numpy as jnp
from jax import lax
from jax.experimental import pallas as pl
from jax.experimental.pallas import tpu as pltpu
from jax.sharding import Mesh, PartitionSpec as P

HEADS = 4
HEAD = 512
SLOTS = 64
TP = 4
ALL = ("z", "t", "c")
F32 = jnp.float32
BF16 = jnp.bfloat16
SPAN = 80.0


def mm(a, b, dims):
    return lax.dot_general(a, b, (dims, ((), ())), preferred_element_type=F32)


NN, NT, TN = ((1,), (0,)), ((1,), (1,)), ((0,), (0,))


def split(a):
    high = a.astype(BF16)
    return high, (a - high.astype(F32)).astype(BF16)


def mm3(a, b, dims):
    ah, al = split(a)
    bh, bl = split(b)
    return mm(ah, bh, dims) + (mm(ah, bl, dims) + mm(al, bh, dims))


def mm_exact(mask, b, dims):
    b1, rest = split(b)
    b2 = rest
    b3 = (b - b1.astype(F32) - b2.astype(F32)).astype(BF16)
    return mm(mask, b1, dims) + (mm(mask, b2, dims) + mm(mask, b3, dims))


def swish_parts(v):
    sig = 1.0 / (1.0 + jnp.exp(-v))
    return v * sig, sig * (1.0 + v * (1.0 - sig))


def gates(f_low, wfu):
    f_pre = mm(f_low, wfu, NN)
    soft = jnp.log(1.0 + jnp.exp(-jnp.abs(f_pre)))
    log_f = (jnp.minimum(f_pre, 0.0) - soft) * 0.125
    return f_pre, log_f


def lower_tri(n, kind=BF16):
    rows = lax.broadcasted_iota(jnp.int32, (n, n), 0)
    cols = lax.broadcasted_iota(jnp.int32, (n, n), 1)
    return rows >= cols


def column(a, j):
    picked = lax.broadcasted_iota(jnp.int32, a.shape, 1) == j
    return jnp.sum(jnp.where(picked, a, 0.0), axis=1, keepdims=True)


def row(a, j):
    picked = lax.broadcasted_iota(jnp.int32, a.shape, 0) == j
    return jnp.sum(jnp.where(picked, a, 0.0), axis=0, keepdims=True)


def gap(total, j):
    return jnp.exp(jnp.minimum(total - row(total, j), 0.0))


def softmax(scores):
    e = jnp.exp(scores - jnp.max(scores, axis=1, keepdims=True))
    return e / jnp.sum(e, axis=1, keepdims=True)


def far_near(total):
    mid = 0.5 * total[-1:]
    return jnp.exp(total - mid), jnp.exp(mid - total)


def sum_over_j(mats, total, unit, fast, dest):
    n = total.shape[0]

    @pl.when(fast)
    def _():
        near, far = far_near(total)
        got = mm3(jnp.concatenate(mats, axis=0), far * unit, NN)
        for i, d in enumerate(dest):
            d[...] = got[i * n:(i + 1) * n] * near

    @pl.when(jnp.logical_not(fast))
    def _():
        for d in dest:
            d[...] = jnp.zeros_like(total)

        def step(j, _):
            e = gap(total, j) * row(unit, j)
            for d, m in zip(dest, mats):
                d[...] += column(m, j) * e
            return 0

        lax.fori_loop(0, n, step, 0)


def sum_over_m(probs, total, unit, fast, dest):
    n = total.shape[0]

    @pl.when(fast)
    def _():
        near, far = far_near(total)
        got = mm3(jnp.concatenate([p * near for p in probs], axis=0), far * unit, NT)
        for i, d in enumerate(dest):
            d[...] = got[i * n:(i + 1) * n]

    @pl.when(jnp.logical_not(fast))
    def _():
        cols = lax.broadcasted_iota(jnp.int32, (n, n), 1)

        def step(j, _):
            e = gap(total, j) * row(unit, j)
            for d, p in zip(dest, probs):
                d[...] = jnp.where(cols == j, jnp.sum(p * e, axis=1, keepdims=True), d[...])
            return 0

        lax.fori_loop(0, n, step, 0)


def sum_over_t(mats, probs, total, fast, dest):
    n = total.shape[0]

    @pl.when(fast)
    def _():
        near, far = far_near(total)
        got = mm3(jnp.concatenate(mats, axis=0), jnp.concatenate([p * near for p in probs], axis=0), TN)
        dest[...] = got * far

    @pl.when(jnp.logical_not(fast))
    def _():
        rows = lax.broadcasted_iota(jnp.int32, total.shape, 0)

        def step(j, _):
            e = gap(total, j)
            s = sum(column(m, j) * p for m, p in zip(mats, probs))
            dest[...] = jnp.where(rows == j, jnp.sum(s * e, axis=0, keepdims=True), dest[...])
            return 0

        lax.fori_loop(0, n, step, 0)


def mixer_forward(pre_ref, f_low_ref, wfu_ref, doc_col_ref, doc_row_ref, score_ref, mix_ref):
    pre = pre_ref[...]
    q, q_slope = swish_parts(pre[:, :HEAD])
    k, k_slope = swish_parts(pre[:, HEAD:2 * HEAD])
    q, k, v = q.astype(BF16), k.astype(BF16), pre[:, 2 * HEAD:3 * HEAD].astype(BF16)
    n = q.shape[0]
    tri = lower_tri(n)
    keep = tri & (doc_col_ref[0] == doc_row_ref[0])
    inner = jnp.where(keep, mm(q, k, NT) * HEAD ** -0.5, 0.0)
    f_pre, log_f = gates(f_low_ref[...], wfu_ref[...])
    total = mm_exact(tri.astype(BF16), log_f, NN)
    unit = 1.0 - jnp.exp(log_f)
    fast = jnp.min(total[-1:]) > -SPAN
    return q, k, v, q_slope, k_slope, keep, inner, f_pre, log_f, total, unit, fast


def forward_kernel(pre_ref, f_low_ref, wfu_ref, gain_ref, doc_col_ref, doc_row_ref, act_ref, score_ref, mix_ref):
    q, k, v, _, _, keep, inner, _, _, total, unit, fast = mixer_forward(
        pre_ref, f_low_ref, wfu_ref, doc_col_ref, doc_row_ref, score_ref, mix_ref)
    sum_over_j([inner], total, unit, fast, [score_ref])
    probs = softmax(score_ref[...])
    sum_over_m([probs], total, unit, fast, [mix_ref])
    mixing = jnp.where(keep, mix_ref[...], 0.0).astype(BF16)
    out = mm(mixing, v, NN)
    scale = lax.rsqrt(jnp.mean(out * out, axis=1, keepdims=True) + 1e-06)
    gate, _ = swish_parts(pre_ref[:, 3 * HEAD:])
    act_ref[...] = (out * scale * gain_ref[...] * gate).astype(BF16)


def backward_kernel(pre_ref, f_low_ref, wfu_ref, gain_ref, doc_col_ref, doc_row_ref, d_act_ref,
                    d_pre_ref, d_f_ref, d_low_ref, g_gain_ref,
                    score_ref, d_p_ref, mix_ref, d_inner_ref, k_ref):
    q, k, v, q_slope, k_slope, keep, inner, f_pre, log_f, total, unit, fast = mixer_forward(
        pre_ref, f_low_ref, wfu_ref, doc_col_ref, doc_row_ref, score_ref, mix_ref)
    sum_over_j([inner], total, unit, fast, [score_ref])
    scores = score_ref[...]
    probs = softmax(scores)
    sum_over_m([probs], total, unit, fast, [mix_ref])
    mixing = jnp.where(keep, mix_ref[...], 0.0).astype(BF16)
    out = mm(mixing, v, NN)

    scale = lax.rsqrt(jnp.mean(out * out, axis=1, keepdims=True) + 1e-06)
    gain = gain_ref[...]
    gate, gate_slope = swish_parts(pre_ref[:, 3 * HEAD:])
    d_act = d_act_ref[...].astype(F32)
    d_gate = d_act * out * scale * gain * gate_slope
    d_norm = d_act * gate
    g_gain = jnp.sum(d_norm * out * scale, axis=0, keepdims=True)

    @pl.when(pl.program_id(0) == 0)
    def _():
        g_gain_ref[...] = jnp.zeros_like(g_gain_ref)

    g_gain_ref[...] += g_gain
    d_norm = d_norm * gain
    d_out = scale * (d_norm - out * (scale * scale) * jnp.mean(d_norm * out, axis=1, keepdims=True))
    d_out = d_out.astype(BF16)

    d_mix = jnp.where(keep, mm(d_out, v, NT), 0.0)
    d_v = mm(mixing, d_out, TN)
    sum_over_j([d_mix], total, unit, fast, [d_p_ref])
    d_p = d_p_ref[...]
    d_score = probs * (d_p - jnp.sum(probs * d_p, axis=1, keepdims=True))
    sum_over_m([d_score], total, unit, fast, [d_inner_ref])
    d_inner = jnp.where(keep, d_inner_ref[...], 0.0).astype(BF16)
    sum_over_t([d_mix, inner], [probs, d_score], total, fast, k_ref)
    k_sum = k_ref[...]
    d_total = probs * d_p + d_score * scores - unit * k_sum
    n = q.shape[0]
    tri = lower_tri(n).astype(BF16)
    d_log = mm_exact(tri, d_total, TN) - jnp.exp(log_f) * k_sum
    d_f = (d_log * (0.125 / (1.0 + jnp.exp(f_pre)))).astype(BF16)
    d_f_ref[...] = d_f
    d_low_ref[...] = mm(d_f, wfu_ref[...], NT).astype(BF16)
    d_q = mm(d_inner, k, NN) * HEAD ** -0.5
    d_k = mm(d_inner, q, TN) * HEAD ** -0.5
    d_pre_ref[:, :HEAD] = (d_q * q_slope).astype(BF16)
    d_pre_ref[:, HEAD:2 * HEAD] = (d_k * k_slope).astype(BF16)
    d_pre_ref[:, 2 * HEAD:3 * HEAD] = d_v.astype(BF16)
    d_pre_ref[:, 3 * HEAD:] = d_gate.astype(BF16)


def mixer_specs(length, rank):
    return [
        pl.BlockSpec((length, 4 * HEAD), lambda i: (i, 0)),
        pl.BlockSpec((length, rank), lambda i: (i, 0)),
        pl.BlockSpec((rank, SLOTS), lambda i: (0, 0)),
        pl.BlockSpec((1, HEAD), lambda i: (0, 0)),
        pl.BlockSpec((1, length, 1), lambda i: (i, 0, 0)),
        pl.BlockSpec((1, 1, length), lambda i: (i, 0, 0)),
    ]


def slots_forward(pre, f_low, wfu, gain, docs):
    count, length = docs.shape
    tm = pltpu.VMEM((length, SLOTS), F32)
    tj = pltpu.VMEM((length, length), F32)
    return pl.pallas_call(
        forward_kernel,
        out_shape=jax.ShapeDtypeStruct((count * length, HEAD), BF16),
        grid=(count,),
        in_specs=mixer_specs(length, f_low.shape[1]),
        out_specs=pl.BlockSpec((length, HEAD), lambda i: (i, 0)),
        scratch_shapes=[tm, tj],
        compiler_params=pltpu.CompilerParams(vmem_limit_bytes=32 << 20),
        name="slots_forward",
    )(pre, f_low, wfu, gain, docs[:, :, None], docs[:, None, :])


def slots_backward(pre, f_low, wfu, gain, docs, d_act):
    count, length = docs.shape
    rank = f_low.shape[1]
    tm = pltpu.VMEM((length, SLOTS), F32)
    tj = pltpu.VMEM((length, length), F32)
    block = lambda width: pl.BlockSpec((length, width), lambda i: (i, 0))
    return pl.pallas_call(
        backward_kernel,
        out_shape=(
            jax.ShapeDtypeStruct((count * length, 4 * HEAD), BF16),
            jax.ShapeDtypeStruct((count * length, SLOTS), BF16),
            jax.ShapeDtypeStruct((count * length, rank), BF16),
            jax.ShapeDtypeStruct((1, HEAD), F32),
        ),
        grid=(count,),
        in_specs=mixer_specs(length, rank) + [block(HEAD)],
        out_specs=(block(4 * HEAD), block(SLOTS), block(rank), pl.BlockSpec((1, HEAD), lambda i: (0, 0))),
        scratch_shapes=[tm, tm, tj, tj, tm],
        compiler_params=pltpu.CompilerParams(vmem_limit_bytes=32 << 20),
        name="slots_backward",
    )(pre, f_low, wfu, gain, docs[:, :, None], docs[:, None, :], d_act)


def place(index, cs):
    return (index // (TP * cs), (index // cs) % TP, index % cs)


def greet_all(n, cs, me):
    barrier = pltpu.get_barrier_semaphore()

    def greet(step, _):
        pl.semaphore_signal(barrier, inc=1, device_id=place((me + step) % n, cs), device_id_type=pl.DeviceIdType.MESH)
        return 0

    lax.fori_loop(1, n, greet, 0)
    pl.semaphore_wait(barrier, n - 1)


def my_index(cs):
    return (lax.axis_index("z") * TP + lax.axis_index("t")) * cs + lax.axis_index("c")


def share_kernel(n, cs, x_ref, o_ref, send_sem, recv_sem):
    me = my_index(cs)
    greet_all(n, cs, me)

    def send(step, _):
        pltpu.make_async_remote_copy(
            src_ref=x_ref, dst_ref=o_ref.at[me], send_sem=send_sem, recv_sem=recv_sem,
            device_id=place((me + step) % n, cs), device_id_type=pl.DeviceIdType.MESH).start()
        return 0

    lax.fori_loop(1, n, send, 0)
    o_ref[me] = x_ref[...]
    others = o_ref.at[pl.ds(0, n - 1)]
    pltpu.make_async_copy(others, others, recv_sem).wait()
    pltpu.make_async_copy(others, others, send_sem).wait()


def share(x, n, cs):
    return pl.pallas_call(
        functools.partial(share_kernel, n, cs),
        out_shape=jax.ShapeDtypeStruct((n,) + x.shape, x.dtype),
        in_specs=[pl.BlockSpec(memory_space=pltpu.VMEM)],
        out_specs=pl.BlockSpec(memory_space=pltpu.VMEM),
        scratch_shapes=[pltpu.SemaphoreType.DMA, pltpu.SemaphoreType.DMA],
        compiler_params=pltpu.CompilerParams(collective_id=0, has_side_effects=True, vmem_limit_bytes=32 << 20),
        name="share_small",
    )(x)


def total_kernel(n, cs, x_ref, o_ref, got_ref, send_sem, recv_sem):
    me = my_index(cs)
    greet_all(n, cs, me)

    def send(step, _):
        peer = (me + step) % n
        pltpu.make_async_remote_copy(
            src_ref=x_ref.at[peer], dst_ref=got_ref.at[me], send_sem=send_sem, recv_sem=recv_sem,
            device_id=place(peer, cs), device_id_type=pl.DeviceIdType.MESH).start()
        return 0

    lax.fori_loop(1, n, send, 0)
    got_ref[me] = x_ref[me]
    others = got_ref.at[pl.ds(0, n - 1)]
    pltpu.make_async_copy(others, others, recv_sem).wait()
    pltpu.make_async_copy(others, others, send_sem).wait()
    o_ref[...] = jnp.sum(got_ref[...], axis=0)


def total_to_owner(x, n, cs):
    return pl.pallas_call(
        functools.partial(total_kernel, n, cs),
        out_shape=jax.ShapeDtypeStruct(x.shape[1:], x.dtype),
        in_specs=[pl.BlockSpec(memory_space=pltpu.VMEM)],
        out_specs=pl.BlockSpec(memory_space=pltpu.VMEM),
        scratch_shapes=[pltpu.VMEM(x.shape, x.dtype), pltpu.SemaphoreType.DMA, pltpu.SemaphoreType.DMA],
        compiler_params=pltpu.CompilerParams(collective_id=1, has_side_effects=True, vmem_limit_bytes=32 << 20),
        name="sum_small",
    )(x)


def pack_rows(parts, unit):
    flat = jnp.concatenate(parts, axis=-1)
    size = flat.shape[-1]
    padded = -(-size // (unit * 128)) * unit * 128
    flat = jnp.pad(flat, [(0, 0)] * (flat.ndim - 1) + [(0, padded - size)])
    return flat.reshape(flat.shape[:-1] + (padded // 128, 128))


def cut(flat, sizes):
    at, pieces = 0, []
    for size in sizes:
        pieces.append(flat[..., at:at + size])
        at += size
    return pieces


def send_t(x, step):
    return lax.ppermute(x, "t", [(i, i ^ step) for i in range(TP)])


def send_c(x):
    return lax.ppermute(x, "c", [(0, 1), (1, 0)])


def gather_t(x):
    half = x.shape[0] // 2
    one, two = send_t(x, 1), send_t(x, 2)
    three = [send_t(two[:half], 1), send_t(one[half:], 2)]
    return jnp.concatenate([x, one, two] + three, axis=0)


def scatter_t(x):
    count = x.shape[0] // TP
    half = count // 2
    p = [(x[k * count:k * count + half], x[k * count + half:(k + 1) * count]) for k in range(TP)]
    first = send_t(jnp.concatenate([p[1][0], p[3][0]], axis=0).astype(BF16), 1).astype(F32)
    second = send_t(jnp.concatenate([p[2][1], p[3][1]], axis=0).astype(BF16), 2).astype(F32)
    on_a = (p[2][0] + first[half:]).astype(BF16)
    on_b = (p[1][1] + second[half:]).astype(BF16)
    a = p[0][0] + first[:half] + send_t(on_a, 2).astype(F32)
    b = p[0][1] + second[:half] + send_t(on_b, 1).astype(F32)
    return jnp.concatenate([a, b], axis=0)


def swap_t(x):
    t = lax.axis_index("t")

    def block(a, j):
        return lax.dynamic_index_in_dim(a, j, 0, keepdims=False)

    got = jnp.stack([block(x, t)] + [send_t(block(x, t ^ k), k) for k in (1, 2, 3)])
    return jnp.stack([block(got, t ^ j) for j in range(TP)])


def dot(left, right):
    return mm(left, right, NN)


def dot_nt(left, right):
    return mm(left, right, NT)


def dot_tn(left, right):
    return mm(left, right, TN)


def rms_norm(v, gain):
    return v * lax.rsqrt(jnp.mean(v * v, axis=-1, keepdims=True) + 1e-06) * gain


def swiglu(gate_val, up_val):
    return jax.nn.silu(gate_val) * up_val


def per_device(zs, cs, tokens, starts, w_query, w_key, w_value, w_gate_out, w_out, w_forget_down,
               w_forget_up, norm_attn, norm_head, norm_mlp, w_gate, w_up, w_down, cotangent):
    seqs, seq_len, D = tokens.shape
    n = zs * TP * cs
    rows = w_query.shape[0]
    ff_rows = w_down.shape[0]
    rank = w_forget_down.shape[1]
    fu_cols = w_forget_up.shape[1]
    mine = seqs * seq_len
    half = D // cs
    t_idx = lax.axis_index("t")
    first_core = lax.axis_index("c") == 0

    def own_first(v, axis):
        a, b = (lax.index_in_dim(v, i, axis, keepdims=False) for i in range(2))
        return jnp.stack([jnp.where(first_core, a, b), jnp.where(first_core, b, a)], axis=axis)

    def to_k(v):
        v = v.reshape(-1, zs, TP, cs, rows).transpose(0, 3, 1, 2, 4)
        return own_first(v, 1).reshape(-1, D)

    def from_k(v):
        v = own_first(v.reshape(-1, cs, zs, TP, rows), 1)
        return v.transpose(0, 2, 3, 1, 4).reshape(-1, D)

    def gather_z(v):
        return lax.all_gather(v, "z", axis=0, tiled=True)

    def sum_z(v):
        return lax.psum_scatter(v, "z", scatter_dimension=0, tiled=True)

    docs = jnp.cumsum(starts, axis=1).astype(BF16)
    small = pack_rows([w_forget_down.reshape(-1), w_forget_up.reshape(-1), norm_attn, norm_head, norm_mlp,
                       docs.reshape(-1)], 16)
    sizes = [rows * rank, rank * fu_cols, norm_attn.shape[0], norm_head.shape[0], norm_mlp.shape[0]]
    small = share(small, n, cs).reshape(n, -1)
    pieces = cut(small, sizes + [mine])
    wfd = to_k(pieces[0].reshape(D, rank).T).T
    wfu = pieces[1].reshape(n, rank, fu_cols).transpose(1, 0, 2).reshape(rank, n * fu_cols)
    wfu = lax.dynamic_slice_in_dim(wfu, t_idx * SLOTS, SLOTS, axis=1)
    gain_attn = pieces[2].reshape(-1).astype(F32)
    gain_head = pieces[3].reshape(1, -1).astype(F32)
    gain_mlp = pieces[4].reshape(-1).astype(F32)
    all_docs = pieces[5].reshape(zs, TP, cs, mine)
    all_docs = lax.dynamic_index_in_dim(all_docs, lax.axis_index("z"), 0, keepdims=False)
    all_docs = lax.dynamic_index_in_dim(all_docs, lax.axis_index("c"), 1, keepdims=False)
    docs = jnp.concatenate([lax.dynamic_index_in_dim(all_docs, t_idx ^ k, 0) for k in range(TP)], axis=0)
    docs = docs.astype(F32).reshape(TP * seqs, seq_len)

    w4 = jnp.stack([w_query, w_key, w_value, w_gate_out]).reshape(4, rows, HEADS, HEAD)
    w4 = swap_t(w4.transpose(2, 1, 0, 3)).reshape(TP * rows, 4 * HEAD)
    w4 = gather_z(w4)
    w4 = jnp.concatenate([w4, send_c(w4)], axis=0)
    wo = swap_t(gather_z(w_out).reshape(TP, zs // TP, rows, D))
    wo = own_first(jnp.stack([wo, send_c(wo)]), 0)
    wo = wo.transpose(2, 1, 0, 3, 4).reshape(HEAD, D)

    middle = (ff_rows // 2 + 15) // 16 * 16
    parts = [(0, middle), (middle, ff_rows)]

    def ff_weights(low, high):
        width = zs * (high - low)

        def columns(w):
            w = w.reshape(rows, zs, TP, cs, ff_rows)[..., low:high].transpose(2, 0, 3, 1, 4)
            return own_first(w.reshape(TP, rows, cs, width), 2).reshape(TP, rows, cs * width)

        gu = swap_t(jnp.concatenate([columns(w_gate), columns(w_up)], axis=2))
        gu = gather_z(gu.reshape(TP * rows, 4 * width))
        other = send_c(gu)
        other = jnp.concatenate([other[:, i * width:(i + 1) * width] for i in (1, 0, 3, 2)], axis=1)
        gu = jnp.concatenate([gu, other], axis=0)
        down = gather_z(w_down[low:high])
        return gu, jnp.concatenate([down, send_c(down)], axis=0)

    ff = [ff_weights(*p) for p in parts]

    x = tokens.reshape(mine, D).astype(F32)
    normed_in, norm_in_back = jax.vjp(rms_norm, x, gain_attn)
    h = gather_t(to_k(normed_in.astype(BF16)))
    d_branch = gather_t(cotangent.reshape(mine, D))
    pre = dot(h, w4)
    f_low = dot(h, wfd).astype(BF16)
    act = slots_forward(pre, f_low, wfu, gain_head, docs)
    resid = x + scatter_t(dot(act, wo))
    normed_mlp, norm_mlp_back = jax.vjp(rms_norm, resid, gain_mlp)
    hm = gather_t(to_k(normed_mlp.astype(BF16)))

    branch = d_hm = 0.0
    gu_grads, down_grads = [], []
    for (low, high), (gu, down) in zip(parts, ff):
        width = zs * (high - low)
        pre_ff = dot(hm, gu)
        hidden, swiglu_back = jax.vjp(swiglu, pre_ff[:, :2 * width], pre_ff[:, 2 * width:])
        hidden = hidden.astype(BF16)
        branch = branch + dot(hidden, down)
        d_gate, d_up = swiglu_back(dot_nt(d_branch, down))
        d_gate, d_up = d_gate.astype(BF16), d_up.astype(BF16)
        d_gu = jnp.concatenate([d_gate, d_up], axis=1)
        d_gu_other = jnp.concatenate([d_gate[:, width:], d_gate[:, :width], d_up[:, width:], d_up[:, :width]], axis=1)
        got = send_c(dot_tn(hm[:, half:], d_gu_other).astype(BF16))
        g_gu = (dot_tn(hm[:, :half], d_gu) + got.astype(F32)).astype(BF16)
        got = send_c(dot_tn(hidden[:, width:], d_branch).astype(BF16))
        g_down = (dot_tn(hidden[:, :width], d_branch) + got.astype(F32)).astype(BF16)
        gu_grads.append(swap_t(sum_z(g_gu).reshape(TP, rows, 4 * width)))
        down_grads.append(sum_z(g_down))
        d_hm = d_hm + dot_nt(d_gu, gu)
    mixed = (resid + scatter_t(branch)).astype(BF16)
    d_resid, g_norm_mlp = norm_mlp_back(from_k(scatter_t(d_hm)))
    d_resid = d_resid + cotangent.reshape(mine, D).astype(F32)

    d_attn = gather_t(d_resid.astype(BF16))
    d_pre, d_f, d_low, g_norm_head = slots_backward(pre, f_low, wfu, gain_head, docs, dot_nt(d_attn, wo))
    g_out = dot_tn(act, d_attn).astype(BF16).reshape(zs // TP, TP, cs, rows, D)
    g_out = own_first(g_out, 2)
    got = send_c(g_out[:, :, 1])
    g_out = (g_out[:, :, 0].astype(F32) + got.astype(F32)).astype(BF16)
    g_out = sum_z(swap_t(g_out.transpose(1, 0, 2, 3)).reshape(zs * rows, D)).astype(F32)
    got = send_c(dot_tn(h[:, half:], d_pre).astype(BF16))
    g4 = (dot_tn(h[:, :half], d_pre) + got.astype(F32)).astype(BF16)
    g4 = swap_t(sum_z(g4).reshape(TP, rows, 4 * HEAD)).reshape(HEADS, rows, 4, HEAD)
    g4 = g4.transpose(2, 1, 0, 3).reshape(4, rows, D).astype(F32)
    g_fu = dot_tn(f_low, d_f)
    g_fd = dot_tn(h, d_low)
    d_h = from_k(scatter_t(dot_nt(d_pre, w4) + dot_nt(d_low, wfd)))
    d_x, g_norm_attn = norm_in_back(d_h)
    tokens_grad = (d_resid + d_x).astype(BF16)

    def to_columns(i):
        out = []
        for (low, high), g in zip(parts, gu_grads):
            width = zs * (high - low)
            g = g[:, :, 2 * i * width:2 * (i + 1) * width].astype(F32).reshape(TP, rows, cs, zs, high - low)
            out.append(own_first(g, 2).transpose(1, 3, 0, 2, 4))
        return jnp.concatenate(out, axis=-1).reshape(rows, n * ff_rows)

    g_down = jnp.concatenate(down_grads, axis=0).astype(F32)
    fu_full = lax.dynamic_update_slice_in_dim(jnp.zeros((rank, n * fu_cols), F32), g_fu, t_idx * SLOTS, axis=1)
    flat = pack_rows([
        from_k(g_fd.T).T.reshape(n, -1),
        fu_full.reshape(rank, n, fu_cols).transpose(1, 0, 2).reshape(n, -1),
        g_norm_attn.reshape(n, -1),
        g_norm_head.reshape(n, -1),
        g_norm_mlp.reshape(n, -1),
    ], 8)
    pieces = cut(total_to_owner(flat, n, cs).reshape(-1), sizes)
    return (
        mixed.reshape(tokens.shape),
        tokens_grad.reshape(tokens.shape),
        g4[0], g4[1], g4[2], g4[3],
        g_out,
        pieces[0].reshape(rows, rank),
        pieces[1].reshape(rank, fu_cols),
        pieces[2],
        pieces[3],
        pieces[4],
        to_columns(0), to_columns(1),
        g_down,
    )


def solution(mesh):
    cs = mesh.shape["outer"]
    zs = mesh.shape["dp"] // TP
    grid = Mesh(mesh.devices.reshape(zs, TP, cs), ALL)
    whole, row, vec = P(ALL, None, None), P(ALL, None), P(ALL)
    cols = P(None, ALL)

    def body(*args):
        return per_device(zs, cs, *args)

    return jax.shard_map(
        body,
        mesh=grid,
        in_specs=(whole, row, row, row, row, row, row, row, cols, vec, vec, vec, row, row, row, whole),
        out_specs=(whole, whole, row, row, row, row, row, row, cols, vec, vec, vec, row, row, row),
        check_vma=False,
    )
```

```python
import functools

import jax
import jax.numpy as jnp
from jax import lax
from jax.experimental import pallas as pl
from jax.experimental.pallas import tpu as pltpu
from jax.sharding import Mesh, PartitionSpec as P

HEADS = 4
HEAD = 512
SLOTS = 64
TP = 4
ALL = ("z", "t", "c")
F32 = jnp.float32
BF16 = jnp.bfloat16
SPAN = 80.0


def mm(a, b, dims):
    return lax.dot_general(a, b, (dims, ((), ())), preferred_element_type=F32)


NN, NT, TN = ((1,), (0,)), ((1,), (1,)), ((0,), (0,))


def split(a):
    high = a.astype(BF16)
    return high, (a - high.astype(F32)).astype(BF16)


def mm3(a, b, dims):
    ah, al = split(a)
    bh, bl = split(b)
    return mm(ah, bh, dims) + (mm(ah, bl, dims) + mm(al, bh, dims))


def mm_exact(mask, b, dims):
    b1, rest = split(b)
    b2 = rest
    b3 = (b - b1.astype(F32) - b2.astype(F32)).astype(BF16)
    return mm(mask, b1, dims) + (mm(mask, b2, dims) + mm(mask, b3, dims))


def swish_parts(v):
    sig = 1.0 / (1.0 + jnp.exp(-v))
    return v * sig, sig * (1.0 + v * (1.0 - sig))


def gates(f_low, wfu):
    f_pre = mm(f_low, wfu, NN)
    soft = jnp.log(1.0 + jnp.exp(-jnp.abs(f_pre)))
    log_f = (jnp.minimum(f_pre, 0.0) - soft) * 0.125
    return f_pre, log_f


def lower_tri(n, kind=BF16):
    rows = lax.broadcasted_iota(jnp.int32, (n, n), 0)
    cols = lax.broadcasted_iota(jnp.int32, (n, n), 1)
    return rows >= cols


def column(a, j):
    picked = lax.broadcasted_iota(jnp.int32, a.shape, 1) == j
    return jnp.sum(jnp.where(picked, a, 0.0), axis=1, keepdims=True)


def row(a, j):
    picked = lax.broadcasted_iota(jnp.int32, a.shape, 0) == j
    return jnp.sum(jnp.where(picked, a, 0.0), axis=0, keepdims=True)


def gap(total, j):
    return jnp.exp(jnp.minimum(total - row(total, j), 0.0))


def softmax(scores):
    e = jnp.exp(scores - jnp.max(scores, axis=1, keepdims=True))
    return e / jnp.sum(e, axis=1, keepdims=True)


def far_near(total):
    mid = 0.5 * total[-1:]
    return jnp.exp(total - mid), jnp.exp(mid - total)


def sum_over_j(mats, total, unit, fast, dest):
    n = total.shape[0]

    @pl.when(fast)
    def _():
        near, far = far_near(total)
        got = mm3(jnp.concatenate(mats, axis=0), far * unit, NN)
        for i, d in enumerate(dest):
            d[...] = got[i * n:(i + 1) * n] * near

    @pl.when(jnp.logical_not(fast))
    def _():
        for d in dest:
            d[...] = jnp.zeros_like(total)

        def step(j, _):
            e = gap(total, j) * row(unit, j)
            for d, m in zip(dest, mats):
                d[...] += column(m, j) * e
            return 0

        lax.fori_loop(0, n, step, 0)


def sum_over_m(probs, total, unit, fast, dest):
    n = total.shape[0]

    @pl.when(fast)
    def _():
        near, far = far_near(total)
        got = mm3(jnp.concatenate([p * near for p in probs], axis=0), far * unit, NT)
        for i, d in enumerate(dest):
            d[...] = got[i * n:(i + 1) * n]

    @pl.when(jnp.logical_not(fast))
    def _():
        cols = lax.broadcasted_iota(jnp.int32, (n, n), 1)

        def step(j, _):
            e = gap(total, j) * row(unit, j)
            for d, p in zip(dest, probs):
                d[...] = jnp.where(cols == j, jnp.sum(p * e, axis=1, keepdims=True), d[...])
            return 0

        lax.fori_loop(0, n, step, 0)


def sum_over_t(mats, probs, total, fast, dest):
    n = total.shape[0]

    @pl.when(fast)
    def _():
        near, far = far_near(total)
        got = mm3(jnp.concatenate(mats, axis=0), jnp.concatenate([p * near for p in probs], axis=0), TN)
        dest[...] = got * far

    @pl.when(jnp.logical_not(fast))
    def _():
        rows = lax.broadcasted_iota(jnp.int32, total.shape, 0)

        def step(j, _):
            e = gap(total, j)
            s = sum(column(m, j) * p for m, p in zip(mats, probs))
            dest[...] = jnp.where(rows == j, jnp.sum(s * e, axis=0, keepdims=True), dest[...])
            return 0

        lax.fori_loop(0, n, step, 0)


def mixer_forward(pre_ref, f_low_ref, wfu_ref, doc_col_ref, doc_row_ref, score_ref, mix_ref):
    pre = pre_ref[...]
    q, q_slope = swish_parts(pre[:, :HEAD])
    k, k_slope = swish_parts(pre[:, HEAD:2 * HEAD])
    q, k, v = q.astype(BF16), k.astype(BF16), pre[:, 2 * HEAD:3 * HEAD].astype(BF16)
    n = q.shape[0]
    tri = lower_tri(n)
    keep = tri & (doc_col_ref[0] == doc_row_ref[0])
    inner = jnp.where(keep, mm(q, k, NT) * HEAD ** -0.5, 0.0)
    f_pre, log_f = gates(f_low_ref[...], wfu_ref[...])
    total = mm_exact(tri.astype(BF16), log_f, NN)
    unit = 1.0 - jnp.exp(log_f)
    fast = jnp.min(total[-1:]) > -SPAN
    return q, k, v, q_slope, k_slope, keep, inner, f_pre, log_f, total, unit, fast


def forward_kernel(pre_ref, f_low_ref, wfu_ref, gain_ref, doc_col_ref, doc_row_ref, act_ref, score_ref, mix_ref):
    q, k, v, _, _, keep, inner, _, _, total, unit, fast = mixer_forward(
        pre_ref, f_low_ref, wfu_ref, doc_col_ref, doc_row_ref, score_ref, mix_ref)
    sum_over_j([inner], total, unit, fast, [score_ref])
    probs = softmax(score_ref[...])
    sum_over_m([probs], total, unit, fast, [mix_ref])
    mixing = jnp.where(keep, mix_ref[...], 0.0).astype(BF16)
    out = mm(mixing, v, NN)
    scale = lax.rsqrt(jnp.mean(out * out, axis=1, keepdims=True) + 1e-06)
    gate, _ = swish_parts(pre_ref[:, 3 * HEAD:])
    act_ref[...] = (out * scale * gain_ref[...] * gate).astype(BF16)


def backward_kernel(pre_ref, f_low_ref, wfu_ref, gain_ref, doc_col_ref, doc_row_ref, d_act_ref,
                    d_pre_ref, d_f_ref, d_low_ref, g_gain_ref,
                    score_ref, d_p_ref, mix_ref, d_inner_ref, k_ref):
    q, k, v, q_slope, k_slope, keep, inner, f_pre, log_f, total, unit, fast = mixer_forward(
        pre_ref, f_low_ref, wfu_ref, doc_col_ref, doc_row_ref, score_ref, mix_ref)
    sum_over_j([inner], total, unit, fast, [score_ref])
    scores = score_ref[...]
    probs = softmax(scores)
    sum_over_m([probs], total, unit, fast, [mix_ref])
    mixing = jnp.where(keep, mix_ref[...], 0.0).astype(BF16)
    out = mm(mixing, v, NN)

    scale = lax.rsqrt(jnp.mean(out * out, axis=1, keepdims=True) + 1e-06)
    gain = gain_ref[...]
    gate, gate_slope = swish_parts(pre_ref[:, 3 * HEAD:])
    d_act = d_act_ref[...].astype(F32)
    d_gate = d_act * out * scale * gain * gate_slope
    d_norm = d_act * gate
    g_gain = jnp.sum(d_norm * out * scale, axis=0, keepdims=True)

    @pl.when(pl.program_id(0) == 0)
    def _():
        g_gain_ref[...] = jnp.zeros_like(g_gain_ref)

    g_gain_ref[...] += g_gain
    d_norm = d_norm * gain
    d_out = scale * (d_norm - out * (scale * scale) * jnp.mean(d_norm * out, axis=1, keepdims=True))
    d_out = d_out.astype(BF16)

    d_mix = jnp.where(keep, mm(d_out, v, NT), 0.0)
    d_v = mm(mixing, d_out, TN)
    sum_over_j([d_mix], total, unit, fast, [d_p_ref])
    d_p = d_p_ref[...]
    d_score = probs * (d_p - jnp.sum(probs * d_p, axis=1, keepdims=True))
    sum_over_m([d_score], total, unit, fast, [d_inner_ref])
    d_inner = jnp.where(keep, d_inner_ref[...], 0.0).astype(BF16)
    sum_over_t([d_mix, inner], [probs, d_score], total, fast, k_ref)
    k_sum = k_ref[...]
    d_total = probs * d_p + d_score * scores - unit * k_sum
    n = q.shape[0]
    tri = lower_tri(n).astype(BF16)
    d_log = mm_exact(tri, d_total, TN) - jnp.exp(log_f) * k_sum
    d_f = (d_log * (0.125 / (1.0 + jnp.exp(f_pre)))).astype(BF16)
    d_f_ref[...] = d_f
    d_low_ref[...] = mm(d_f, wfu_ref[...], NT).astype(BF16)
    d_q = mm(d_inner, k, NN) * HEAD ** -0.5
    d_k = mm(d_inner, q, TN) * HEAD ** -0.5
    d_pre_ref[:, :HEAD] = (d_q * q_slope).astype(BF16)
    d_pre_ref[:, HEAD:2 * HEAD] = (d_k * k_slope).astype(BF16)
    d_pre_ref[:, 2 * HEAD:3 * HEAD] = d_v.astype(BF16)
    d_pre_ref[:, 3 * HEAD:] = d_gate.astype(BF16)


def mixer_specs(length, rank):
    return [
        pl.BlockSpec((length, 4 * HEAD), lambda i: (i, 0)),
        pl.BlockSpec((length, rank), lambda i: (i, 0)),
        pl.BlockSpec((rank, SLOTS), lambda i: (0, 0)),
        pl.BlockSpec((1, HEAD), lambda i: (0, 0)),
        pl.BlockSpec((1, length, 1), lambda i: (i, 0, 0)),
        pl.BlockSpec((1, 1, length), lambda i: (i, 0, 0)),
    ]


def slots_forward(pre, f_low, wfu, gain, docs):
    count, length = docs.shape
    tm = pltpu.VMEM((length, SLOTS), F32)
    tj = pltpu.VMEM((length, length), F32)
    return pl.pallas_call(
        forward_kernel,
        out_shape=jax.ShapeDtypeStruct((count * length, HEAD), BF16),
        grid=(count,),
        in_specs=mixer_specs(length, f_low.shape[1]),
        out_specs=pl.BlockSpec((length, HEAD), lambda i: (i, 0)),
        scratch_shapes=[tm, tj],
        compiler_params=pltpu.CompilerParams(vmem_limit_bytes=32 << 20),
        name="slots_forward",
    )(pre, f_low, wfu, gain, docs[:, :, None], docs[:, None, :])


def slots_backward(pre, f_low, wfu, gain, docs, d_act):
    count, length = docs.shape
    rank = f_low.shape[1]
    tm = pltpu.VMEM((length, SLOTS), F32)
    tj = pltpu.VMEM((length, length), F32)
    block = lambda width: pl.BlockSpec((length, width), lambda i: (i, 0))
    return pl.pallas_call(
        backward_kernel,
        out_shape=(
            jax.ShapeDtypeStruct((count * length, 4 * HEAD), BF16),
            jax.ShapeDtypeStruct((count * length, SLOTS), BF16),
            jax.ShapeDtypeStruct((count * length, rank), BF16),
            jax.ShapeDtypeStruct((1, HEAD), F32),
        ),
        grid=(count,),
        in_specs=mixer_specs(length, rank) + [block(HEAD)],
        out_specs=(block(4 * HEAD), block(SLOTS), block(rank), pl.BlockSpec((1, HEAD), lambda i: (0, 0))),
        scratch_shapes=[tm, tm, tj, tj, tm],
        compiler_params=pltpu.CompilerParams(vmem_limit_bytes=32 << 20),
        name="slots_backward",
    )(pre, f_low, wfu, gain, docs[:, :, None], docs[:, None, :], d_act)


def place(index, cs):
    return (index // (TP * cs), (index // cs) % TP, index % cs)


def greet_all(n, cs, me):
    barrier = pltpu.get_barrier_semaphore()

    def greet(step, _):
        pl.semaphore_signal(barrier, inc=1, device_id=place((me + step) % n, cs), device_id_type=pl.DeviceIdType.MESH)
        return 0

    lax.fori_loop(1, n, greet, 0)
    pl.semaphore_wait(barrier, n - 1)


def my_index(cs):
    return (lax.axis_index("z") * TP + lax.axis_index("t")) * cs + lax.axis_index("c")


def chip_peer(t, step):
    high, low = t // 2, t % 2
    return (high + step // 2) % 2 * 2 + (low + step % 2) % 2


def spread_kernel(n, cs, plan, share, *refs):
    count = len(plan)
    srcs, refs = refs[:count], refs[count:]
    if share:
        x_ref, refs = refs[0], refs[1:]
    outs = 1 + max(p[0] for p in plan)
    dsts, refs = refs[:outs], refs[outs:]
    if share:
        o_ref, refs = refs[0], refs[1:]
    own_sem, send_sem, recv_sem = refs[:3]
    z, t, c = (lax.axis_index(a) for a in ALL)
    me = my_index(cs)
    if share:
        greet_all(n, cs, me)
    else:
        greet_plane(z, t, c)

    def block(i, to, at):
        out, offset, width = plan[i]
        src = srcs[i].at[:, pl.ds(pl.multiple_of(to * width, 128), width)]
        return src, dsts[out].at[at, :, pl.ds(offset, width)]

    copies = []
    for step in (3, 1, 2):
        peer = chip_peer(t, step)
        for i in range(count):
            src, dst = block(i, peer, t)
            copies.append(pltpu.make_async_remote_copy(
                src_ref=src, dst_ref=dst, send_sem=send_sem.at[step - 1, i], recv_sem=recv_sem.at[step - 1, i],
                device_id=(z, peer, c), device_id_type=pl.DeviceIdType.MESH))
            copies[-1].start()
    for i in range(count):
        src, dst = block(i, t, t)
        copies.append(pltpu.make_async_copy(src, dst, own_sem.at[i]))
        copies[-1].start()
    if share:
        small_send, small_recv = refs[3:]

        def send(step, _):
            pltpu.make_async_remote_copy(
                src_ref=x_ref, dst_ref=o_ref.at[me], send_sem=small_send, recv_sem=small_recv,
                device_id=place((me + step) % n, cs), device_id_type=pl.DeviceIdType.MESH).start()
            return 0

        lax.fori_loop(1, n, send, 0)
        o_ref[me] = x_ref[...]
        others = o_ref.at[pl.ds(0, n - 1)]
        pltpu.make_async_copy(others, others, small_recv).wait()
        pltpu.make_async_copy(others, others, small_send).wait()
    for copy in copies:
        copy.wait()


def greet_plane(z, t, c):
    barrier = pltpu.get_barrier_semaphore()
    for step in (1, 2, 3):
        pl.semaphore_signal(barrier, inc=1, device_id=(z, chip_peer(t, step), c), device_id_type=pl.DeviceIdType.MESH)
    pl.semaphore_wait(barrier, TP - 1)


def spread(groups, small, n, cs, ident):
    plan, weights, shapes = [], [], []
    for out, group in enumerate(groups):
        at = 0
        for w in group:
            plan.append((out, at, w.shape[1] // TP))
            weights.append(w)
            at += w.shape[1] // TP
        shapes.append(jax.ShapeDtypeStruct((TP, group[0].shape[0], at), group[0].dtype))
    anywhere = pl.BlockSpec(memory_space=pl.ANY)
    fast = pl.BlockSpec(memory_space=pltpu.VMEM)
    sems = [pltpu.SemaphoreType.DMA((len(plan),))] + [pltpu.SemaphoreType.DMA((TP - 1, len(plan)))] * 2
    share = small is not None
    if share:
        shapes.append(jax.ShapeDtypeStruct((n,) + small.shape, small.dtype))
        sems += [pltpu.SemaphoreType.DMA] * 2
    return pl.pallas_call(
        functools.partial(spread_kernel, n, cs, plan, share),
        out_shape=tuple(shapes),
        in_specs=[anywhere] * len(plan) + [fast] * share,
        out_specs=tuple([anywhere] * len(groups) + [fast] * share),
        scratch_shapes=sems,
        compiler_params=pltpu.CompilerParams(collective_id=ident, has_side_effects=True, vmem_limit_bytes=32 << 20),
        name="spread",
    )(*weights, *([small] if share else []))


def spread_ff_kernel(zs, wg_ref, wu_ref, o_ref, packed, own_sem, send_sem, recv_sem):
    z, t, c = (lax.axis_index(a) for a in ALL)
    count = packed.shape[2] // 2
    piece = count // zs
    greet_plane(z, t, c)
    for j in range(TP):
        for i, w in enumerate((wg_ref, wu_ref)):
            for k in range(zs):
                at = i * count + k * piece
                packed[j, :, at:at + piece] = w[:, (k * TP + j) * piece:(k * TP + j + 1) * piece]
    copies = []
    for step in (3, 1, 2):
        peer = chip_peer(t, step)
        copies.append(pltpu.make_async_remote_copy(
            src_ref=packed.at[peer], dst_ref=o_ref.at[t], send_sem=send_sem.at[step - 1],
            recv_sem=recv_sem.at[step - 1], device_id=(z, peer, c), device_id_type=pl.DeviceIdType.MESH))
        copies[-1].start()
    copies.append(pltpu.make_async_copy(packed.at[t], o_ref.at[t], own_sem))
    copies[-1].start()
    for copy in copies:
        copy.wait()


def spread_ff(w_gate, w_up, zs, ident):
    rows, units = w_gate.shape
    shape = (TP, rows, 2 * units // TP)
    fast = pl.BlockSpec(memory_space=pltpu.VMEM)
    return pl.pallas_call(
        functools.partial(spread_ff_kernel, zs),
        out_shape=jax.ShapeDtypeStruct(shape, w_gate.dtype),
        in_specs=[fast, fast],
        out_specs=pl.BlockSpec(memory_space=pl.ANY),
        scratch_shapes=[pltpu.VMEM(shape, w_gate.dtype), pltpu.SemaphoreType.DMA,
                        pltpu.SemaphoreType.DMA((TP - 1,)), pltpu.SemaphoreType.DMA((TP - 1,))],
        compiler_params=pltpu.CompilerParams(collective_id=ident, has_side_effects=True, vmem_limit_bytes=32 << 20),
        name="spread_ff",
    )(w_gate, w_up)


def send_blocks(sources, targets, own_sem, send_sem, recv_sem):
    z, t, c = (lax.axis_index(a) for a in ALL)
    copies = []
    for step in (3, 1, 2):
        peer = chip_peer(t, step)
        for i, (source, target) in enumerate(zip(sources, targets)):
            copies.append(pltpu.make_async_remote_copy(
                src_ref=source.at[peer], dst_ref=target.at[t], send_sem=send_sem.at[step - 1, i],
                recv_sem=recv_sem.at[step - 1, i], device_id=(z, peer, c), device_id_type=pl.DeviceIdType.MESH))
            copies[-1].start()
    for i, (source, target) in enumerate(zip(sources, targets)):
        copies.append(pltpu.make_async_copy(source.at[t], target.at[t], own_sem.at[i]))
        copies[-1].start()
    return copies


def block_sems(count):
    return [pltpu.SemaphoreType.DMA((count,))] + [pltpu.SemaphoreType.DMA((TP - 1, count))] * 2


def widen_kernel(moves, x_ref, *outs):
    for out, at, j, source, width in moves:
        outs[out][:, at:at + width] = x_ref[j, :, source:source + width].astype(F32)


def widen(x, moves, count, columns):
    fast = pl.BlockSpec(memory_space=pltpu.VMEM)
    return pl.pallas_call(
        functools.partial(widen_kernel, moves),
        out_shape=tuple(jax.ShapeDtypeStruct((x.shape[1], columns), F32) for _ in range(count)),
        in_specs=[fast],
        out_specs=tuple(fast for _ in range(count)),
        compiler_params=pltpu.CompilerParams(vmem_limit_bytes=32 << 20),
        name="widen",
    )(x)


def finish_kernel(n, cs, x_ref, blocks_ref, o_ref, back_ref, got_ref, send_sem, recv_sem, *block_sem):
    me = my_index(cs)
    greet_all(n, cs, me)

    def send(step, _):
        peer = (me + step) % n
        pltpu.make_async_remote_copy(
            src_ref=x_ref.at[peer], dst_ref=got_ref.at[me], send_sem=send_sem, recv_sem=recv_sem,
            device_id=place(peer, cs), device_id_type=pl.DeviceIdType.MESH).start()
        return 0

    lax.fori_loop(1, n, send, 0)
    copies = send_blocks([blocks_ref], [back_ref], *block_sem)
    got_ref[me] = x_ref[me]
    others = got_ref.at[pl.ds(0, n - 1)]
    pltpu.make_async_copy(others, others, recv_sem).wait()
    pltpu.make_async_copy(others, others, send_sem).wait()
    o_ref[...] = jnp.sum(got_ref[...], axis=0)
    for copy in copies:
        copy.wait()


def finish(x, blocks, n, cs):
    anywhere = pl.BlockSpec(memory_space=pl.ANY)
    fast = pl.BlockSpec(memory_space=pltpu.VMEM)
    return pl.pallas_call(
        functools.partial(finish_kernel, n, cs),
        out_shape=(jax.ShapeDtypeStruct(x.shape[1:], x.dtype), jax.ShapeDtypeStruct(blocks.shape, blocks.dtype)),
        in_specs=[fast, anywhere],
        out_specs=(fast, anywhere),
        scratch_shapes=[pltpu.VMEM(x.shape, x.dtype), pltpu.SemaphoreType.DMA, pltpu.SemaphoreType.DMA] + block_sems(1),
        compiler_params=pltpu.CompilerParams(collective_id=1, has_side_effects=True, vmem_limit_bytes=32 << 20),
        name="finish",
    )(x, blocks)


def pack_rows(parts, unit):
    flat = jnp.concatenate(parts, axis=-1)
    size = flat.shape[-1]
    padded = -(-size // (unit * 128)) * unit * 128
    flat = jnp.pad(flat, [(0, 0)] * (flat.ndim - 1) + [(0, padded - size)])
    return flat.reshape(flat.shape[:-1] + (padded // 128, 128))


def cut(flat, sizes):
    at, pieces = 0, []
    for size in sizes:
        pieces.append(flat[..., at:at + size])
        at += size
    return pieces


def relay(p_ref, o_ref, got1, pass2, got2, sems, subs, middle, shared=True, beside=None, plane=False):
    z, t, c = (lax.axis_index(a) for a in ALL)
    peers = {step: (z, chip_peer(t, step), c) for step in (1, 2)}
    if plane:
        greet_plane(z, t, c)
    else:
        barrier = pltpu.get_barrier_semaphore()
        for step in (1, 2):
            pl.semaphore_signal(barrier, inc=1, device_id=peers[step], device_id_type=pl.DeviceIdType.MESH)
        pl.semaphore_wait(barrier, 2)
    send_sem, recv_sem = sems
    half = p_ref.shape[1] // 2
    size = half // subs
    ways = ((1, 2), (2, 1))
    copies = []

    def start(src, dst, step, slot, i):
        copy = pltpu.make_async_remote_copy(
            src_ref=src, dst_ref=dst, send_sem=send_sem.at[slot, i], recv_sem=recv_sem.at[slot, i],
            device_id=peers[step], device_id_type=pl.DeviceIdType.MESH)
        copy.start()
        copies.append(copy)
        return copy

    def part(w, i):
        return pl.ds(w * half + i * size, size)

    def local(i):
        return pl.ds(i * size, size)

    first = [[[start(p_ref.at[near if j == 0 else 3, part(w, i)], got1.at[w, j, local(i)], near, 2 * w + j, i)
               for j in (0, 1)] for w, (near, far) in enumerate(ways)] for i in range(subs)]
    second, third, fourth = [None] * subs, [None] * subs, []
    for i in range(subs + 2):
        if i < subs:
            second[i] = []
            for w, (near, far) in enumerate(ways):
                first[i][w][1].wait_recv()
                both = p_ref[far, part(w, i)].astype(F32) + got1[w, 1, local(i)].astype(F32)
                pass2[w, local(i)] = both.astype(BF16)
                second[i].append(start(pass2.at[w, local(i)], got2.at[w, local(i)], far, 4 + w, i))
        if 1 <= i <= subs:
            k = i - 1
            third[k] = []
            for w in (0, 1):
                first[k][w][0].wait_recv()
                second[k][w].wait_recv()
                total = p_ref[0, part(w, k)].astype(F32) + got1[w, 0, local(k)].astype(F32)
                total = total + got2[w, local(k)].astype(F32)
                rows = middle(w * half + k * size, size, total)
                if not shared:
                    o_ref[part(w, k)] = rows
                    continue
                o_ref[0, part(w, k)] = rows
                third[k].append([start(o_ref.at[0, part(w, k)], o_ref.at[step, part(w, k)], step, 5 + 2 * w + step, k)
                                 for step in (1, 2)])
        if beside is not None:
            beside(i)
        if i >= 2 and shared:
            k = i - 2
            for w, (near, far) in enumerate(ways):
                third[k][w][far - 1].wait_recv()
                fourth.append(start(o_ref.at[far, part(w, k)], o_ref.at[3, part(w, k)], near, 10 + w, k))
    for copy in copies:
        copy.wait_send()
    for k in range(subs if shared else 0):
        for w, (near, far) in enumerate(ways):
            third[k][w][near - 1].wait_recv()
    for copy in fourth:
        copy.wait_recv()


def forward_relay_kernel(unit, subs, p_ref, x_ref, gain_ref, o_ref, resid_ref, got1, pass2, got2, ordered, *sems):
    def middle(at, size, total):
        rows = pl.ds(at, size)
        resid = total + x_ref[rows].astype(F32)
        resid_ref[rows] = resid
        normed = resid * lax.rsqrt(jnp.mean(resid * resid, axis=1, keepdims=True) + 1e-06) * gain_ref[...]
        half = normed.shape[1] // 2
        for j in range(half // unit):
            for k in (0, 1):
                ordered[:, k * half + j * unit:k * half + (j + 1) * unit] = normed[:, (2 * j + k) * unit:(2 * j + k + 1) * unit]
        return ordered[...].astype(BF16)

    relay(p_ref, o_ref, got1, pass2, got2, sems, subs, middle)


def norm_backward(unit, resid_ref, gain_ref, g_gain_ref, ordered, finish):
    g_gain_ref[...] = jnp.zeros_like(g_gain_ref)

    def middle(at, size, total):
        rows = pl.ds(at, size)
        half = total.shape[1] // 2
        for j in range(half // unit):
            for k in (0, 1):
                ordered[:, (2 * j + k) * unit:(2 * j + k + 1) * unit] = total[:, k * half + j * unit:k * half + (j + 1) * unit]
        d = ordered[...]
        resid = resid_ref[rows].astype(F32)
        scale = lax.rsqrt(jnp.mean(resid * resid, axis=1, keepdims=True) + 1e-06)
        unit_resid = resid * scale
        g_gain_ref[...] += jnp.sum(d * unit_resid, axis=0, keepdims=True)
        d = d * gain_ref[...]
        d = scale * (d - unit_resid * jnp.mean(d * unit_resid, axis=1, keepdims=True))
        return finish(rows, d)

    return middle


def backward_relay_kernel(unit, subs, p_ref, resid_ref, cot_ref, gain_ref, hidden_hbm, branch_hbm, down_hbm,
                          o_ref, d_resid_ref, g_gain_ref, g_down_hbm, terms_hbm,
                          got1, pass2, got2, ordered, send_sem, recv_sem,
                          hidden, branch, down, g_down, terms, in_sem, out_sem):
    loads = [pltpu.make_async_copy(src, dst, in_sem.at[i])
             for i, (src, dst) in enumerate([(hidden_hbm, hidden), (branch_hbm, branch), (down_hbm, down)])]
    for copy in loads:
        copy.start()
    D = branch.shape[1]
    width = D // subs
    stores = []

    def beside(i):
        if i == 0:
            for copy in loads:
                copy.wait()
        if i >= subs:
            return
        cols = slice(i * width, (i + 1) * width)
        g_down[i] = mm(hidden[...], branch[:, cols], TN).astype(BF16)
        terms[i] = mm(hidden[...], down[:, cols], NN).astype(BF16)
        for j, (src, dst) in enumerate([(g_down, g_down_hbm), (terms, terms_hbm)]):
            stores.append(pltpu.make_async_copy(src.at[i], dst.at[:, cols], out_sem.at[j, i]))
            stores[-1].start()

    def finish(rows, d):
        d = d + cot_ref[rows].astype(F32)
        d_resid_ref[rows] = d
        return d.astype(BF16)

    middle = norm_backward(unit, resid_ref, gain_ref, g_gain_ref, ordered, finish)
    relay(p_ref, o_ref, got1, pass2, got2, (send_sem, recv_sem), subs, middle, True, beside)
    for copy in stores:
        copy.wait()


def settle_kernel(unit, count, subs, p_ref, x_ref, d_resid_ref, gain_ref, *refs):
    blocks, refs = refs[:count], refs[count:]
    o_ref, g_gain_ref, refs = refs[0], refs[1], refs[2:]
    returned, refs = refs[:count], refs[count:]
    got1, pass2, got2, ordered, send_sem, recv_sem, own_sem, back_send, back_recv = refs
    copies = []

    def beside(i):
        if i == 0:
            copies.extend(send_blocks(blocks, returned, own_sem, back_send, back_recv))

    def finish(rows, d):
        return (d + d_resid_ref[rows]).astype(BF16)

    middle = norm_backward(unit, x_ref, gain_ref, g_gain_ref, ordered, finish)
    relay(p_ref, o_ref, got1, pass2, got2, (send_sem, recv_sem), subs, middle, False, beside, True)
    for copy in copies:
        copy.wait()


def relay_scratch(count, D, subs):
    half, size = count // 2, count // 2 // subs
    return [
        pltpu.VMEM((2, 2, half, D), BF16),
        pltpu.VMEM((2, half, D), BF16),
        pltpu.VMEM((2, half, D), BF16),
        pltpu.VMEM((size, D), F32),
        pltpu.SemaphoreType.DMA((12, subs)),
        pltpu.SemaphoreType.DMA((12, subs)),
    ]


SUBS = 4


def relay_forward(p, x, gain, unit, ident):
    _, count, D = p.shape
    fast = pl.BlockSpec(memory_space=pltpu.VMEM)
    return pl.pallas_call(
        functools.partial(forward_relay_kernel, unit, SUBS),
        out_shape=(jax.ShapeDtypeStruct(p.shape, BF16), jax.ShapeDtypeStruct(x.shape, F32)),
        in_specs=[fast] * 3,
        out_specs=(fast,) * 2,
        scratch_shapes=relay_scratch(count, D, SUBS),
        compiler_params=pltpu.CompilerParams(collective_id=ident, has_side_effects=True, vmem_limit_bytes=40 << 20),
        name="relay_forward",
    )(p, x, gain)


def relay_backward(p, resid, cot, gain, hidden, branch, down, unit, ident):
    _, count, D = p.shape
    tokens, units = hidden.shape
    width = D // SUBS
    fast = pl.BlockSpec(memory_space=pltpu.VMEM)
    anywhere = pl.BlockSpec(memory_space=pl.ANY)
    return pl.pallas_call(
        functools.partial(backward_relay_kernel, unit, SUBS),
        out_shape=(
            jax.ShapeDtypeStruct(p.shape, BF16),
            jax.ShapeDtypeStruct(resid.shape, F32),
            jax.ShapeDtypeStruct((1, D), F32),
            jax.ShapeDtypeStruct((units, D), BF16),
            jax.ShapeDtypeStruct((tokens, D), BF16),
        ),
        in_specs=[fast] * 4 + [anywhere] * 3,
        out_specs=(fast,) * 3 + (anywhere,) * 2,
        scratch_shapes=relay_scratch(count, D, SUBS) + [
            pltpu.VMEM(hidden.shape, BF16),
            pltpu.VMEM(branch.shape, BF16),
            pltpu.VMEM(down.shape, BF16),
            pltpu.VMEM((SUBS, units, width), BF16),
            pltpu.VMEM((SUBS, tokens, width), BF16),
            pltpu.SemaphoreType.DMA((3,)),
            pltpu.SemaphoreType.DMA((2, SUBS)),
        ],
        compiler_params=pltpu.CompilerParams(collective_id=ident, has_side_effects=True, vmem_limit_bytes=58 << 20),
        name="relay_backward",
    )(p, resid, cot, gain, hidden, branch, down)


def settle(p, x, d_resid, gain, blocks, unit, ident):
    _, count, D = p.shape
    fast = pl.BlockSpec(memory_space=pltpu.VMEM)
    anywhere = pl.BlockSpec(memory_space=pl.ANY)
    number = len(blocks)
    return pl.pallas_call(
        functools.partial(settle_kernel, unit, number, SUBS),
        out_shape=(jax.ShapeDtypeStruct(p.shape[1:], BF16), jax.ShapeDtypeStruct((1, D), F32))
        + tuple(jax.ShapeDtypeStruct(b.shape, b.dtype) for b in blocks),
        in_specs=[fast] * 4 + [anywhere] * number,
        out_specs=(fast,) * 2 + (anywhere,) * number,
        scratch_shapes=relay_scratch(count, D, SUBS) + block_sems(number),
        compiler_params=pltpu.CompilerParams(collective_id=ident, has_side_effects=True, vmem_limit_bytes=40 << 20),
        name="settle",
    )(p, x, d_resid, gain, *blocks)


def ff_kernel(tile, hm_ref, gate_ref, up_ref, d_hidden_ref, hidden_ref, d_gate_ref, d_up_ref):
    width = gate_ref.shape[1]
    weights = jnp.concatenate([gate_ref[...], up_ref[...]], axis=1)
    for at in range(0, hm_ref.shape[0], tile):
        rows = slice(at, at + tile)
        pre = mm(hm_ref[rows, :], weights, NN)
        gate, up = pre[:, :width], pre[:, width:]
        sig = 0.5 * jnp.tanh(0.5 * gate) + 0.5
        act = gate * sig
        d_hidden = d_hidden_ref[rows, :]
        hidden_ref[rows, :] = (act * up).astype(BF16)
        d_gate_ref[rows, :] = (d_hidden * up * (sig + act * (1.0 - sig))).astype(BF16)
        d_up_ref[rows, :] = (d_hidden * act).astype(BF16)


def ff_forward(hm, gu, d_hidden):
    tokens, D = hm.shape
    units = d_hidden.shape[1]
    width = 128
    steps = units // width
    block = pl.BlockSpec((tokens, width), lambda j: (0, j))
    shape = jax.ShapeDtypeStruct((tokens, units), BF16)
    return pl.pallas_call(
        functools.partial(ff_kernel, 256),
        out_shape=(shape,) * 3,
        grid=(steps,),
        in_specs=[
            pl.BlockSpec((tokens, D), lambda j: (0, 0)),
            pl.BlockSpec((D, width), lambda j: (0, j)),
            pl.BlockSpec((D, width), lambda j: (0, j + steps)),
            block,
        ],
        out_specs=(block,) * 3,
        compiler_params=pltpu.CompilerParams(vmem_limit_bytes=48 << 20),
        name="feed_forward",
    )(hm, gu, gu, d_hidden)


def d_hm_kernel(tile, d_gate_ref, d_up_ref, gu_ref, o_ref):
    units = d_gate_ref.shape[1]
    for at in range(0, d_gate_ref.shape[0], tile):
        rows = slice(at, at + tile)
        out = mm(d_gate_ref[rows, :], gu_ref[:, :units], NT) + mm(d_up_ref[rows, :], gu_ref[:, units:], NT)
        o_ref[rows, :] = out.astype(BF16)


def d_hm_product(d_gate, d_up, gu):
    tokens, units = d_gate.shape
    D = gu.shape[0]
    width = 256
    whole = pl.BlockSpec((tokens, units), lambda j: (0, 0))
    return pl.pallas_call(
        functools.partial(d_hm_kernel, 256),
        out_shape=jax.ShapeDtypeStruct((tokens, D), BF16),
        grid=(D // width,),
        in_specs=[whole, whole, pl.BlockSpec((width, 2 * units), lambda j: (j, 0))],
        out_specs=pl.BlockSpec((tokens, width), lambda j: (0, j)),
        compiler_params=pltpu.CompilerParams(vmem_limit_bytes=48 << 20),
        name="d_hm",
    )(d_gate, d_up, gu)


def send_t(x, step):
    return lax.ppermute(x, "t", [(i, i ^ step) for i in range(TP)])


def send_c(x):
    return lax.ppermute(x, "c", [(0, 1), (1, 0)])


def gather_t(x):
    half = x.shape[0] // 2
    one, two = send_t(x, 1), send_t(x, 2)
    three = [send_t(two[:half], 1), send_t(one[half:], 2)]
    return jnp.concatenate([x, one, two] + three, axis=0)


def scatter_t_begin(x):
    count = x.shape[0] // TP
    half = count // 2
    p = [(x[k * count:k * count + half], x[k * count + half:(k + 1) * count]) for k in range(TP)]
    first = send_t(jnp.concatenate([p[1][0], p[3][0]], axis=0), 1).astype(F32)
    second = send_t(jnp.concatenate([p[2][1], p[3][1]], axis=0), 2).astype(F32)
    on_a = (p[2][0].astype(F32) + first[half:]).astype(BF16)
    on_b = (p[1][1].astype(F32) + second[half:]).astype(BF16)
    return on_a, on_b, p[0][0].astype(F32) + first[:half], p[0][1].astype(F32) + second[:half]


def scatter_t_end(on_a, on_b, a, b):
    return jnp.concatenate([a + send_t(on_a, 2).astype(F32), b + send_t(on_b, 1).astype(F32)], axis=0)


def swap_t(x):
    t = lax.axis_index("t")

    def block(a, j):
        return lax.dynamic_index_in_dim(a, j, 0, keepdims=False)

    got = jnp.stack([block(x, t)] + [send_t(block(x, t ^ k), k) for k in (1, 2, 3)])
    return jnp.stack([block(got, t ^ j) for j in range(TP)])


def dot(left, right):
    return mm(left, right, NN)


def dot_nt(left, right):
    return mm(left, right, NT)


def dot_tn(left, right):
    return mm(left, right, TN)


def after(x, *others):
    return lax.optimization_barrier((x,) + others)[:2]


def rms_norm(v, gain):
    return v * lax.rsqrt(jnp.mean(v * v, axis=-1, keepdims=True) + 1e-06) * gain


def swiglu(gate_val, up_val):
    return jax.nn.silu(gate_val) * up_val


def per_device(zs, cs, tokens, starts, w_query, w_key, w_value, w_gate_out, w_out, w_forget_down,
               w_forget_up, norm_attn, norm_head, norm_mlp, w_gate, w_up, w_down, cotangent):
    seqs, seq_len, D = tokens.shape
    n = zs * TP * cs
    rows = w_query.shape[0]
    ff_rows = w_down.shape[0]
    rank = w_forget_down.shape[1]
    fu_cols = w_forget_up.shape[1]
    mine = seqs * seq_len
    half = D // cs
    t_idx, c_idx = lax.axis_index("t"), lax.axis_index("c")

    def to_k(v):
        return v.reshape(-1, zs, TP, cs, rows).transpose(0, 3, 1, 2, 4).reshape(-1, D)

    def from_k(v):
        return v.reshape(-1, cs, zs, TP, rows).transpose(0, 2, 3, 1, 4).reshape(-1, D)

    def sum_z(v):
        return lax.psum_scatter(v, "z", scatter_dimension=0, tiled=True)

    docs = jnp.cumsum(starts, axis=1).astype(BF16)
    small = pack_rows([w_forget_down.reshape(-1), w_forget_up.reshape(-1), norm_attn, norm_head, norm_mlp,
                       docs.reshape(-1)], 16)
    sizes = [rows * rank, rank * fu_cols, norm_attn.shape[0], norm_head.shape[0], norm_mlp.shape[0]]
    w4, small = spread([[w_query, w_key, w_value, w_gate_out]], small, n, cs, 0)
    gu = spread_ff(w_gate, w_up, zs, 2)
    pieces = cut(small.reshape(n, -1), sizes + [mine])
    wfd = to_k(pieces[0].reshape(D, rank).T).T
    wfu = pieces[1].reshape(n, rank, fu_cols).transpose(1, 0, 2).reshape(rank, n * fu_cols)
    wfu = lax.dynamic_slice_in_dim(wfu, t_idx * SLOTS, SLOTS, axis=1)
    gain_attn = pieces[2].reshape(-1).astype(F32)
    gain_head = pieces[3].reshape(1, -1).astype(F32)
    gain_mlp = pieces[4].reshape(1, -1).astype(F32)
    all_docs = pieces[5].reshape(zs, TP, cs, mine)
    all_docs = lax.dynamic_index_in_dim(all_docs, lax.axis_index("z"), 0, keepdims=False)
    all_docs = lax.dynamic_index_in_dim(all_docs, lax.axis_index("c"), 1, keepdims=False)
    docs = jnp.concatenate([lax.dynamic_index_in_dim(all_docs, t_idx ^ k, 0) for k in range(TP)], axis=0)
    docs = docs.astype(F32).reshape(TP * seqs, seq_len)

    def by_columns(w):
        return lax.all_gather(w.reshape(TP * rows, -1), ("c", "z"), axis=0, tiled=True)

    by_rows = lax.all_gather(jnp.concatenate([w_out, w_down], axis=0), ("z", "c"), axis=0, tiled=True)
    by_rows = by_rows.reshape(zs, cs, rows + ff_rows, D)
    down = by_rows[:, :, rows:].reshape(-1, D)
    wo = swap_t(by_rows[:, :, :rows].reshape(TP, -1, rows, D))
    wo = wo.reshape(TP, zs // TP, cs, rows, D).transpose(1, 0, 2, 3, 4).reshape(HEAD, D)
    w4 = by_columns(w4)
    gu = by_columns(gu)
    hidden_count = down.shape[0]

    x = tokens.reshape(mine, D).astype(F32)
    normed_in, norm_in_back = jax.vjp(rms_norm, x, gain_attn)
    h = gather_t(to_k(normed_in.astype(BF16)))
    d_branch = gather_t(cotangent.reshape(mine, D))
    pre = dot(h, w4)
    f_low = dot(h, wfd).astype(BF16)
    act = slots_forward(pre, f_low, wfu, gain_head, docs)
    terms = dot(act, wo).astype(BF16)
    d_hidden = dot_nt(d_branch, down)
    terms, d_hidden = after(terms, d_hidden)
    tokens_flat = tokens.reshape(mine, D)
    hm, resid = relay_forward(terms.reshape(TP, mine, D), tokens_flat, gain_mlp, rows, 6)
    hm = hm.reshape(TP * mine, D)

    hidden, d_gate, d_up = ff_forward(hm, gu, d_hidden)

    def core_half(v, core):
        return lax.dynamic_slice_in_dim(v, core * half, half, axis=1)

    def other_term(left, right):
        return dot_tn(core_half(left, 1 - c_idx), right).astype(BF16)

    def own_term(left, right, other):
        return (dot_tn(core_half(left, c_idx), right) + send_c(other).astype(F32)).astype(BF16)

    def row_term(g):
        axis = g.ndim - 3
        got = send_c(lax.dynamic_index_in_dim(g, 1 - c_idx, axis, keepdims=False))
        g = lax.dynamic_index_in_dim(g, c_idx, axis, keepdims=False)
        return (g.astype(F32) + got.astype(F32)).astype(BF16)

    g_gate, g_up = other_term(hm, d_gate), other_term(hm, d_up)
    hm, g_up = after(hm, g_up)
    g_gate = own_term(hm, d_gate, g_gate)
    hm, g_gate = after(hm, g_gate)
    g_up = own_term(hm, d_up, g_up)
    d_up, g_up = after(d_up, g_up)
    d_hm = d_hm_product(d_gate, d_up, gu)
    g_gate, g_up = sum_z(g_gate), sum_z(g_up)
    cot = cotangent.reshape(mine, D)
    d_attn, d_resid, g_norm_mlp, g_down, branch = relay_backward(
        d_hm.reshape(TP, mine, D), resid, cot, gain_mlp, hidden, d_branch, down, rows, 7)
    d_attn = d_attn.reshape(TP * mine, D)
    g_down = row_term(g_down.reshape(zs, cs, ff_rows, D))
    g_down = sum_z(g_down.reshape(-1, D))

    g_out = row_term(dot_tn(act, d_attn).astype(BF16).reshape(zs // TP, TP, cs, rows, D))
    d_attn, g_out = after(d_attn, g_out)
    g_out = sum_z(swap_t(g_out.transpose(1, 0, 2, 3)).reshape(-1, D))
    d_attn, g_gate = after(d_attn, g_gate)
    d_pre, d_f, d_low, g_norm_head = slots_backward(pre, f_low, wfu, gain_head, docs, dot_nt(d_attn, wo))
    d_pre, g_up = after(d_pre, g_up)
    part = scatter_t_begin(branch)
    d_pre, part = after(d_pre, part)
    mixed = (resid + scatter_t_end(*part)).astype(BF16)
    g4 = own_term(h, d_pre, other_term(h, d_pre))
    d_pre, g4 = after(d_pre, g4)
    g4 = sum_z(g4)
    d_pre, g_down = after(d_pre, g_down)
    d_pre, mixed = after(d_pre, mixed)
    d_h = (dot_nt(d_pre, w4) + dot_nt(d_low, wfd)).astype(BF16)
    d_h, g_out = after(d_h, g_out)
    tokens_grad, g_norm_attn, g_gate, g_up = settle(
        d_h.reshape(TP, mine, D), tokens_flat, d_resid, gain_attn.reshape(1, D),
        [g_gate.reshape(TP, rows, -1), g_up.reshape(TP, rows, -1)], rows, 8)
    g_fu = dot_tn(f_low, d_f)
    g_fd = dot_tn(h, d_low)

    fu_full = lax.dynamic_update_slice_in_dim(jnp.zeros((rank, n * fu_cols), F32), g_fu, t_idx * SLOTS, axis=1)
    flat = pack_rows([
        from_k(g_fd.T).T.reshape(n, -1),
        fu_full.reshape(rank, n, fu_cols).transpose(1, 0, 2).reshape(n, -1),
        g_norm_attn.reshape(n, -1),
        g_norm_head.reshape(n, -1),
        g_norm_mlp.reshape(n, -1),
    ], 8)
    piece = cs * ff_rows
    ff_moves = [(0, (k * TP + j) * piece, j, k * piece, piece) for j in range(TP) for k in range(zs)]
    (g_gate,), (g_up,) = (widen(g, ff_moves, 1, n * ff_rows) for g in (g_gate, g_up))
    g_down, g_out = g_down.astype(F32), g_out.astype(F32)
    g4, mixed, tokens_grad, g_gate, g_up, g_down, g_out = lax.optimization_barrier(
        (g4, mixed, tokens_grad, g_gate, g_up, g_down, g_out))
    small, g4 = finish(flat, g4.reshape(TP, rows, -1), n, cs)
    pieces = cut(small.reshape(-1), sizes)
    head_moves = [(i, j * HEAD, j, i * HEAD, HEAD) for i in range(4) for j in range(TP)]
    g_query, g_key, g_value, g_gate_out = widen(g4, head_moves, 4, D)
    return (
        mixed.reshape(tokens.shape),
        tokens_grad.reshape(tokens.shape),
        g_query, g_key, g_value, g_gate_out,
        g_out,
        pieces[0].reshape(rows, rank),
        pieces[1].reshape(rank, fu_cols),
        pieces[2],
        pieces[3],
        pieces[4],
        g_gate, g_up,
        g_down,
    )


def solution(mesh):
    cs = mesh.shape["outer"]
    zs = mesh.shape["dp"] // TP
    grid = Mesh(mesh.devices.reshape(zs, TP, cs), ALL)
    whole, row, vec = P(ALL, None, None), P(ALL, None), P(ALL)
    cols = P(None, ALL)

    def body(*args):
        return per_device(zs, cs, *args)

    return jax.shard_map(
        body,
        mesh=grid,
        in_specs=(whole, row, row, row, row, row, row, row, cols, vec, vec, vec, row, row, row, whole),
        out_specs=(whole, whole, row, row, row, row, row, row, cols, vec, vec, vec, row, row, row),
        check_vma=False,
    )
```

```python
import functools

import jax
import jax.numpy as jnp
from jax import lax
from jax.experimental import pallas as pl
from jax.experimental.pallas import tpu as pltpu
from jax.sharding import Mesh, PartitionSpec as P

HEADS = 4
HEAD = 512
SLOTS = 64
TP = 4
ALL = ("z", "t", "c")
F32 = jnp.float32
BF16 = jnp.bfloat16
SPAN = 80.0


def mm(a, b, dims):
    return lax.dot_general(a, b, (dims, ((), ())), preferred_element_type=F32)


NN, NT, TN = ((1,), (0,)), ((1,), (1,)), ((0,), (0,))


def split(a):
    high = a.astype(BF16)
    return high, (a - high.astype(F32)).astype(BF16)


def mm3(a, b, dims):
    ah, al = split(a)
    bh, bl = split(b)
    return mm(ah, bh, dims) + (mm(ah, bl, dims) + mm(al, bh, dims))


def mm_exact(mask, b, dims):
    b1, rest = split(b)
    b2 = rest
    b3 = (b - b1.astype(F32) - b2.astype(F32)).astype(BF16)
    return mm(mask, b1, dims) + (mm(mask, b2, dims) + mm(mask, b3, dims))


def swish_parts(v):
    sig = 1.0 / (1.0 + jnp.exp(-v))
    return v * sig, sig * (1.0 + v * (1.0 - sig))


def gates(f_low, wfu):
    f_pre = mm(f_low, wfu, NN)
    soft = jnp.log(1.0 + jnp.exp(-jnp.abs(f_pre)))
    log_f = (jnp.minimum(f_pre, 0.0) - soft) * 0.125
    return f_pre, log_f


def lower_tri(n, kind=BF16):
    rows = lax.broadcasted_iota(jnp.int32, (n, n), 0)
    cols = lax.broadcasted_iota(jnp.int32, (n, n), 1)
    return rows >= cols


def column(a, j):
    picked = lax.broadcasted_iota(jnp.int32, a.shape, 1) == j
    return jnp.sum(jnp.where(picked, a, 0.0), axis=1, keepdims=True)


def row(a, j):
    picked = lax.broadcasted_iota(jnp.int32, a.shape, 0) == j
    return jnp.sum(jnp.where(picked, a, 0.0), axis=0, keepdims=True)


def gap(total, j):
    return jnp.exp(jnp.minimum(total - row(total, j), 0.0))


def softmax(scores):
    e = jnp.exp(scores - jnp.max(scores, axis=1, keepdims=True))
    return e / jnp.sum(e, axis=1, keepdims=True)


def far_near(total):
    mid = 0.5 * total[-1:]
    return jnp.exp(total - mid), jnp.exp(mid - total)


def sum_over_j(mats, total, unit, fast, dest):
    n = total.shape[0]

    @pl.when(fast)
    def _():
        near, far = far_near(total)
        got = mm3(jnp.concatenate(mats, axis=0), far * unit, NN)
        for i, d in enumerate(dest):
            d[...] = got[i * n:(i + 1) * n] * near

    @pl.when(jnp.logical_not(fast))
    def _():
        for d in dest:
            d[...] = jnp.zeros_like(total)

        def step(j, _):
            e = gap(total, j) * row(unit, j)
            for d, m in zip(dest, mats):
                d[...] += column(m, j) * e
            return 0

        lax.fori_loop(0, n, step, 0)


def sum_over_m(probs, total, unit, fast, dest):
    n = total.shape[0]

    @pl.when(fast)
    def _():
        near, far = far_near(total)
        got = mm3(jnp.concatenate([p * near for p in probs], axis=0), far * unit, NT)
        for i, d in enumerate(dest):
            d[...] = got[i * n:(i + 1) * n]

    @pl.when(jnp.logical_not(fast))
    def _():
        cols = lax.broadcasted_iota(jnp.int32, (n, n), 1)

        def step(j, _):
            e = gap(total, j) * row(unit, j)
            for d, p in zip(dest, probs):
                d[...] = jnp.where(cols == j, jnp.sum(p * e, axis=1, keepdims=True), d[...])
            return 0

        lax.fori_loop(0, n, step, 0)


def sum_over_t(mats, probs, total, fast, dest):
    n = total.shape[0]

    @pl.when(fast)
    def _():
        near, far = far_near(total)
        got = mm3(jnp.concatenate(mats, axis=0), jnp.concatenate([p * near for p in probs], axis=0), TN)
        dest[...] = got * far

    @pl.when(jnp.logical_not(fast))
    def _():
        rows = lax.broadcasted_iota(jnp.int32, total.shape, 0)

        def step(j, _):
            e = gap(total, j)
            s = sum(column(m, j) * p for m, p in zip(mats, probs))
            dest[...] = jnp.where(rows == j, jnp.sum(s * e, axis=0, keepdims=True), dest[...])
            return 0

        lax.fori_loop(0, n, step, 0)


def mixer_forward(pre_ref, f_low_ref, wfu_ref, doc_col_ref, doc_row_ref, score_ref, mix_ref):
    pre = pre_ref[...]
    q, q_slope = swish_parts(pre[:, :HEAD])
    k, k_slope = swish_parts(pre[:, HEAD:2 * HEAD])
    q, k, v = q.astype(BF16), k.astype(BF16), pre[:, 2 * HEAD:3 * HEAD].astype(BF16)
    n = q.shape[0]
    tri = lower_tri(n)
    keep = tri & (doc_col_ref[0] == doc_row_ref[0])
    inner = jnp.where(keep, mm(q, k, NT) * HEAD ** -0.5, 0.0)
    f_pre, log_f = gates(f_low_ref[...], wfu_ref[...])
    total = mm_exact(tri.astype(BF16), log_f, NN)
    unit = 1.0 - jnp.exp(log_f)
    fast = jnp.min(total[-1:]) > -SPAN
    return q, k, v, q_slope, k_slope, keep, inner, f_pre, log_f, total, unit, fast


def forward_kernel(pre_ref, f_low_ref, wfu_ref, gain_ref, doc_col_ref, doc_row_ref, act_ref, score_ref, mix_ref):
    q, k, v, _, _, keep, inner, _, _, total, unit, fast = mixer_forward(
        pre_ref, f_low_ref, wfu_ref, doc_col_ref, doc_row_ref, score_ref, mix_ref)
    sum_over_j([inner], total, unit, fast, [score_ref])
    probs = softmax(score_ref[...])
    sum_over_m([probs], total, unit, fast, [mix_ref])
    mixing = jnp.where(keep, mix_ref[...], 0.0).astype(BF16)
    out = mm(mixing, v, NN)
    scale = lax.rsqrt(jnp.mean(out * out, axis=1, keepdims=True) + 1e-06)
    gate, _ = swish_parts(pre_ref[:, 3 * HEAD:])
    act_ref[...] = (out * scale * gain_ref[...] * gate).astype(BF16)


def backward_kernel(pre_ref, f_low_ref, wfu_ref, gain_ref, doc_col_ref, doc_row_ref, d_act_ref, *refs):
    d_pre_ref, d_f_ref, d_low_ref, g_gain_ref, score_ref, d_p_ref, mix_ref, d_inner_ref, k_ref = refs[-9:]
    q, k, v, q_slope, k_slope, keep, inner, f_pre, log_f, total, unit, fast = mixer_forward(
        pre_ref, f_low_ref, wfu_ref, doc_col_ref, doc_row_ref, score_ref, mix_ref)
    sum_over_j([inner], total, unit, fast, [score_ref])
    scores = score_ref[...]
    probs = softmax(scores)
    sum_over_m([probs], total, unit, fast, [mix_ref])
    mixing = jnp.where(keep, mix_ref[...], 0.0).astype(BF16)
    out = mm(mixing, v, NN)

    scale = lax.rsqrt(jnp.mean(out * out, axis=1, keepdims=True) + 1e-06)
    gain = gain_ref[...]
    gate, gate_slope = swish_parts(pre_ref[:, 3 * HEAD:])
    d_act = d_act_ref[...].astype(F32)
    d_gate = d_act * out * scale * gain * gate_slope
    d_norm = d_act * gate
    g_gain = jnp.sum(d_norm * out * scale, axis=0, keepdims=True)

    @pl.when(pl.program_id(0) == 0)
    def _():
        g_gain_ref[...] = jnp.zeros_like(g_gain_ref)

    g_gain_ref[...] += g_gain
    d_norm = d_norm * gain
    d_out = scale * (d_norm - out * (scale * scale) * jnp.mean(d_norm * out, axis=1, keepdims=True))
    d_out = d_out.astype(BF16)

    d_mix = jnp.where(keep, mm(d_out, v, NT), 0.0)
    d_v = mm(mixing, d_out, TN)
    sum_over_j([d_mix], total, unit, fast, [d_p_ref])
    d_p = d_p_ref[...]
    d_score = probs * (d_p - jnp.sum(probs * d_p, axis=1, keepdims=True))
    sum_over_m([d_score], total, unit, fast, [d_inner_ref])
    d_inner = jnp.where(keep, d_inner_ref[...], 0.0).astype(BF16)
    sum_over_t([d_mix, inner], [probs, d_score], total, fast, k_ref)
    k_sum = k_ref[...]
    d_total = probs * d_p + d_score * scores - unit * k_sum
    n = q.shape[0]
    tri = lower_tri(n).astype(BF16)
    d_log = mm_exact(tri, d_total, TN) - jnp.exp(log_f) * k_sum
    d_f = (d_log * (0.125 / (1.0 + jnp.exp(f_pre)))).astype(BF16)
    d_f_ref[...] = d_f
    d_low_ref[...] = mm(d_f, wfu_ref[...], NT).astype(BF16)
    d_q = mm(d_inner, k, NN) * HEAD ** -0.5
    d_k = mm(d_inner, q, TN) * HEAD ** -0.5
    d_pre_ref[:, :HEAD] = (d_q * q_slope).astype(BF16)
    d_pre_ref[:, HEAD:2 * HEAD] = (d_k * k_slope).astype(BF16)
    d_pre_ref[:, 2 * HEAD:3 * HEAD] = d_v.astype(BF16)
    d_pre_ref[:, 3 * HEAD:] = d_gate.astype(BF16)


def mixer_specs(length, rank, first=0):
    return [
        pl.BlockSpec((length, 4 * HEAD), lambda i: (i + first, 0)),
        pl.BlockSpec((length, rank), lambda i: (i + first, 0)),
        pl.BlockSpec((rank, SLOTS), lambda i: (0, 0)),
        pl.BlockSpec((1, HEAD), lambda i: (0, 0)),
        pl.BlockSpec((1, length, 1), lambda i: (i + first, 0, 0)),
        pl.BlockSpec((1, 1, length), lambda i: (i + first, 0, 0)),
    ]


def slots_forward(pre, f_low, wfu, gain, docs):
    count, length = docs.shape
    tm = pltpu.VMEM((length, SLOTS), F32)
    tj = pltpu.VMEM((length, length), F32)
    return pl.pallas_call(
        forward_kernel,
        out_shape=jax.ShapeDtypeStruct((count * length, HEAD), BF16),
        grid=(count,),
        in_specs=mixer_specs(length, f_low.shape[1]),
        out_specs=pl.BlockSpec((length, HEAD), lambda i: (i, 0)),
        scratch_shapes=[tm, tj],
        compiler_params=pltpu.CompilerParams(vmem_limit_bytes=32 << 20),
        name="slots_forward",
    )(pre, f_low, wfu, gain, docs[:, :, None], docs[:, None, :])


def slots_backward(pre, f_low, wfu, gain, docs, d_act, first, steps, begun=()):
    count, length = docs.shape
    rank = f_low.shape[1]
    tm = pltpu.VMEM((length, SLOTS), F32)
    tj = pltpu.VMEM((length, length), F32)
    block = lambda width: pl.BlockSpec((length, width), lambda i: (i + first, 0))
    return pl.pallas_call(
        backward_kernel,
        out_shape=(
            jax.ShapeDtypeStruct((count * length, 4 * HEAD), BF16),
            jax.ShapeDtypeStruct((count * length, SLOTS), BF16),
            jax.ShapeDtypeStruct((count * length, rank), BF16),
            jax.ShapeDtypeStruct((1, HEAD), F32),
        ),
        grid=(steps,),
        in_specs=mixer_specs(length, rank, first) + [block(HEAD)] + [pl.BlockSpec(memory_space=pl.ANY)] * len(begun),
        out_specs=(block(4 * HEAD), block(SLOTS), block(rank), pl.BlockSpec((1, HEAD), lambda i: (0, 0))),
        scratch_shapes=[tm, tm, tj, tj, tm],
        input_output_aliases={7 + i: i for i in range(len(begun))},
        compiler_params=pltpu.CompilerParams(vmem_limit_bytes=32 << 20),
        name="slots_backward",
    )(pre, f_low, wfu, gain, docs[:, :, None], docs[:, None, :], d_act, *begun)


def place(index, cs):
    return (index // (TP * cs), (index // cs) % TP, index % cs)


def greet_all(n, cs, me):
    barrier = pltpu.get_barrier_semaphore()

    def greet(step, _):
        pl.semaphore_signal(barrier, inc=1, device_id=place((me + step) % n, cs), device_id_type=pl.DeviceIdType.MESH)
        return 0

    lax.fori_loop(1, n, greet, 0)
    pl.semaphore_wait(barrier, n - 1)


def my_index(cs):
    return (lax.axis_index("z") * TP + lax.axis_index("t")) * cs + lax.axis_index("c")


def chip_peer(t, step):
    high, low = t // 2, t % 2
    return (high + step // 2) % 2 * 2 + (low + step % 2) % 2


def share_kernel(n, cs, x_ref, o_ref, send_sem, recv_sem):
    me = my_index(cs)
    greet_all(n, cs, me)

    def send(step, _):
        pltpu.make_async_remote_copy(
            src_ref=x_ref, dst_ref=o_ref.at[me], send_sem=send_sem, recv_sem=recv_sem,
            device_id=place((me + step) % n, cs), device_id_type=pl.DeviceIdType.MESH).start()
        return 0

    lax.fori_loop(1, n, send, 0)
    o_ref[me] = x_ref[...]
    others = o_ref.at[pl.ds(0, n - 1)]
    pltpu.make_async_copy(others, others, recv_sem).wait()
    pltpu.make_async_copy(others, others, send_sem).wait()


def share(x, n, cs, ident):
    return pl.pallas_call(
        functools.partial(share_kernel, n, cs),
        out_shape=jax.ShapeDtypeStruct((n,) + x.shape, x.dtype),
        in_specs=[pl.BlockSpec(memory_space=pltpu.VMEM)],
        out_specs=pl.BlockSpec(memory_space=pltpu.VMEM),
        scratch_shapes=[pltpu.SemaphoreType.DMA, pltpu.SemaphoreType.DMA],
        compiler_params=pltpu.CompilerParams(collective_id=ident, has_side_effects=True, vmem_limit_bytes=32 << 20),
        name="share_small",
    )(x)


def spread_kernel(count, *refs):
    srcs, (out, own_sem, send_sem, recv_sem) = refs[:count], refs[count:]
    z, t, c = (lax.axis_index(a) for a in ALL)
    greet_plane(z, t, c)
    width = srcs[0].shape[1] // TP

    def block(i, to, at):
        src = srcs[i].at[:, pl.ds(pl.multiple_of(to * width, 128), width)]
        return src, out.at[at, :, pl.ds(i * width, width)]

    copies = []
    for step in (3, 1, 2):
        peer = chip_peer(t, step)
        for i in range(count):
            src, dst = block(i, peer, t)
            copies.append(pltpu.make_async_remote_copy(
                src_ref=src, dst_ref=dst, send_sem=send_sem.at[step - 1, i], recv_sem=recv_sem.at[step - 1, i],
                device_id=(z, peer, c), device_id_type=pl.DeviceIdType.MESH))
            copies[-1].start()
    for i in range(count):
        src, dst = block(i, t, t)
        copies.append(pltpu.make_async_copy(src, dst, own_sem.at[i]))
        copies[-1].start()
    for copy in copies:
        copy.wait()


def spread(weights, ident):
    rows, columns = weights[0].shape
    anywhere = pl.BlockSpec(memory_space=pl.ANY)
    return pl.pallas_call(
        functools.partial(spread_kernel, len(weights)),
        out_shape=jax.ShapeDtypeStruct((TP, rows, len(weights) * columns // TP), weights[0].dtype),
        in_specs=[anywhere] * len(weights),
        out_specs=anywhere,
        scratch_shapes=block_sems(len(weights)),
        compiler_params=pltpu.CompilerParams(collective_id=ident, has_side_effects=True),
        name="spread",
    )(*weights)


def greet_plane(z, t, c):
    barrier = pltpu.get_barrier_semaphore()
    for step in (1, 2, 3):
        pl.semaphore_signal(barrier, inc=1, device_id=(z, chip_peer(t, step), c), device_id_type=pl.DeviceIdType.MESH)
    pl.semaphore_wait(barrier, TP - 1)


LANES = 128


def unit_runs(piece, units):
    cuts = sorted(set(range(0, units, piece)) | set(range(0, units, LANES)) | {units})
    return [(low, high - low) for low, high in zip(cuts, cuts[1:])]


def packed_at(unit, up):
    return unit // LANES * 2 * LANES + up * LANES + unit % LANES


def natural_at(unit, piece, chip):
    return (unit // piece * TP + chip) * piece + unit % piece


def spread_ff_kernel(piece, parts, wg_ref, wu_ref, *refs):
    outs, (packed, own_sem, send_sem, recv_sem) = refs[:len(parts)], refs[len(parts):]
    z, t, c = (lax.axis_index(a) for a in ALL)
    greet_plane(z, t, c)
    for j in range(TP):
        for up, w in enumerate((wg_ref, wu_ref)):
            for unit, count in unit_runs(piece, packed.shape[2] // 2):
                at, source = packed_at(unit, up), natural_at(unit, piece, j)
                packed[j, :, at:at + count] = w[:, source:source + count]
    copies = []
    for step in (3, 1, 2):
        peer = chip_peer(t, step)
        for i, ((low, high), out) in enumerate(zip(parts, outs)):
            copies.append(pltpu.make_async_remote_copy(
                src_ref=packed.at[peer, :, low:high], dst_ref=out.at[t], send_sem=send_sem.at[step - 1, i],
                recv_sem=recv_sem.at[step - 1, i], device_id=(z, peer, c), device_id_type=pl.DeviceIdType.MESH))
            copies[-1].start()
    for i, ((low, high), out) in enumerate(zip(parts, outs)):
        copies.append(pltpu.make_async_copy(packed.at[t, :, low:high], out.at[t], own_sem.at[i]))
        copies[-1].start()
    for copy in copies:
        copy.wait()


def spread_ff(w_gate, w_up, piece, parts, ident):
    rows, units = w_gate.shape
    fast = pl.BlockSpec(memory_space=pltpu.VMEM)
    anywhere = pl.BlockSpec(memory_space=pl.ANY)
    return pl.pallas_call(
        functools.partial(spread_ff_kernel, piece, parts),
        out_shape=tuple(jax.ShapeDtypeStruct((TP, rows, high - low), w_gate.dtype) for low, high in parts),
        in_specs=[fast, fast],
        out_specs=(anywhere,) * len(parts),
        scratch_shapes=[pltpu.VMEM((TP, rows, 2 * units // TP), w_gate.dtype)] + block_sems(len(parts)),
        compiler_params=pltpu.CompilerParams(collective_id=ident, has_side_effects=True, vmem_limit_bytes=32 << 20),
        name="spread_ff",
    )(w_gate, w_up)


def send_blocks(sources, targets, own_sem, send_sem, recv_sem):
    z, t, c = (lax.axis_index(a) for a in ALL)
    copies = []
    for step in (3, 1, 2):
        peer = chip_peer(t, step)
        for i, (source, target) in enumerate(zip(sources, targets)):
            copies.append(pltpu.make_async_remote_copy(
                src_ref=source.at[peer], dst_ref=target.at[t], send_sem=send_sem.at[step - 1, i],
                recv_sem=recv_sem.at[step - 1, i], device_id=(z, peer, c), device_id_type=pl.DeviceIdType.MESH))
            copies[-1].start()
    for i, (source, target) in enumerate(zip(sources, targets)):
        copies.append(pltpu.make_async_copy(source.at[t], target.at[t], own_sem.at[i]))
        copies[-1].start()
    return copies


def block_sems(count):
    return [pltpu.SemaphoreType.DMA((count,))] + [pltpu.SemaphoreType.DMA((TP - 1, count))] * 2


def ff_moves(piece, units, parts):
    moves = []
    for j in range(TP):
        for up in (0, 1):
            for unit, count in unit_runs(piece, units):
                at = packed_at(unit, up)
                source = [i for i, (low, high) in enumerate(parts) if low <= at < high][0]
                moves.append((up, natural_at(unit, piece, j), source, j, at - parts[source][0], count))
    return moves


def widen_kernel(moves, sources, *refs):
    for out, at, source, j, start, width in moves:
        refs[sources + out][:, at:at + width] = refs[source][j, :, start:start + width].astype(F32)


def widen(xs, moves, count, columns):
    fast = pl.BlockSpec(memory_space=pltpu.VMEM)
    return pl.pallas_call(
        functools.partial(widen_kernel, moves, len(xs)),
        out_shape=tuple(jax.ShapeDtypeStruct((xs[0].shape[1], columns), F32) for _ in range(count)),
        in_specs=[fast] * len(xs),
        out_specs=tuple(fast for _ in range(count)),
        compiler_params=pltpu.CompilerParams(vmem_limit_bytes=32 << 20),
        name="widen",
    )(*xs)


def finish_kernel(n, cs, x_ref, blocks_ref, o_ref, back_ref, got_ref, send_sem, recv_sem, *block_sem):
    me = my_index(cs)
    greet_all(n, cs, me)

    def send(step, _):
        peer = (me + step) % n
        pltpu.make_async_remote_copy(
            src_ref=x_ref.at[peer], dst_ref=got_ref.at[me], send_sem=send_sem, recv_sem=recv_sem,
            device_id=place(peer, cs), device_id_type=pl.DeviceIdType.MESH).start()
        return 0

    lax.fori_loop(1, n, send, 0)
    copies = send_blocks([blocks_ref], [back_ref], *block_sem)
    got_ref[me] = x_ref[me]
    others = got_ref.at[pl.ds(0, n - 1)]
    pltpu.make_async_copy(others, others, recv_sem).wait()
    pltpu.make_async_copy(others, others, send_sem).wait()
    o_ref[...] = jnp.sum(got_ref[...], axis=0)
    for copy in copies:
        copy.wait()


def finish(x, blocks, n, cs):
    anywhere = pl.BlockSpec(memory_space=pl.ANY)
    fast = pl.BlockSpec(memory_space=pltpu.VMEM)
    return pl.pallas_call(
        functools.partial(finish_kernel, n, cs),
        out_shape=(jax.ShapeDtypeStruct(x.shape[1:], x.dtype), jax.ShapeDtypeStruct(blocks.shape, blocks.dtype)),
        in_specs=[fast, anywhere],
        out_specs=(fast, anywhere),
        scratch_shapes=[pltpu.VMEM(x.shape, x.dtype), pltpu.SemaphoreType.DMA, pltpu.SemaphoreType.DMA] + block_sems(1),
        compiler_params=pltpu.CompilerParams(collective_id=1, has_side_effects=True, vmem_limit_bytes=32 << 20),
        name="finish",
    )(x, blocks)


def pack_rows(parts, unit):
    flat = jnp.concatenate(parts, axis=-1)
    size = flat.shape[-1]
    padded = -(-size // (unit * 128)) * unit * 128
    flat = jnp.pad(flat, [(0, 0)] * (flat.ndim - 1) + [(0, padded - size)])
    return flat.reshape(flat.shape[:-1] + (padded // 128, 128))


def cut(flat, sizes):
    at, pieces = 0, []
    for size in sizes:
        pieces.append(flat[..., at:at + size])
        at += size
    return pieces


def relay(p_ref, o_ref, got1, pass2, got2, sems, subs, middle, shared=True, beside=None, plane=False, cores=False):
    z, t, c = (lax.axis_index(a) for a in ALL)
    peers = {step: (z, chip_peer(t, step), c) for step in (1, 2)}
    barrier = pltpu.get_barrier_semaphore()
    met = [peers[1], peers[2]] + [(z, chip_peer(t, 3), c)] * plane + [(z, t, 1 - c)] * cores
    for device in met:
        pl.semaphore_signal(barrier, inc=1, device_id=device, device_id_type=pl.DeviceIdType.MESH)
    pl.semaphore_wait(barrier, len(met))
    send_sem, recv_sem = sems
    half = p_ref.shape[1] // 2
    size = half // subs
    ways = ((1, 2), (2, 1))
    copies = []

    def start(src, dst, step, slot, i):
        copy = pltpu.make_async_remote_copy(
            src_ref=src, dst_ref=dst, send_sem=send_sem.at[slot, i], recv_sem=recv_sem.at[slot, i],
            device_id=peers[step], device_id_type=pl.DeviceIdType.MESH)
        copy.start()
        copies.append(copy)
        return copy

    def part(w, i):
        return pl.ds(w * half + i * size, size)

    def local(i):
        return pl.ds(i * size, size)

    first = [[[start(p_ref.at[near if j == 0 else 3, part(w, i)], got1.at[w, j, local(i)], near, 2 * w + j, i)
               for j in (0, 1)] for w, (near, far) in enumerate(ways)] for i in range(subs)]
    second, third, fourth = [None] * subs, [None] * subs, []
    for i in range(subs + 2):
        if i < subs:
            second[i] = []
            for w, (near, far) in enumerate(ways):
                first[i][w][1].wait_recv()
                both = p_ref[far, part(w, i)].astype(F32) + got1[w, 1, local(i)].astype(F32)
                pass2[w, local(i)] = both.astype(BF16)
                second[i].append(start(pass2.at[w, local(i)], got2.at[w, local(i)], far, 4 + w, i))
        if 1 <= i <= subs:
            k = i - 1
            third[k] = []
            for w in (0, 1):
                first[k][w][0].wait_recv()
                second[k][w].wait_recv()
                total = p_ref[0, part(w, k)].astype(F32) + got1[w, 0, local(k)].astype(F32)
                total = total + got2[w, local(k)].astype(F32)
                rows = middle(w * half + k * size, size, total)
                if not shared:
                    o_ref[part(w, k)] = rows
                    continue
                o_ref[0, part(w, k)] = rows
                third[k].append([start(o_ref.at[0, part(w, k)], o_ref.at[step, part(w, k)], step, 5 + 2 * w + step, k)
                                 for step in (1, 2)])
        if beside is not None:
            beside(i)
        if i >= 2 and shared:
            k = i - 2
            for w, (near, far) in enumerate(ways):
                third[k][w][far - 1].wait_recv()
                fourth.append(start(o_ref.at[far, part(w, k)], o_ref.at[3, part(w, k)], near, 10 + w, k))
    for copy in copies:
        copy.wait_send()
    for k in range(subs if shared else 0):
        for w, (near, far) in enumerate(ways):
            third[k][w][near - 1].wait_recv()
    for copy in fourth:
        copy.wait_recv()


def forward_relay_kernel(unit, subs, p_ref, x_ref, gain_ref, o_ref, resid_ref, got1, pass2, got2, ordered, *sems):
    def middle(at, size, total):
        rows = pl.ds(at, size)
        resid = total + x_ref[rows].astype(F32)
        resid_ref[rows] = resid
        normed = resid * lax.rsqrt(jnp.mean(resid * resid, axis=1, keepdims=True) + 1e-06) * gain_ref[...]
        half = normed.shape[1] // 2
        for j in range(half // unit):
            for k in (0, 1):
                ordered[:, k * half + j * unit:k * half + (j + 1) * unit] = normed[:, (2 * j + k) * unit:(2 * j + k + 1) * unit]
        return ordered[...].astype(BF16)

    relay(p_ref, o_ref, got1, pass2, got2, sems, subs, middle)


def norm_backward(unit, resid_ref, gain_ref, g_gain_ref, ordered, finish):
    g_gain_ref[...] = jnp.zeros_like(g_gain_ref)

    def middle(at, size, total):
        rows = pl.ds(at, size)
        half = total.shape[1] // 2
        for j in range(half // unit):
            for k in (0, 1):
                ordered[:, (2 * j + k) * unit:(2 * j + k + 1) * unit] = total[:, k * half + j * unit:k * half + (j + 1) * unit]
        d = ordered[...]
        resid = resid_ref[rows].astype(F32)
        scale = lax.rsqrt(jnp.mean(resid * resid, axis=1, keepdims=True) + 1e-06)
        unit_resid = resid * scale
        g_gain_ref[...] += jnp.sum(d * unit_resid, axis=0, keepdims=True)
        d = d * gain_ref[...]
        d = scale * (d - unit_resid * jnp.mean(d * unit_resid, axis=1, keepdims=True))
        return finish(rows, d)

    return middle


def backward_relay_kernel(unit, subs, parts, p_ref, resid_ref, cot_ref, gain_ref, *refs):
    hidden_hbm, (branch_hbm, down_hbm, o_ref, d_resid_ref, g_gain_ref, g_down_hbm, terms_hbm, *refs) = refs[:parts], refs[parts:]
    (got1, pass2, got2, ordered, send_sem, recv_sem, hidden, branch, down, g_down, g_other, terms,
     in_sem, out_sem, core_send, core_recv) = refs
    z, t, c = (lax.axis_index(a) for a in ALL)
    loads, at = [], 0
    for source in hidden_hbm:
        loads.append((source, hidden.at[:, at:at + source.shape[1]]))
        at += source.shape[1]
    loads += [(branch_hbm, branch), (down_hbm, down)]
    loads = [pltpu.make_async_copy(src, dst, in_sem.at[i]) for i, (src, dst) in enumerate(loads)]
    for copy in loads:
        copy.start()
    width = branch.shape[1] // subs
    _, zs, cs, count, _ = g_down.shape
    stores, crossings = [], []

    def beside(i):
        if i == 0:
            for copy in loads:
                copy.wait()
        cols = slice(i * width, (i + 1) * width)
        if i < subs:
            g = mm(hidden[...], branch[:, cols], TN).astype(BF16)
            for j in range(zs):
                for k in range(cs):
                    at = (j * cs + k) * count
                    g_down[i, j, k] = g[at:at + count]
            crossings.append(pltpu.make_async_remote_copy(
                src_ref=g_down.at[i, :, 1 - c], dst_ref=g_other.at[i], send_sem=core_send.at[i], recv_sem=core_recv.at[i],
                device_id=(z, t, 1 - c), device_id_type=pl.DeviceIdType.MESH))
            crossings[i].start()
            terms[i] = mm(hidden[...], down[:, cols], NN).astype(BF16)
            stores.append(pltpu.make_async_copy(terms.at[i], terms_hbm.at[:, cols], out_sem.at[0, i]))
            stores[-1].start()
        if 1 <= i <= subs:
            k = i - 1
            crossings[k].wait()
            g_other[k] = (g_other[k].astype(F32) + g_down[k, :, c].astype(F32)).astype(BF16)
            stores.append(pltpu.make_async_copy(
                g_other.at[k], g_down_hbm.at[:, :, slice(k * width, (k + 1) * width)], out_sem.at[1, k]))
            stores[-1].start()

    def finish(rows, d):
        d = d + cot_ref[rows].astype(F32)
        d_resid_ref[rows] = d
        return d.astype(BF16)

    middle = norm_backward(unit, resid_ref, gain_ref, g_gain_ref, ordered, finish)
    relay(p_ref, o_ref, got1, pass2, got2, (send_sem, recv_sem), subs, middle, beside=beside, cores=True)
    for copy in stores:
        copy.wait()


def settle_kernel(unit, count, subs, p_ref, x_ref, d_resid_ref, gain_ref, d_low_ref, f_low_ref, d_f_ref, g_head_ref,
                  g_mlp_ref, act_hbm, d_attn_hbm, h_hbm, *refs):
    blocks, refs = refs[:count], refs[count:]
    o_ref, flat_ref, g_out_hbm, refs = refs[0], refs[1], refs[2], refs[3:]
    returned, refs = refs[:count], refs[count:]
    (got1, pass2, got2, ordered, send_sem, recv_sem, own_sem, back_send, back_recv,
     act, d_attn, h, g_out, g_sum, g_gain_ref, in_sem, core_send, core_recv, swap_own, swap_send, swap_recv) = refs
    z, t, c = (lax.axis_index(a) for a in ALL)
    loads = [pltpu.make_async_copy(src, dst, in_sem.at[i])
             for i, (src, dst) in enumerate([(act_hbm, act), (d_attn_hbm, d_attn), (h_hbm, h)])]
    for copy in loads:
        copy.start()
    crossing = pltpu.make_async_remote_copy(
        src_ref=g_out.at[:, :, 1 - c], dst_ref=g_sum, send_sem=core_send, recv_sem=core_recv,
        device_id=(z, t, 1 - c), device_id_type=pl.DeviceIdType.MESH)
    copies = []
    n = flat_ref.shape[0]
    deep, _, cs, rows, D = g_out.shape
    rank = f_low_ref.shape[1]

    def beside(i):
        if i == 0:
            copies.extend(send_blocks(blocks, returned, own_sem, back_send, back_recv))
            for copy in loads:
                copy.wait()
            for low in range(0, D, D // 4):
                cols = slice(low, low + D // 4)
                g = mm(act[...], d_attn[:, cols], TN).astype(BF16)
                for j in range(deep):
                    for k in range(TP):
                        for m in range(cs):
                            at = ((j * TP + k) * cs + m) * rows
                            g_out[j, k, m, :, cols] = g[at:at + rows]
            crossing.start()
        if i == 1:
            crossing.wait()
            g_sum[...] = (g_sum[...].astype(F32) + g_out[:, :, c].astype(F32)).astype(BF16)
            for step in (3, 1, 2):
                peer = chip_peer(t, step)
                copies.append(pltpu.make_async_remote_copy(
                    src_ref=g_sum.at[:, peer], dst_ref=g_out_hbm.at[t], send_sem=swap_send.at[step - 1],
                    recv_sem=swap_recv.at[step - 1], device_id=(z, peer, c), device_id_type=pl.DeviceIdType.MESH))
                copies[-1].start()
            copies.append(pltpu.make_async_copy(g_sum.at[:, t], g_out_hbm.at[t], swap_own))
            copies[-1].start()
        if i == 2:
            flat_ref[...] = jnp.zeros_like(flat_ref)
            g_fd = mm(d_low_ref[...], h[...], TN)
            g_fu = mm(f_low_ref[...], d_f_ref[...], TN)
            zs = n // (TP * cs)
            each, wide = n // TP, g_fu.shape[1] * TP // n
            heads = g_head_ref.shape[1] // n
            for j in range(n):
                at = ((j % cs) * zs + j // (TP * cs)) * TP + j // cs % TP
                flat_ref[j, :rank, :unit] = g_fd[:, at * unit:(at + 1) * unit]
                flat_ref[j, rank:rank + 1, unit:unit + heads] = g_head_ref[:, j * heads:(j + 1) * heads]
                flat_ref[j, rank + 1:rank + 2, :unit] = g_mlp_ref[:, j * unit:(j + 1) * unit]
            for j in range(each):
                flat_ref[t * each + j, :rank, unit:unit + wide] = g_fu[:, j * wide:(j + 1) * wide]

    def finish(at, d):
        return (d + d_resid_ref[at]).astype(BF16)

    middle = norm_backward(unit, x_ref, gain_ref, g_gain_ref, ordered, finish)
    relay(p_ref, o_ref, got1, pass2, got2, (send_sem, recv_sem), subs, middle, False, beside, True, True)
    for j in range(n):
        flat_ref[j, rank:rank + 1, :unit] = g_gain_ref[:, j * unit:(j + 1) * unit]
    for copy in copies:
        copy.wait()


def relay_scratch(count, D, subs):
    half, size = count // 2, count // 2 // subs
    return [
        pltpu.VMEM((2, 2, half, D), BF16),
        pltpu.VMEM((2, half, D), BF16),
        pltpu.VMEM((2, half, D), BF16),
        pltpu.VMEM((size, D), F32),
        pltpu.SemaphoreType.DMA((12, subs)),
        pltpu.SemaphoreType.DMA((12, subs)),
    ]


SUBS = 4


def relay_forward(p, x, gain, unit, ident):
    _, count, D = p.shape
    fast = pl.BlockSpec(memory_space=pltpu.VMEM)
    return pl.pallas_call(
        functools.partial(forward_relay_kernel, unit, SUBS),
        out_shape=(jax.ShapeDtypeStruct(p.shape, BF16), jax.ShapeDtypeStruct(x.shape, F32)),
        in_specs=[fast] * 3,
        out_specs=(fast,) * 2,
        scratch_shapes=relay_scratch(count, D, SUBS),
        compiler_params=pltpu.CompilerParams(collective_id=ident, has_side_effects=True, vmem_limit_bytes=40 << 20),
        name="relay_forward",
    )(p, x, gain)


def relay_backward(p, resid, cot, gain, hidden, branch, down, unit, zs, cs, ident):
    _, count, D = p.shape
    tokens = hidden[0].shape[0]
    units = down.shape[0]
    width = D // SUBS
    each = units // (zs * cs)
    fast = pl.BlockSpec(memory_space=pltpu.VMEM)
    anywhere = pl.BlockSpec(memory_space=pl.ANY)
    return pl.pallas_call(
        functools.partial(backward_relay_kernel, unit, SUBS, len(hidden)),
        out_shape=(
            jax.ShapeDtypeStruct(p.shape, BF16),
            jax.ShapeDtypeStruct(resid.shape, F32),
            jax.ShapeDtypeStruct((1, D), F32),
            jax.ShapeDtypeStruct((zs, each, D), BF16),
            jax.ShapeDtypeStruct((tokens, D), BF16),
        ),
        in_specs=[fast] * 4 + [anywhere] * (len(hidden) + 2),
        out_specs=(fast,) * 3 + (anywhere,) * 2,
        scratch_shapes=relay_scratch(count, D, SUBS) + [
            pltpu.VMEM((tokens, units), BF16),
            pltpu.VMEM(branch.shape, BF16),
            pltpu.VMEM(down.shape, BF16),
            pltpu.VMEM((SUBS, zs, cs, each, width), BF16),
            pltpu.VMEM((SUBS, zs, each, width), BF16),
            pltpu.VMEM((SUBS, tokens, width), BF16),
            pltpu.SemaphoreType.DMA((len(hidden) + 2,)),
            pltpu.SemaphoreType.DMA((2, SUBS)),
            pltpu.SemaphoreType.DMA((SUBS,)),
            pltpu.SemaphoreType.DMA((SUBS,)),
        ],
        compiler_params=pltpu.CompilerParams(collective_id=ident, has_side_effects=True, vmem_limit_bytes=60 << 20),
        name="relay_backward",
    )(p, resid, cot, gain, *hidden, branch, down)


def settle(p, x, d_resid, gain, d_low, f_low, d_f, g_head, g_mlp, act, d_attn, h, blocks, unit, zs, cs, ident):
    _, count, D = p.shape
    fast = pl.BlockSpec(memory_space=pltpu.VMEM)
    anywhere = pl.BlockSpec(memory_space=pl.ANY)
    number = len(blocks)
    deep = zs // TP
    rank = f_low.shape[1]
    return pl.pallas_call(
        functools.partial(settle_kernel, unit, number, SUBS),
        out_shape=(
            jax.ShapeDtypeStruct(p.shape[1:], BF16),
            jax.ShapeDtypeStruct((zs * TP * cs, rank + 8, LANES), F32),
            jax.ShapeDtypeStruct((TP, deep, unit, D), BF16),
        ) + tuple(jax.ShapeDtypeStruct(b.shape, b.dtype) for b in blocks),
        in_specs=[fast] * 9 + [anywhere] * (3 + number),
        out_specs=(fast,) * 2 + (anywhere,) * (1 + number),
        scratch_shapes=relay_scratch(count, D, SUBS) + block_sems(number) + [
            pltpu.VMEM(act.shape, BF16),
            pltpu.VMEM(d_attn.shape, BF16),
            pltpu.VMEM(h.shape, BF16),
            pltpu.VMEM((deep, TP, cs, unit, D), BF16),
            pltpu.VMEM((deep, TP, unit, D), BF16),
            pltpu.VMEM((1, D), F32),
            pltpu.SemaphoreType.DMA((3,)),
            pltpu.SemaphoreType.DMA,
            pltpu.SemaphoreType.DMA,
            pltpu.SemaphoreType.DMA,
            pltpu.SemaphoreType.DMA((TP - 1,)),
            pltpu.SemaphoreType.DMA((TP - 1,)),
        ],
        compiler_params=pltpu.CompilerParams(collective_id=ident, has_side_effects=True, vmem_limit_bytes=56 << 20),
        name="settle",
    )(p, x, d_resid, gain, d_low, f_low, d_f, g_head, g_mlp, act, d_attn, h, *blocks)


def ff_kernel(tile, hm_ref, gu_ref, d_hidden_ref, hidden_ref, d_gu_ref):
    for at in range(0, hm_ref.shape[0], tile):
        rows = slice(at, at + tile)
        pre = mm(hm_ref[rows, :], gu_ref[...], NN)
        gate, up = pre[:, :LANES], pre[:, LANES:]
        sig = 0.5 * jnp.tanh(0.5 * gate) + 0.5
        act = gate * sig
        d_hidden = d_hidden_ref[rows, :]
        hidden_ref[rows, :] = (act * up).astype(BF16)
        d_gu_ref[rows, :LANES] = (d_hidden * up * (sig + act * (1.0 - sig))).astype(BF16)
        d_gu_ref[rows, LANES:] = (d_hidden * act).astype(BF16)


def ff_forward(hm, gu, d_hidden, first):
    tokens, D = hm.shape
    columns = gu.shape[1]
    wide = pl.BlockSpec((tokens, 2 * LANES), lambda j: (0, j))
    return pl.pallas_call(
        functools.partial(ff_kernel, 256),
        out_shape=(jax.ShapeDtypeStruct((tokens, columns // 2), BF16), jax.ShapeDtypeStruct((tokens, columns), BF16)),
        grid=(columns // (2 * LANES),),
        in_specs=[
            pl.BlockSpec((tokens, D), lambda j: (0, 0)),
            pl.BlockSpec((D, 2 * LANES), lambda j: (0, j)),
            pl.BlockSpec((tokens, LANES), lambda j: (0, j + first)),
        ],
        out_specs=(pl.BlockSpec((tokens, LANES), lambda j: (0, j)), wide),
        compiler_params=pltpu.CompilerParams(vmem_limit_bytes=48 << 20),
        name="feed_forward",
    )(hm, gu, d_hidden)


def d_hm_kernel(tile, count, *refs):
    grads, weights, o_ref = refs[:count], refs[count:2 * count], refs[2 * count]
    for at in range(0, o_ref.shape[0], tile):
        rows = slice(at, at + tile)
        o_ref[rows, :] = sum(mm(g[rows, :], w[...], NT) for g, w in zip(grads, weights)).astype(BF16)


def d_hm_product(grads, weights):
    tokens, D = grads[0].shape[0], weights[0].shape[0]
    width = 256
    return pl.pallas_call(
        functools.partial(d_hm_kernel, 256, len(grads)),
        out_shape=jax.ShapeDtypeStruct((tokens, D), BF16),
        grid=(D // width,),
        in_specs=[pl.BlockSpec(g.shape, lambda j: (0, 0)) for g in grads]
        + [pl.BlockSpec((width, w.shape[1]), lambda j: (j, 0)) for w in weights],
        out_specs=pl.BlockSpec((tokens, width), lambda j: (0, j)),
        compiler_params=pltpu.CompilerParams(vmem_limit_bytes=48 << 20),
        name="d_hm",
    )(*grads, *weights)


def send_t(x, step):
    return lax.ppermute(x, "t", [(i, i ^ step) for i in range(TP)])


def send_c(x):
    return lax.ppermute(x, "c", [(0, 1), (1, 0)])


def gather_t_begin(x):
    return send_t(x, 1), send_t(x, 2)


def gather_t_end(x, one, two):
    half = x.shape[0] // 2
    return jnp.concatenate([x, one, two, send_t(two[:half], 1), send_t(one[half:], 2)], axis=0)


def scatter_t_send(x):
    count = x.shape[0] // TP
    half = count // 2
    p = [(x[k * count:k * count + half], x[k * count + half:(k + 1) * count]) for k in range(TP)]
    return send_t(jnp.concatenate([p[1][0], p[3][0]], axis=0), 1), send_t(jnp.concatenate([p[2][1], p[3][1]], axis=0), 2)


def scatter_t_middle(x, got):
    count = x.shape[0] // TP
    half = count // 2
    first, second = got

    def add(low, v):
        return x[low:low + half].astype(F32) + v.astype(F32)

    on_a = add(2 * count, first[half:]).astype(BF16)
    on_b = add(count + half, second[half:]).astype(BF16)
    part = jnp.concatenate([add(0, first[:half]), add(half, second[:half])], axis=0)
    return part, (on_a, on_b)


def scatter_t_pass(passed):
    return send_t(passed[0], 2), send_t(passed[1], 1)


def swap_t(x):
    t = lax.axis_index("t")

    def block(a, j):
        return lax.dynamic_index_in_dim(a, j, 0, keepdims=False)

    got = jnp.stack([block(x, t)] + [send_t(block(x, t ^ k), k) for k in (1, 2, 3)])
    return jnp.stack([block(got, t ^ j) for j in range(TP)])


def dot(left, right):
    return mm(left, right, NN)


def dot_nt(left, right):
    return mm(left, right, NT)


def dot_tn(left, right):
    return mm(left, right, TN)


def after(x, *others):
    return lax.optimization_barrier((x,) + others)[:2]


def rms_norm(v, gain):
    return v * lax.rsqrt(jnp.mean(v * v, axis=-1, keepdims=True) + 1e-06) * gain


def swiglu(gate_val, up_val):
    return jax.nn.silu(gate_val) * up_val


def per_device(zs, cs, tokens, starts, w_query, w_key, w_value, w_gate_out, w_out, w_forget_down,
               w_forget_up, norm_attn, norm_head, norm_mlp, w_gate, w_up, w_down, cotangent):
    seqs, seq_len, D = tokens.shape
    n = zs * TP * cs
    rows = w_query.shape[0]
    ff_rows = w_down.shape[0]
    rank = w_forget_down.shape[1]
    fu_cols = w_forget_up.shape[1]
    mine = seqs * seq_len
    half = D // cs
    t_idx, c_idx = lax.axis_index("t"), lax.axis_index("c")

    def to_k(v):
        return v.reshape(-1, zs, TP, cs, rows).transpose(0, 3, 1, 2, 4).reshape(-1, D)

    def from_k(v):
        return v.reshape(-1, cs, zs, TP, rows).transpose(0, 2, 3, 1, 4).reshape(-1, D)

    def sum_z(v):
        return lax.psum_scatter(v, "z", scatter_dimension=0, tiled=True)

    def core_half(v, core):
        return lax.dynamic_slice_in_dim(v, core * half, half, axis=1)

    def other_term(left, right):
        return dot_tn(left, right).astype(BF16)

    def own_term(left, right, other):
        return (dot_tn(left, right) + send_c(other).astype(F32)).astype(BF16)

    docs = jnp.cumsum(starts, axis=1).astype(BF16)
    small = pack_rows([w_forget_down.reshape(-1), w_forget_up.reshape(-1), norm_attn, norm_head, norm_mlp,
                       docs.reshape(-1)], 16)
    sizes = [rows * rank, rank * fu_cols, norm_attn.shape[0], norm_head.shape[0], norm_mlp.shape[0]]
    by_rows = lax.all_gather(jnp.concatenate([w_out, w_down], axis=0), ("z", "c"), axis=0, tiled=True)
    by_rows = by_rows.reshape(zs, cs, rows + ff_rows, D)
    cot = cotangent.reshape(mine, D)
    w4 = spread([w_query, w_key, w_value, w_gate_out], 0)
    small, w4 = after(small, w4)
    small = share(small, n, cs, 9)
    piece = cs * ff_rows
    units = zs * piece
    middle = (units // LANES + 1) // 2 * 2 * LANES
    parts = ((0, middle), (middle, 2 * units))
    w_gate, small = after(w_gate, small)
    gus = spread_ff(w_gate, w_up, piece, parts, 2)
    pieces = cut(small.reshape(n, -1), sizes + [mine])
    wfd = to_k(pieces[0].reshape(D, rank).T).T
    wfu = pieces[1].reshape(n, rank, fu_cols).transpose(1, 0, 2).reshape(rank, n * fu_cols)
    wfu = lax.dynamic_slice_in_dim(wfu, t_idx * SLOTS, SLOTS, axis=1)
    gain_attn = pieces[2].reshape(-1).astype(F32)
    gain_head = pieces[3].reshape(1, -1).astype(F32)
    gain_mlp = pieces[4].reshape(1, -1).astype(F32)
    all_docs = pieces[5].reshape(zs, TP, cs, mine)
    all_docs = lax.dynamic_index_in_dim(all_docs, lax.axis_index("z"), 0, keepdims=False)
    all_docs = lax.dynamic_index_in_dim(all_docs, lax.axis_index("c"), 1, keepdims=False)
    docs = jnp.concatenate([lax.dynamic_index_in_dim(all_docs, t_idx ^ k, 0) for k in range(TP)], axis=0)
    docs = docs.astype(F32).reshape(TP * seqs, seq_len)

    def by_columns(w):
        return lax.all_gather(w.reshape(TP * rows, -1), ("c", "z"), axis=0, tiled=True)

    w4 = by_columns(w4)
    gus = [by_columns(gu) for gu in gus]
    down = by_rows[:, :, rows:].reshape(-1, D)
    wo = swap_t(by_rows[:, :, :rows].reshape(TP, -1, rows, D)).reshape(TP, zs // TP, cs, rows, D)
    wo = wo.transpose(1, 0, 2, 3, 4).reshape(HEAD, D)

    x = tokens.reshape(mine, D).astype(F32)
    normed_in, norm_in_back = jax.vjp(rms_norm, x, gain_attn)
    h = to_k(normed_in.astype(BF16))
    h = gather_t_end(h, *gather_t_begin(h))
    d_branch = gather_t_end(cot, *gather_t_begin(cot))
    d_hidden = dot_nt(d_branch, down)
    h, d_hidden = after(h, d_hidden)
    h, wo = after(h, wo)
    h_own, h_other = after(core_half(h, c_idx), core_half(h, 1 - c_idx))
    h, h_own = after(h, h_own)
    pre = dot(h, w4)
    f_low = dot(h, wfd).astype(BF16)
    act = slots_forward(pre, f_low, wfu, gain_head, docs)
    terms = dot(act, wo).astype(BF16)
    tokens_flat = tokens.reshape(mine, D)
    hm, resid = relay_forward(terms.reshape(TP, mine, D), tokens_flat, gain_mlp, rows, 6)
    hm = hm.reshape(TP * mine, D)

    hidden, d_gus, g_gus = [], [], []
    for gu, (low, _) in zip(gus, parts):
        part, d_gu = ff_forward(hm, gu, d_hidden, low // (2 * LANES))
        g_gu = own_term(core_half(hm, c_idx), d_gu, other_term(core_half(hm, 1 - c_idx), d_gu))
        hm, g_gu = after(hm, g_gu)
        hidden.append(part)
        d_gus.append(d_gu)
        g_gus.append(sum_z(g_gu).reshape(TP, rows, -1))
        last = g_gu
    d_gus[-1], _ = after(d_gus[-1], last)
    d_hm = d_hm_product(d_gus, gus)
    d_attn, d_resid, g_norm_mlp, g_down, branch = relay_backward(
        d_hm.reshape(TP, mine, D), resid, cot, gain_mlp, hidden, d_branch, down, rows, zs, cs, 7)
    d_attn = d_attn.reshape(TP * mine, D)
    g_down = sum_z(g_down.reshape(-1, D))

    d_attn, g_gus[0] = after(d_attn, g_gus[0])
    d_attn, g_gus[1] = after(d_attn, g_gus[1])
    first = scatter_t_send(branch)
    d_act = dot_nt(d_attn, wo)
    count = TP * seqs
    *begun, g_norm_head = slots_backward(pre, f_low, wfu, gain_head, docs, d_act, 0, count // 2)
    first, begun = after(first, begun)
    part, passed = scatter_t_middle(branch, first)
    d_act, passed = after(d_act, passed)
    second = scatter_t_pass(passed)
    d_pre, d_f, d_low, g_more = slots_backward(
        pre, f_low, wfu, gain_head, docs, d_act, count // 2, count - count // 2, begun)
    g_norm_head = g_norm_head + g_more
    g4 = other_term(h_other, d_pre)
    d_pre, g4 = after(d_pre, g4)
    d_h = (dot_nt(d_pre, w4) + dot_nt(d_low, wfd)).astype(BF16)
    d_pre, d_h = after(d_pre, d_h)
    d_pre, g_down = after(d_pre, g_down)
    d_pre, second = after(d_pre, second)
    g4 = own_term(h_own, d_pre, g4)
    d_h, _ = after(d_h, g4)
    g4 = sum_z(g4)
    tokens_grad, flat, g_out, *g_gus = settle(
        d_h.reshape(TP, mine, D), tokens_flat, d_resid, gain_attn.reshape(1, D), d_low, f_low, d_f, g_norm_head,
        g_norm_mlp, act, d_attn, h, g_gus, rows, zs, cs, 8)
    g_out = sum_z(g_out.reshape(-1, D))
    second, tokens_grad = after(second, tokens_grad)
    mixed = (resid + part + jnp.concatenate(second, axis=0).astype(F32)).astype(BF16)

    g_gate, g_up = widen(g_gus, ff_moves(piece, units, parts), 2, n * ff_rows)
    g_down = g_down.astype(F32)
    g4, mixed, tokens_grad, g_gate, g_up, g_down = lax.optimization_barrier(
        (g4, mixed, tokens_grad, g_gate, g_up, g_down))
    small, g4 = finish(flat, g4.reshape(TP, rows, -1), n, cs)
    heads = norm_head.shape[0]
    head_moves = [(i, j * HEAD, 0, j, i * HEAD, HEAD) for i in range(4) for j in range(TP)]
    g_heads, g_out = after(widen([g4], head_moves, 4, D), g_out)
    g_query, g_key, g_value, g_gate_out = g_heads
    g_out = g_out.astype(F32)
    return (
        mixed.reshape(tokens.shape),
        tokens_grad.reshape(tokens.shape),
        g_query, g_key, g_value, g_gate_out,
        g_out,
        small[:rank, :rows].T,
        small[:rank, rows:rows + fu_cols],
        small[rank, :rows],
        small[rank, rows:rows + heads],
        small[rank + 1, :rows],
        g_gate, g_up,
        g_down,
    )


def solution(mesh):
    cs = mesh.shape["outer"]
    zs = mesh.shape["dp"] // TP
    grid = Mesh(mesh.devices.reshape(zs, TP, cs), ALL)
    whole, row, vec = P(ALL, None, None), P(ALL, None), P(ALL)
    cols = P(None, ALL)

    def body(*args):
        return per_device(zs, cs, *args)

    return jax.shard_map(
        body,
        mesh=grid,
        in_specs=(whole, row, row, row, row, row, row, row, cols, vec, vec, vec, row, row, row, whole),
        out_specs=(whole, whole, row, row, row, row, row, row, cols, vec, vec, vec, row, row, row),
        check_vma=False,
    )
```

```python
import functools

import jax
import jax.numpy as jnp
from jax import lax
from jax.experimental import pallas as pl
from jax.experimental.pallas import tpu as pltpu
from jax.sharding import Mesh, PartitionSpec as P

HEADS = 4
HEAD = 512
SLOTS = 64
TP = 4
ALL = ("z", "t", "c")
F32 = jnp.float32
BF16 = jnp.bfloat16
SPAN = 80.0


def mm(a, b, dims):
    return lax.dot_general(a, b, (dims, ((), ())), preferred_element_type=F32)


NN, NT, TN = ((1,), (0,)), ((1,), (1,)), ((0,), (0,))


def split(a):
    high = a.astype(BF16)
    return high, (a - high.astype(F32)).astype(BF16)


def mm3(a, b, dims):
    ah, al = split(a)
    bh, bl = split(b)
    return mm(ah, bh, dims) + (mm(ah, bl, dims) + mm(al, bh, dims))


def mm_exact(mask, b, dims):
    b1, rest = split(b)
    b2 = rest
    b3 = (b - b1.astype(F32) - b2.astype(F32)).astype(BF16)
    return mm(mask, b1, dims) + (mm(mask, b2, dims) + mm(mask, b3, dims))


def swish_parts(v):
    sig = 1.0 / (1.0 + jnp.exp(-v))
    return v * sig, sig * (1.0 + v * (1.0 - sig))


def gates(f_low, wfu):
    f_pre = mm(f_low, wfu, NN)
    soft = jnp.log(1.0 + jnp.exp(-jnp.abs(f_pre)))
    log_f = (jnp.minimum(f_pre, 0.0) - soft) * 0.125
    return f_pre, log_f


def lower_tri(n, kind=BF16):
    rows = lax.broadcasted_iota(jnp.int32, (n, n), 0)
    cols = lax.broadcasted_iota(jnp.int32, (n, n), 1)
    return rows >= cols


def column(a, j):
    picked = lax.broadcasted_iota(jnp.int32, a.shape, 1) == j
    return jnp.sum(jnp.where(picked, a, 0.0), axis=1, keepdims=True)


def row(a, j):
    picked = lax.broadcasted_iota(jnp.int32, a.shape, 0) == j
    return jnp.sum(jnp.where(picked, a, 0.0), axis=0, keepdims=True)


def gap(total, j):
    return jnp.exp(jnp.minimum(total - row(total, j), 0.0))


def softmax(scores):
    e = jnp.exp(scores - jnp.max(scores, axis=1, keepdims=True))
    return e / jnp.sum(e, axis=1, keepdims=True)


def far_near(total):
    mid = 0.5 * total[-1:]
    return jnp.exp(total - mid), jnp.exp(mid - total)


def sum_over_j(mats, total, unit, fast, dest):
    n = total.shape[0]

    @pl.when(fast)
    def _():
        near, far = far_near(total)
        got = mm3(jnp.concatenate(mats, axis=0), far * unit, NN)
        for i, d in enumerate(dest):
            d[...] = got[i * n:(i + 1) * n] * near

    @pl.when(jnp.logical_not(fast))
    def _():
        for d in dest:
            d[...] = jnp.zeros_like(total)

        def step(j, _):
            e = gap(total, j) * row(unit, j)
            for d, m in zip(dest, mats):
                d[...] += column(m, j) * e
            return 0

        lax.fori_loop(0, n, step, 0)


def sum_over_m(probs, total, unit, fast, dest):
    n = total.shape[0]

    @pl.when(fast)
    def _():
        near, far = far_near(total)
        got = mm3(jnp.concatenate([p * near for p in probs], axis=0), far * unit, NT)
        for i, d in enumerate(dest):
            d[...] = got[i * n:(i + 1) * n]

    @pl.when(jnp.logical_not(fast))
    def _():
        cols = lax.broadcasted_iota(jnp.int32, (n, n), 1)

        def step(j, _):
            e = gap(total, j) * row(unit, j)
            for d, p in zip(dest, probs):
                d[...] = jnp.where(cols == j, jnp.sum(p * e, axis=1, keepdims=True), d[...])
            return 0

        lax.fori_loop(0, n, step, 0)


def sum_over_t(mats, probs, total, fast, dest):
    n = total.shape[0]

    @pl.when(fast)
    def _():
        near, far = far_near(total)
        got = mm3(jnp.concatenate(mats, axis=0), jnp.concatenate([p * near for p in probs], axis=0), TN)
        dest[...] = got * far

    @pl.when(jnp.logical_not(fast))
    def _():
        rows = lax.broadcasted_iota(jnp.int32, total.shape, 0)

        def step(j, _):
            e = gap(total, j)
            s = sum(column(m, j) * p for m, p in zip(mats, probs))
            dest[...] = jnp.where(rows == j, jnp.sum(s * e, axis=0, keepdims=True), dest[...])
            return 0

        lax.fori_loop(0, n, step, 0)


def mixer_forward(pre_ref, f_low_ref, wfu_ref, doc_col_ref, doc_row_ref, score_ref, mix_ref):
    pre = pre_ref[...]
    q, q_slope = swish_parts(pre[:, :HEAD])
    k, k_slope = swish_parts(pre[:, HEAD:2 * HEAD])
    q, k, v = q.astype(BF16), k.astype(BF16), pre[:, 2 * HEAD:3 * HEAD].astype(BF16)
    n = q.shape[0]
    tri = lower_tri(n)
    keep = tri & (doc_col_ref[0] == doc_row_ref[0])
    inner = jnp.where(keep, mm(q, k, NT) * HEAD ** -0.5, 0.0)
    f_pre, log_f = gates(f_low_ref[...], wfu_ref[...])
    total = mm_exact(tri.astype(BF16), log_f, NN)
    unit = 1.0 - jnp.exp(log_f)
    fast = jnp.min(total[-1:]) > -SPAN
    return q, k, v, q_slope, k_slope, keep, inner, f_pre, log_f, total, unit, fast


def forward_kernel(pre_ref, f_low_ref, wfu_ref, gain_ref, doc_col_ref, doc_row_ref, act_ref, score_ref, mix_ref):
    q, k, v, _, _, keep, inner, _, _, total, unit, fast = mixer_forward(
        pre_ref, f_low_ref, wfu_ref, doc_col_ref, doc_row_ref, score_ref, mix_ref)
    sum_over_j([inner], total, unit, fast, [score_ref])
    probs = softmax(score_ref[...])
    sum_over_m([probs], total, unit, fast, [mix_ref])
    mixing = jnp.where(keep, mix_ref[...], 0.0).astype(BF16)
    out = mm(mixing, v, NN)
    scale = lax.rsqrt(jnp.mean(out * out, axis=1, keepdims=True) + 1e-06)
    gate, _ = swish_parts(pre_ref[:, 3 * HEAD:])
    act_ref[...] = (out * scale * gain_ref[...] * gate).astype(BF16)


def backward_kernel(pre_ref, f_low_ref, wfu_ref, gain_ref, doc_col_ref, doc_row_ref, d_act_ref, *refs):
    d_pre_ref, d_f_ref, d_low_ref, g_gain_ref, score_ref, d_p_ref, mix_ref, d_inner_ref, k_ref = refs[-9:]
    q, k, v, q_slope, k_slope, keep, inner, f_pre, log_f, total, unit, fast = mixer_forward(
        pre_ref, f_low_ref, wfu_ref, doc_col_ref, doc_row_ref, score_ref, mix_ref)
    sum_over_j([inner], total, unit, fast, [score_ref])
    scores = score_ref[...]
    probs = softmax(scores)
    sum_over_m([probs], total, unit, fast, [mix_ref])
    mixing = jnp.where(keep, mix_ref[...], 0.0).astype(BF16)
    out = mm(mixing, v, NN)

    scale = lax.rsqrt(jnp.mean(out * out, axis=1, keepdims=True) + 1e-06)
    gain = gain_ref[...]
    gate, gate_slope = swish_parts(pre_ref[:, 3 * HEAD:])
    d_act = d_act_ref[...].astype(F32)
    d_gate = d_act * out * scale * gain * gate_slope
    d_norm = d_act * gate
    g_gain = jnp.sum(d_norm * out * scale, axis=0, keepdims=True)

    @pl.when(pl.program_id(0) == 0)
    def _():
        g_gain_ref[...] = jnp.zeros_like(g_gain_ref)

    g_gain_ref[...] += g_gain
    d_norm = d_norm * gain
    d_out = scale * (d_norm - out * (scale * scale) * jnp.mean(d_norm * out, axis=1, keepdims=True))
    d_out = d_out.astype(BF16)

    d_mix = jnp.where(keep, mm(d_out, v, NT), 0.0)
    d_v = mm(mixing, d_out, TN)
    sum_over_j([d_mix], total, unit, fast, [d_p_ref])
    d_p = d_p_ref[...]
    d_score = probs * (d_p - jnp.sum(probs * d_p, axis=1, keepdims=True))
    sum_over_m([d_score], total, unit, fast, [d_inner_ref])
    d_inner = jnp.where(keep, d_inner_ref[...], 0.0).astype(BF16)
    sum_over_t([d_mix, inner], [probs, d_score], total, fast, k_ref)
    k_sum = k_ref[...]
    d_total = probs * d_p + d_score * scores - unit * k_sum
    n = q.shape[0]
    tri = lower_tri(n).astype(BF16)
    d_log = mm_exact(tri, d_total, TN) - jnp.exp(log_f) * k_sum
    d_f = (d_log * (0.125 / (1.0 + jnp.exp(f_pre)))).astype(BF16)
    d_f_ref[...] = d_f
    d_low_ref[...] = mm(d_f, wfu_ref[...], NT).astype(BF16)
    d_q = mm(d_inner, k, NN) * HEAD ** -0.5
    d_k = mm(d_inner, q, TN) * HEAD ** -0.5
    d_pre_ref[:, :HEAD] = (d_q * q_slope).astype(BF16)
    d_pre_ref[:, HEAD:2 * HEAD] = (d_k * k_slope).astype(BF16)
    d_pre_ref[:, 2 * HEAD:3 * HEAD] = d_v.astype(BF16)
    d_pre_ref[:, 3 * HEAD:] = d_gate.astype(BF16)


def mixer_specs(length, rank, first=0):
    return [
        pl.BlockSpec((length, 4 * HEAD), lambda i: (i + first, 0)),
        pl.BlockSpec((length, rank), lambda i: (i + first, 0)),
        pl.BlockSpec((rank, SLOTS), lambda i: (0, 0)),
        pl.BlockSpec((1, HEAD), lambda i: (0, 0)),
        pl.BlockSpec((1, length, 1), lambda i: (i + first, 0, 0)),
        pl.BlockSpec((1, 1, length), lambda i: (i + first, 0, 0)),
    ]


def slots_forward(pre, f_low, wfu, gain, docs):
    count, length = docs.shape
    tm = pltpu.VMEM((length, SLOTS), F32)
    tj = pltpu.VMEM((length, length), F32)
    return pl.pallas_call(
        forward_kernel,
        out_shape=jax.ShapeDtypeStruct((count * length, HEAD), BF16),
        grid=(count,),
        in_specs=mixer_specs(length, f_low.shape[1]),
        out_specs=pl.BlockSpec((length, HEAD), lambda i: (i, 0)),
        scratch_shapes=[tm, tj],
        compiler_params=pltpu.CompilerParams(vmem_limit_bytes=32 << 20),
        name="slots_forward",
    )(pre, f_low, wfu, gain, docs[:, :, None], docs[:, None, :])


def slots_backward(pre, f_low, wfu, gain, docs, d_act, first, steps, begun=()):
    count, length = docs.shape
    rank = f_low.shape[1]
    tm = pltpu.VMEM((length, SLOTS), F32)
    tj = pltpu.VMEM((length, length), F32)
    block = lambda width: pl.BlockSpec((length, width), lambda i: (i + first, 0))
    return pl.pallas_call(
        backward_kernel,
        out_shape=(
            jax.ShapeDtypeStruct((count * length, 4 * HEAD), BF16),
            jax.ShapeDtypeStruct((count * length, SLOTS), BF16),
            jax.ShapeDtypeStruct((count * length, rank), BF16),
            jax.ShapeDtypeStruct((1, HEAD), F32),
        ),
        grid=(steps,),
        in_specs=mixer_specs(length, rank, first) + [block(HEAD)] + [pl.BlockSpec(memory_space=pl.ANY)] * len(begun),
        out_specs=(block(4 * HEAD), block(SLOTS), block(rank), pl.BlockSpec((1, HEAD), lambda i: (0, 0))),
        scratch_shapes=[tm, tm, tj, tj, tm],
        input_output_aliases={7 + i: i for i in range(len(begun))},
        compiler_params=pltpu.CompilerParams(vmem_limit_bytes=32 << 20),
        name="slots_backward",
    )(pre, f_low, wfu, gain, docs[:, :, None], docs[:, None, :], d_act, *begun)


def place(index, cs):
    return (index // (TP * cs), (index // cs) % TP, index % cs)


def greet_all(n, cs, me):
    barrier = pltpu.get_barrier_semaphore()

    def greet(step, _):
        pl.semaphore_signal(barrier, inc=1, device_id=place((me + step) % n, cs), device_id_type=pl.DeviceIdType.MESH)
        return 0

    lax.fori_loop(1, n, greet, 0)
    pl.semaphore_wait(barrier, n - 1)


def my_index(cs):
    return (lax.axis_index("z") * TP + lax.axis_index("t")) * cs + lax.axis_index("c")


def chip_peer(t, step):
    high, low = t // 2, t % 2
    return (high + step // 2) % 2 * 2 + (low + step % 2) % 2


def share_kernel(n, cs, x_ref, o_ref, send_sem, recv_sem):
    me = my_index(cs)
    greet_all(n, cs, me)

    def send(step, _):
        pltpu.make_async_remote_copy(
            src_ref=x_ref, dst_ref=o_ref.at[me], send_sem=send_sem, recv_sem=recv_sem,
            device_id=place((me + step) % n, cs), device_id_type=pl.DeviceIdType.MESH).start()
        return 0

    lax.fori_loop(1, n, send, 0)
    o_ref[me] = x_ref[...]
    others = o_ref.at[pl.ds(0, n - 1)]
    pltpu.make_async_copy(others, others, recv_sem).wait()
    pltpu.make_async_copy(others, others, send_sem).wait()


def share(x, n, cs, ident):
    return pl.pallas_call(
        functools.partial(share_kernel, n, cs),
        out_shape=jax.ShapeDtypeStruct((n,) + x.shape, x.dtype),
        in_specs=[pl.BlockSpec(memory_space=pltpu.VMEM)],
        out_specs=pl.BlockSpec(memory_space=pltpu.VMEM),
        scratch_shapes=[pltpu.SemaphoreType.DMA, pltpu.SemaphoreType.DMA],
        compiler_params=pltpu.CompilerParams(collective_id=ident, has_side_effects=True, vmem_limit_bytes=32 << 20),
        name="share_small",
    )(x)


def spread_kernel(count, *refs):
    srcs, (out, own_sem, send_sem, recv_sem) = refs[:count], refs[count:]
    z, t, c = (lax.axis_index(a) for a in ALL)
    greet_plane(z, t, c)
    width = srcs[0].shape[1] // TP

    def block(i, to, at):
        src = srcs[i].at[:, pl.ds(pl.multiple_of(to * width, 128), width)]
        return src, out.at[at, :, pl.ds(i * width, width)]

    copies = []
    for step in (3, 1, 2):
        peer = chip_peer(t, step)
        for i in range(count):
            src, dst = block(i, peer, t)
            copies.append(pltpu.make_async_remote_copy(
                src_ref=src, dst_ref=dst, send_sem=send_sem.at[step - 1, i], recv_sem=recv_sem.at[step - 1, i],
                device_id=(z, peer, c), device_id_type=pl.DeviceIdType.MESH))
            copies[-1].start()
    for i in range(count):
        src, dst = block(i, t, t)
        copies.append(pltpu.make_async_copy(src, dst, own_sem.at[i]))
        copies[-1].start()
    for copy in copies:
        copy.wait()


def spread(weights, ident):
    rows, columns = weights[0].shape
    anywhere = pl.BlockSpec(memory_space=pl.ANY)
    return pl.pallas_call(
        functools.partial(spread_kernel, len(weights)),
        out_shape=jax.ShapeDtypeStruct((TP, rows, len(weights) * columns // TP), weights[0].dtype),
        in_specs=[anywhere] * len(weights),
        out_specs=anywhere,
        scratch_shapes=block_sems(len(weights)),
        compiler_params=pltpu.CompilerParams(collective_id=ident, has_side_effects=True),
        name="spread",
    )(*weights)


def greet_plane(z, t, c):
    barrier = pltpu.get_barrier_semaphore()
    for step in (1, 2, 3):
        pl.semaphore_signal(barrier, inc=1, device_id=(z, chip_peer(t, step), c), device_id_type=pl.DeviceIdType.MESH)
    pl.semaphore_wait(barrier, TP - 1)


LANES = 128


def unit_runs(piece, units):
    cuts = sorted(set(range(0, units, piece)) | set(range(0, units, LANES)) | {units})
    return [(low, high - low) for low, high in zip(cuts, cuts[1:])]


def packed_at(unit, up):
    return unit // LANES * 2 * LANES + up * LANES + unit % LANES


def natural_at(unit, piece, chip):
    return (unit // piece * TP + chip) * piece + unit % piece


def spread_ff_kernel(piece, parts, wg_ref, wu_ref, *refs):
    outs, (packed, own_sem, send_sem, recv_sem) = refs[:len(parts)], refs[len(parts):]
    z, t, c = (lax.axis_index(a) for a in ALL)
    greet_plane(z, t, c)
    for j in range(TP):
        for up, w in enumerate((wg_ref, wu_ref)):
            for unit, count in unit_runs(piece, packed.shape[2] // 2):
                at, source = packed_at(unit, up), natural_at(unit, piece, j)
                packed[j, :, at:at + count] = w[:, source:source + count]
    copies = []
    for step in (3, 1, 2):
        peer = chip_peer(t, step)
        for i, ((low, high), out) in enumerate(zip(parts, outs)):
            copies.append(pltpu.make_async_remote_copy(
                src_ref=packed.at[peer, :, low:high], dst_ref=out.at[t], send_sem=send_sem.at[step - 1, i],
                recv_sem=recv_sem.at[step - 1, i], device_id=(z, peer, c), device_id_type=pl.DeviceIdType.MESH))
            copies[-1].start()
    for i, ((low, high), out) in enumerate(zip(parts, outs)):
        copies.append(pltpu.make_async_copy(packed.at[t, :, low:high], out.at[t], own_sem.at[i]))
        copies[-1].start()
    for copy in copies:
        copy.wait()


def spread_ff(w_gate, w_up, piece, parts, ident):
    rows, units = w_gate.shape
    fast = pl.BlockSpec(memory_space=pltpu.VMEM)
    anywhere = pl.BlockSpec(memory_space=pl.ANY)
    return pl.pallas_call(
        functools.partial(spread_ff_kernel, piece, parts),
        out_shape=tuple(jax.ShapeDtypeStruct((TP, rows, high - low), w_gate.dtype) for low, high in parts),
        in_specs=[fast, fast],
        out_specs=(anywhere,) * len(parts),
        scratch_shapes=[pltpu.VMEM((TP, rows, 2 * units // TP), w_gate.dtype)] + block_sems(len(parts)),
        compiler_params=pltpu.CompilerParams(collective_id=ident, has_side_effects=True, vmem_limit_bytes=32 << 20),
        name="spread_ff",
    )(w_gate, w_up)


def send_blocks(sources, targets, own_sem, send_sem, recv_sem):
    z, t, c = (lax.axis_index(a) for a in ALL)
    copies = []
    for step in (3, 1, 2):
        peer = chip_peer(t, step)
        for i, (source, target) in enumerate(zip(sources, targets)):
            copies.append(pltpu.make_async_remote_copy(
                src_ref=source.at[peer], dst_ref=target.at[t], send_sem=send_sem.at[step - 1, i],
                recv_sem=recv_sem.at[step - 1, i], device_id=(z, peer, c), device_id_type=pl.DeviceIdType.MESH))
            copies[-1].start()
    for i, (source, target) in enumerate(zip(sources, targets)):
        copies.append(pltpu.make_async_copy(source.at[t], target.at[t], own_sem.at[i]))
        copies[-1].start()
    return copies


def block_sems(count):
    return [pltpu.SemaphoreType.DMA((count,))] + [pltpu.SemaphoreType.DMA((TP - 1, count))] * 2


def ff_moves(piece, units, parts):
    moves = []
    for j in range(TP):
        for up in (0, 1):
            for unit, count in unit_runs(piece, units):
                at = packed_at(unit, up)
                source = [i for i, (low, high) in enumerate(parts) if low <= at < high][0]
                moves.append((up, natural_at(unit, piece, j), source, j, at - parts[source][0], count))
    return moves


def widen_kernel(moves, sources, *refs):
    for out, at, source, j, start, width in moves:
        refs[sources + out][:, at:at + width] = refs[source][j, :, start:start + width].astype(F32)


def widen(xs, moves, count, columns):
    fast = pl.BlockSpec(memory_space=pltpu.VMEM)
    return pl.pallas_call(
        functools.partial(widen_kernel, moves, len(xs)),
        out_shape=tuple(jax.ShapeDtypeStruct((xs[0].shape[1], columns), F32) for _ in range(count)),
        in_specs=[fast] * len(xs),
        out_specs=tuple(fast for _ in range(count)),
        compiler_params=pltpu.CompilerParams(vmem_limit_bytes=32 << 20),
        name="widen",
    )(*xs)


def finish_kernel(n, cs, x_ref, blocks_ref, o_ref, back_ref, got_ref, send_sem, recv_sem, *block_sem):
    me = my_index(cs)
    greet_all(n, cs, me)

    def send(step, _):
        peer = (me + step) % n
        pltpu.make_async_remote_copy(
            src_ref=x_ref.at[peer], dst_ref=got_ref.at[me], send_sem=send_sem, recv_sem=recv_sem,
            device_id=place(peer, cs), device_id_type=pl.DeviceIdType.MESH).start()
        return 0

    lax.fori_loop(1, n, send, 0)
    copies = send_blocks([blocks_ref], [back_ref], *block_sem)
    got_ref[me] = x_ref[me]
    others = got_ref.at[pl.ds(0, n - 1)]
    pltpu.make_async_copy(others, others, recv_sem).wait()
    pltpu.make_async_copy(others, others, send_sem).wait()
    o_ref[...] = jnp.sum(got_ref[...], axis=0)
    for copy in copies:
        copy.wait()


def finish(x, blocks, n, cs):
    anywhere = pl.BlockSpec(memory_space=pl.ANY)
    fast = pl.BlockSpec(memory_space=pltpu.VMEM)
    return pl.pallas_call(
        functools.partial(finish_kernel, n, cs),
        out_shape=(jax.ShapeDtypeStruct(x.shape[1:], x.dtype), jax.ShapeDtypeStruct(blocks.shape, blocks.dtype)),
        in_specs=[fast, anywhere],
        out_specs=(fast, anywhere),
        scratch_shapes=[pltpu.VMEM(x.shape, x.dtype), pltpu.SemaphoreType.DMA, pltpu.SemaphoreType.DMA] + block_sems(1),
        compiler_params=pltpu.CompilerParams(collective_id=1, has_side_effects=True, vmem_limit_bytes=32 << 20),
        name="finish",
    )(x, blocks)


def pack_rows(parts, unit):
    flat = jnp.concatenate(parts, axis=-1)
    size = flat.shape[-1]
    padded = -(-size // (unit * 128)) * unit * 128
    flat = jnp.pad(flat, [(0, 0)] * (flat.ndim - 1) + [(0, padded - size)])
    return flat.reshape(flat.shape[:-1] + (padded // 128, 128))


def cut(flat, sizes):
    at, pieces = 0, []
    for size in sizes:
        pieces.append(flat[..., at:at + size])
        at += size
    return pieces


def relay(p_ref, o_ref, got1, pass2, got2, sems, subs, middle, shared=True, beside=None, plane=False, cores=False):
    z, t, c = (lax.axis_index(a) for a in ALL)
    peers = {step: (z, chip_peer(t, step), c) for step in (1, 2)}
    barrier = pltpu.get_barrier_semaphore()
    met = [peers[1], peers[2]] + [(z, chip_peer(t, 3), c)] * plane + [(z, t, 1 - c)] * cores
    for device in met:
        pl.semaphore_signal(barrier, inc=1, device_id=device, device_id_type=pl.DeviceIdType.MESH)
    pl.semaphore_wait(barrier, len(met))
    send_sem, recv_sem = sems
    half = p_ref.shape[1] // 2
    size = half // subs
    ways = ((1, 2), (2, 1))
    copies = []

    def start(src, dst, step, slot, i):
        copy = pltpu.make_async_remote_copy(
            src_ref=src, dst_ref=dst, send_sem=send_sem.at[slot, i], recv_sem=recv_sem.at[slot, i],
            device_id=peers[step], device_id_type=pl.DeviceIdType.MESH)
        copy.start()
        copies.append(copy)
        return copy

    def part(w, i):
        return pl.ds(w * half + i * size, size)

    def local(i):
        return pl.ds(i * size, size)

    first = [[[start(p_ref.at[near if j == 0 else 3, part(w, i)], got1.at[w, j, local(i)], near, 2 * w + j, i)
               for j in (0, 1)] for w, (near, far) in enumerate(ways)] for i in range(subs)]
    second, third, fourth = [None] * subs, [None] * subs, []
    for i in range(subs + 2):
        if i < subs:
            second[i] = []
            for w, (near, far) in enumerate(ways):
                first[i][w][1].wait_recv()
                both = p_ref[far, part(w, i)].astype(F32) + got1[w, 1, local(i)].astype(F32)
                pass2[w, local(i)] = both.astype(BF16)
                second[i].append(start(pass2.at[w, local(i)], got2.at[w, local(i)], far, 4 + w, i))
        if 1 <= i <= subs:
            k = i - 1
            third[k] = []
            for w in (0, 1):
                first[k][w][0].wait_recv()
                second[k][w].wait_recv()
                total = p_ref[0, part(w, k)].astype(F32) + got1[w, 0, local(k)].astype(F32)
                total = total + got2[w, local(k)].astype(F32)
                rows = middle(w * half + k * size, size, total)
                if not shared:
                    o_ref[part(w, k)] = rows
                    continue
                o_ref[0, part(w, k)] = rows
                third[k].append([start(o_ref.at[0, part(w, k)], o_ref.at[step, part(w, k)], step, 5 + 2 * w + step, k)
                                 for step in (1, 2)])
        if beside is not None:
            beside(i)
        if i >= 2 and shared:
            k = i - 2
            for w, (near, far) in enumerate(ways):
                third[k][w][far - 1].wait_recv()
                fourth.append(start(o_ref.at[far, part(w, k)], o_ref.at[3, part(w, k)], near, 10 + w, k))
    for copy in copies:
        copy.wait_send()
    for k in range(subs if shared else 0):
        for w, (near, far) in enumerate(ways):
            third[k][w][near - 1].wait_recv()
    for copy in fourth:
        copy.wait_recv()


def forward_relay_kernel(unit, subs, p_ref, x_ref, gain_ref, o_ref, resid_ref, got1, pass2, got2, ordered, *sems):
    def middle(at, size, total):
        rows = pl.ds(at, size)
        resid = total + x_ref[rows].astype(F32)
        resid_ref[rows] = resid
        normed = resid * lax.rsqrt(jnp.mean(resid * resid, axis=1, keepdims=True) + 1e-06) * gain_ref[...]
        half = normed.shape[1] // 2
        for j in range(half // unit):
            for k in (0, 1):
                ordered[:, k * half + j * unit:k * half + (j + 1) * unit] = normed[:, (2 * j + k) * unit:(2 * j + k + 1) * unit]
        return ordered[...].astype(BF16)

    relay(p_ref, o_ref, got1, pass2, got2, sems, subs, middle)


def norm_backward(unit, resid_ref, gain_ref, g_gain_ref, ordered, finish):
    g_gain_ref[...] = jnp.zeros_like(g_gain_ref)

    def middle(at, size, total):
        rows = pl.ds(at, size)
        half = total.shape[1] // 2
        for j in range(half // unit):
            for k in (0, 1):
                ordered[:, (2 * j + k) * unit:(2 * j + k + 1) * unit] = total[:, k * half + j * unit:k * half + (j + 1) * unit]
        d = ordered[...]
        resid = resid_ref[rows].astype(F32)
        scale = lax.rsqrt(jnp.mean(resid * resid, axis=1, keepdims=True) + 1e-06)
        unit_resid = resid * scale
        g_gain_ref[...] += jnp.sum(d * unit_resid, axis=0, keepdims=True)
        d = d * gain_ref[...]
        d = scale * (d - unit_resid * jnp.mean(d * unit_resid, axis=1, keepdims=True))
        return finish(rows, d)

    return middle


def backward_relay_kernel(unit, subs, parts, p_ref, resid_ref, cot_ref, gain_ref, *refs):
    hidden_hbm, (branch_hbm, down_hbm, o_ref, d_resid_ref, g_gain_ref, g_down_hbm, terms_hbm, *refs) = refs[:parts], refs[parts:]
    (got1, pass2, got2, ordered, send_sem, recv_sem, hidden, branch, down, g_down, g_other, terms,
     in_sem, out_sem, core_send, core_recv) = refs
    z, t, c = (lax.axis_index(a) for a in ALL)
    loads, at = [], 0
    for source in hidden_hbm:
        loads.append((source, hidden.at[:, at:at + source.shape[1]]))
        at += source.shape[1]
    loads += [(branch_hbm, branch), (down_hbm, down)]
    loads = [pltpu.make_async_copy(src, dst, in_sem.at[i]) for i, (src, dst) in enumerate(loads)]
    for copy in loads:
        copy.start()
    width = branch.shape[1] // subs
    _, zs, cs, count, _ = g_down.shape
    stores, crossings = [], []

    def beside(i):
        if i == 0:
            for copy in loads:
                copy.wait()
        cols = slice(i * width, (i + 1) * width)
        if i < subs:
            g = mm(hidden[...], branch[:, cols], TN).astype(BF16)
            for j in range(zs):
                for k in range(cs):
                    at = (j * cs + k) * count
                    g_down[i, j, k] = g[at:at + count]
            crossings.append(pltpu.make_async_remote_copy(
                src_ref=g_down.at[i, :, 1 - c], dst_ref=g_other.at[i], send_sem=core_send.at[i], recv_sem=core_recv.at[i],
                device_id=(z, t, 1 - c), device_id_type=pl.DeviceIdType.MESH))
            crossings[i].start()
            terms[i] = mm(hidden[...], down[:, cols], NN).astype(BF16)
            stores.append(pltpu.make_async_copy(terms.at[i], terms_hbm.at[:, cols], out_sem.at[0, i]))
            stores[-1].start()
        if 1 <= i <= subs:
            k = i - 1
            crossings[k].wait()
            g_other[k] = (g_other[k].astype(F32) + g_down[k, :, c].astype(F32)).astype(BF16)
            stores.append(pltpu.make_async_copy(
                g_other.at[k], g_down_hbm.at[:, :, slice(k * width, (k + 1) * width)], out_sem.at[1, k]))
            stores[-1].start()

    def finish(rows, d):
        d = d + cot_ref[rows].astype(F32)
        d_resid_ref[rows] = d
        return d.astype(BF16)

    middle = norm_backward(unit, resid_ref, gain_ref, g_gain_ref, ordered, finish)
    relay(p_ref, o_ref, got1, pass2, got2, (send_sem, recv_sem), subs, middle, beside=beside, cores=True)
    for copy in stores:
        copy.wait()


def settle_kernel(unit, subs, p_ref, x_ref, d_resid_ref, gain_ref, d_low_ref, f_low_ref, d_f_ref, g_head_ref,
                  g_mlp_ref, act_hbm, d_attn_hbm, h_hbm, o_ref, flat_ref, g_out_hbm,
                  got1, pass2, got2, ordered, send_sem, recv_sem,
                  act, d_attn, h, g_out, g_sum, g_gain_ref, in_sem, core_send, core_recv, swap_own, swap_send, swap_recv):
    z, t, c = (lax.axis_index(a) for a in ALL)
    loads = [pltpu.make_async_copy(src, dst, in_sem.at[i])
             for i, (src, dst) in enumerate([(act_hbm, act), (d_attn_hbm, d_attn), (h_hbm, h)])]
    for copy in loads:
        copy.start()
    crossing = pltpu.make_async_remote_copy(
        src_ref=g_out.at[:, :, 1 - c], dst_ref=g_sum, send_sem=core_send, recv_sem=core_recv,
        device_id=(z, t, 1 - c), device_id_type=pl.DeviceIdType.MESH)
    copies = []
    n = flat_ref.shape[0]
    deep, _, cs, rows, D = g_out.shape
    rank = f_low_ref.shape[1]

    def beside(i):
        if i == 0:
            for copy in loads:
                copy.wait()
            for low in range(0, D, D // 4):
                cols = slice(low, low + D // 4)
                g = mm(act[...], d_attn[:, cols], TN).astype(BF16)
                for j in range(deep):
                    for k in range(TP):
                        for m in range(cs):
                            at = ((j * TP + k) * cs + m) * rows
                            g_out[j, k, m, :, cols] = g[at:at + rows]
            crossing.start()
        if i == 1:
            crossing.wait()
            g_sum[...] = (g_sum[...].astype(F32) + g_out[:, :, c].astype(F32)).astype(BF16)
            for step in (3, 1, 2):
                peer = chip_peer(t, step)
                copies.append(pltpu.make_async_remote_copy(
                    src_ref=g_sum.at[:, peer], dst_ref=g_out_hbm.at[t], send_sem=swap_send.at[step - 1],
                    recv_sem=swap_recv.at[step - 1], device_id=(z, peer, c), device_id_type=pl.DeviceIdType.MESH))
                copies[-1].start()
            copies.append(pltpu.make_async_copy(g_sum.at[:, t], g_out_hbm.at[t], swap_own))
            copies[-1].start()
        if i == 2:
            flat_ref[...] = jnp.zeros_like(flat_ref)
            g_fd = mm(d_low_ref[...], h[...], TN)
            g_fu = mm(f_low_ref[...], d_f_ref[...], TN)
            zs = n // (TP * cs)
            each, wide = n // TP, g_fu.shape[1] * TP // n
            heads = g_head_ref.shape[1] // n
            for j in range(n):
                at = ((j % cs) * zs + j // (TP * cs)) * TP + j // cs % TP
                flat_ref[j, :rank, :unit] = g_fd[:, at * unit:(at + 1) * unit]
                flat_ref[j, rank:rank + 1, unit:unit + heads] = g_head_ref[:, j * heads:(j + 1) * heads]
                flat_ref[j, rank + 1:rank + 2, :unit] = g_mlp_ref[:, j * unit:(j + 1) * unit]
            for j in range(each):
                flat_ref[t * each + j, :rank, unit:unit + wide] = g_fu[:, j * wide:(j + 1) * wide]

    def finish(at, d):
        return (d + d_resid_ref[at]).astype(BF16)

    middle = norm_backward(unit, x_ref, gain_ref, g_gain_ref, ordered, finish)
    relay(p_ref, o_ref, got1, pass2, got2, (send_sem, recv_sem), subs, middle, False, beside, True, True)
    for j in range(n):
        flat_ref[j, rank:rank + 1, :unit] = g_gain_ref[:, j * unit:(j + 1) * unit]
    for copy in copies:
        copy.wait()


def relay_scratch(count, D, subs):
    half, size = count // 2, count // 2 // subs
    return [
        pltpu.VMEM((2, 2, half, D), BF16),
        pltpu.VMEM((2, half, D), BF16),
        pltpu.VMEM((2, half, D), BF16),
        pltpu.VMEM((size, D), F32),
        pltpu.SemaphoreType.DMA((12, subs)),
        pltpu.SemaphoreType.DMA((12, subs)),
    ]


SUBS = 4


def relay_forward(p, x, gain, unit, ident):
    _, count, D = p.shape
    fast = pl.BlockSpec(memory_space=pltpu.VMEM)
    return pl.pallas_call(
        functools.partial(forward_relay_kernel, unit, SUBS),
        out_shape=(jax.ShapeDtypeStruct(p.shape, BF16), jax.ShapeDtypeStruct(x.shape, F32)),
        in_specs=[fast] * 3,
        out_specs=(fast,) * 2,
        scratch_shapes=relay_scratch(count, D, SUBS),
        compiler_params=pltpu.CompilerParams(collective_id=ident, has_side_effects=True, vmem_limit_bytes=40 << 20),
        name="relay_forward",
    )(p, x, gain)


def relay_backward(p, resid, cot, gain, hidden, branch, down, unit, zs, cs, ident):
    _, count, D = p.shape
    tokens = hidden[0].shape[0]
    units = down.shape[0]
    width = D // SUBS
    each = units // (zs * cs)
    fast = pl.BlockSpec(memory_space=pltpu.VMEM)
    anywhere = pl.BlockSpec(memory_space=pl.ANY)
    return pl.pallas_call(
        functools.partial(backward_relay_kernel, unit, SUBS, len(hidden)),
        out_shape=(
            jax.ShapeDtypeStruct(p.shape, BF16),
            jax.ShapeDtypeStruct(resid.shape, F32),
            jax.ShapeDtypeStruct((1, D), F32),
            jax.ShapeDtypeStruct((zs, each, D), BF16),
            jax.ShapeDtypeStruct((tokens, D), BF16),
        ),
        in_specs=[fast] * 4 + [anywhere] * (len(hidden) + 2),
        out_specs=(fast,) * 3 + (anywhere,) * 2,
        scratch_shapes=relay_scratch(count, D, SUBS) + [
            pltpu.VMEM((tokens, units), BF16),
            pltpu.VMEM(branch.shape, BF16),
            pltpu.VMEM(down.shape, BF16),
            pltpu.VMEM((SUBS, zs, cs, each, width), BF16),
            pltpu.VMEM((SUBS, zs, each, width), BF16),
            pltpu.VMEM((SUBS, tokens, width), BF16),
            pltpu.SemaphoreType.DMA((len(hidden) + 2,)),
            pltpu.SemaphoreType.DMA((2, SUBS)),
            pltpu.SemaphoreType.DMA((SUBS,)),
            pltpu.SemaphoreType.DMA((SUBS,)),
        ],
        compiler_params=pltpu.CompilerParams(collective_id=ident, has_side_effects=True, vmem_limit_bytes=60 << 20),
        name="relay_backward",
    )(p, resid, cot, gain, *hidden, branch, down)


def settle(p, x, d_resid, gain, d_low, f_low, d_f, g_head, g_mlp, act, d_attn, h, unit, zs, cs, ident):
    _, count, D = p.shape
    fast = pl.BlockSpec(memory_space=pltpu.VMEM)
    anywhere = pl.BlockSpec(memory_space=pl.ANY)
    deep = zs // TP
    rank = f_low.shape[1]
    return pl.pallas_call(
        functools.partial(settle_kernel, unit, SUBS),
        out_shape=(
            jax.ShapeDtypeStruct(p.shape[1:], BF16),
            jax.ShapeDtypeStruct((zs * TP * cs, rank + 8, LANES), F32),
            jax.ShapeDtypeStruct((TP, deep, unit, D), BF16),
        ),
        in_specs=[fast] * 9 + [anywhere] * 3,
        out_specs=(fast,) * 2 + (anywhere,),
        scratch_shapes=relay_scratch(count, D, SUBS) + [
            pltpu.VMEM(act.shape, BF16),
            pltpu.VMEM(d_attn.shape, BF16),
            pltpu.VMEM(h.shape, BF16),
            pltpu.VMEM((deep, TP, cs, unit, D), BF16),
            pltpu.VMEM((deep, TP, unit, D), BF16),
            pltpu.VMEM((1, D), F32),
            pltpu.SemaphoreType.DMA((3,)),
            pltpu.SemaphoreType.DMA,
            pltpu.SemaphoreType.DMA,
            pltpu.SemaphoreType.DMA,
            pltpu.SemaphoreType.DMA((TP - 1,)),
            pltpu.SemaphoreType.DMA((TP - 1,)),
        ],
        compiler_params=pltpu.CompilerParams(collective_id=ident, has_side_effects=True, vmem_limit_bytes=56 << 20),
        name="settle",
    )(p, x, d_resid, gain, d_low, f_low, d_f, g_head, g_mlp, act, d_attn, h)


def ff_kernel(tile, hm_ref, gu_ref, d_hidden_ref, hidden_ref, d_gu_ref):
    for at in range(0, hm_ref.shape[0], tile):
        rows = slice(at, at + tile)
        pre = mm(hm_ref[rows, :], gu_ref[...], NN)
        gate, up = pre[:, :LANES], pre[:, LANES:]
        sig = 0.5 * jnp.tanh(0.5 * gate) + 0.5
        act = gate * sig
        d_hidden = d_hidden_ref[rows, :]
        hidden_ref[rows, :] = (act * up).astype(BF16)
        d_gu_ref[rows, :LANES] = (d_hidden * up * (sig + act * (1.0 - sig))).astype(BF16)
        d_gu_ref[rows, LANES:] = (d_hidden * act).astype(BF16)


def ff_forward(hm, gu, d_hidden, first):
    tokens, D = hm.shape
    columns = gu.shape[1]
    wide = pl.BlockSpec((tokens, 2 * LANES), lambda j: (0, j))
    return pl.pallas_call(
        functools.partial(ff_kernel, 256),
        out_shape=(jax.ShapeDtypeStruct((tokens, columns // 2), BF16), jax.ShapeDtypeStruct((tokens, columns), BF16)),
        grid=(columns // (2 * LANES),),
        in_specs=[
            pl.BlockSpec((tokens, D), lambda j: (0, 0)),
            pl.BlockSpec((D, 2 * LANES), lambda j: (0, j)),
            pl.BlockSpec((tokens, LANES), lambda j: (0, j + first)),
        ],
        out_specs=(pl.BlockSpec((tokens, LANES), lambda j: (0, j)), wide),
        compiler_params=pltpu.CompilerParams(vmem_limit_bytes=48 << 20),
        name="feed_forward",
    )(hm, gu, d_hidden)


def d_hm_kernel(tile, count, *refs):
    grads, weights, o_ref = refs[:count], refs[count:2 * count], refs[2 * count]
    for at in range(0, o_ref.shape[0], tile):
        rows = slice(at, at + tile)
        o_ref[rows, :] = sum(mm(g[rows, :], w[...], NT) for g, w in zip(grads, weights)).astype(BF16)


def d_hm_product(grads, weights):
    tokens, D = grads[0].shape[0], weights[0].shape[0]
    width = 256
    return pl.pallas_call(
        functools.partial(d_hm_kernel, 256, len(grads)),
        out_shape=jax.ShapeDtypeStruct((tokens, D), BF16),
        grid=(D // width,),
        in_specs=[pl.BlockSpec(g.shape, lambda j: (0, 0)) for g in grads]
        + [pl.BlockSpec((width, w.shape[1]), lambda j: (j, 0)) for w in weights],
        out_specs=pl.BlockSpec((tokens, width), lambda j: (0, j)),
        compiler_params=pltpu.CompilerParams(vmem_limit_bytes=48 << 20),
        name="d_hm",
    )(*grads, *weights)


def heads_kernel(steps, count, own_hbm, other_hbm, d_pre_hbm, *refs):
    blocks, (o_hbm, *refs) = refs[:count], refs[count:]
    returned, refs = refs[:count], refs[count:]
    (own, other, d_pre, sent, got, own_sem, back_send, back_recv, in_sem, out_sem, core_send, core_recv) = refs
    z, t, c = (lax.axis_index(a) for a in ALL)
    width = d_pre.shape[2]
    cols = [slice(i * width, (i + 1) * width) for i in range(steps)]
    loads = [pltpu.make_async_copy(other_hbm, other, in_sem.at[0])]
    loads += [pltpu.make_async_copy(d_pre_hbm.at[:, cols[i]], d_pre.at[i], in_sem.at[2 + i]) for i in range(steps)]
    loads += [pltpu.make_async_copy(own_hbm, own, in_sem.at[1])]
    for copy in loads:
        copy.start()
    barrier = pltpu.get_barrier_semaphore()
    for device in [(z, chip_peer(t, step), c) for step in (1, 2, 3)] + [(z, t, 1 - c)]:
        pl.semaphore_signal(barrier, inc=1, device_id=device, device_id_type=pl.DeviceIdType.MESH)
    pl.semaphore_wait(barrier, TP)
    copies = send_blocks(blocks, returned, own_sem, back_send, back_recv)
    crossings = []
    loads[0].wait()
    for i in range(steps):
        loads[1 + i].wait()
        sent[i] = mm(other[...], d_pre[i], TN).astype(BF16)
        crossings.append(pltpu.make_async_remote_copy(
            src_ref=sent.at[i], dst_ref=got.at[i], send_sem=core_send.at[i], recv_sem=core_recv.at[i],
            device_id=(z, t, 1 - c), device_id_type=pl.DeviceIdType.MESH))
        crossings[i].start()
    loads[-1].wait()
    for i in range(steps):
        g = mm(own[...], d_pre[i], TN)
        crossings[i].wait_recv()
        got[i] = (g + got[i].astype(F32)).astype(BF16)
        copies.append(pltpu.make_async_copy(got.at[i], o_hbm.at[:, cols[i]], out_sem.at[i]))
        copies[-1].start()
    for copy in crossings:
        copy.wait_send()
    for copy in copies:
        copy.wait()


def heads_gradient(own, other, d_pre, blocks, ident):
    tokens, half = own.shape
    columns = d_pre.shape[1]
    steps = 4
    width = columns // steps
    count = len(blocks)
    anywhere = pl.BlockSpec(memory_space=pl.ANY)
    return pl.pallas_call(
        functools.partial(heads_kernel, steps, count),
        out_shape=(jax.ShapeDtypeStruct((half, columns), BF16),)
        + tuple(jax.ShapeDtypeStruct(b.shape, b.dtype) for b in blocks),
        in_specs=[anywhere] * (3 + count),
        out_specs=(anywhere,) * (1 + count),
        scratch_shapes=[
            pltpu.VMEM((tokens, half), BF16),
            pltpu.VMEM((tokens, half), BF16),
            pltpu.VMEM((steps, tokens, width), BF16),
            pltpu.VMEM((steps, half, width), BF16),
            pltpu.VMEM((steps, half, width), BF16),
        ] + block_sems(count) + [
            pltpu.SemaphoreType.DMA((2 + steps,)),
            pltpu.SemaphoreType.DMA((steps,)),
            pltpu.SemaphoreType.DMA((steps,)),
            pltpu.SemaphoreType.DMA((steps,)),
        ],
        compiler_params=pltpu.CompilerParams(collective_id=ident, has_side_effects=True, vmem_limit_bytes=56 << 20),
        name="heads_gradient",
    )(own, other, d_pre, *blocks)


def send_t(x, step):
    return lax.ppermute(x, "t", [(i, i ^ step) for i in range(TP)])


def send_c(x):
    return lax.ppermute(x, "c", [(0, 1), (1, 0)])


def gather_t_begin(x):
    return send_t(x, 1), send_t(x, 2)


def gather_t_end(x, one, two):
    half = x.shape[0] // 2
    return jnp.concatenate([x, one, two, send_t(two[:half], 1), send_t(one[half:], 2)], axis=0)


def scatter_t_send(x):
    count = x.shape[0] // TP
    half = count // 2
    p = [(x[k * count:k * count + half], x[k * count + half:(k + 1) * count]) for k in range(TP)]
    return send_t(jnp.concatenate([p[1][0], p[3][0]], axis=0), 1), send_t(jnp.concatenate([p[2][1], p[3][1]], axis=0), 2)


def scatter_t_middle(x, got):
    count = x.shape[0] // TP
    half = count // 2
    first, second = got

    def add(low, v):
        return x[low:low + half].astype(F32) + v.astype(F32)

    on_a = add(2 * count, first[half:]).astype(BF16)
    on_b = add(count + half, second[half:]).astype(BF16)
    part = jnp.concatenate([add(0, first[:half]), add(half, second[:half])], axis=0)
    return part, (on_a, on_b)


def scatter_t_pass(passed):
    return send_t(passed[0], 2), send_t(passed[1], 1)


def swap_t(x):
    t = lax.axis_index("t")

    def block(a, j):
        return lax.dynamic_index_in_dim(a, j, 0, keepdims=False)

    got = jnp.stack([block(x, t)] + [send_t(block(x, t ^ k), k) for k in (1, 2, 3)])
    return jnp.stack([block(got, t ^ j) for j in range(TP)])


def dot(left, right):
    return mm(left, right, NN)


def dot_nt(left, right):
    return mm(left, right, NT)


def dot_tn(left, right):
    return mm(left, right, TN)


def after(x, *others):
    return lax.optimization_barrier((x,) + others)[:2]


def rms_norm(v, gain):
    return v * lax.rsqrt(jnp.mean(v * v, axis=-1, keepdims=True) + 1e-06) * gain


def swiglu(gate_val, up_val):
    return jax.nn.silu(gate_val) * up_val


def per_device(zs, cs, tokens, starts, w_query, w_key, w_value, w_gate_out, w_out, w_forget_down,
               w_forget_up, norm_attn, norm_head, norm_mlp, w_gate, w_up, w_down, cotangent):
    seqs, seq_len, D = tokens.shape
    n = zs * TP * cs
    rows = w_query.shape[0]
    ff_rows = w_down.shape[0]
    rank = w_forget_down.shape[1]
    fu_cols = w_forget_up.shape[1]
    mine = seqs * seq_len
    half = D // cs
    t_idx, c_idx = lax.axis_index("t"), lax.axis_index("c")

    def to_k(v):
        return v.reshape(-1, zs, TP, cs, rows).transpose(0, 3, 1, 2, 4).reshape(-1, D)

    def from_k(v):
        return v.reshape(-1, cs, zs, TP, rows).transpose(0, 2, 3, 1, 4).reshape(-1, D)

    def sum_z(v):
        return lax.psum_scatter(v, "z", scatter_dimension=0, tiled=True)

    def core_half(v, core):
        return lax.dynamic_slice_in_dim(v, core * half, half, axis=1)

    def other_term(left, right):
        return dot_tn(left, right).astype(BF16)

    def own_term(left, right, other):
        return (dot_tn(left, right) + send_c(other).astype(F32)).astype(BF16)

    docs = jnp.cumsum(starts, axis=1).astype(BF16)
    small = pack_rows([w_forget_down.reshape(-1), w_forget_up.reshape(-1), norm_attn, norm_head, norm_mlp,
                       docs.reshape(-1)], 16)
    sizes = [rows * rank, rank * fu_cols, norm_attn.shape[0], norm_head.shape[0], norm_mlp.shape[0]]
    by_rows = lax.all_gather(jnp.concatenate([w_out, w_down], axis=0), ("z", "c"), axis=0, tiled=True)
    by_rows = by_rows.reshape(zs, cs, rows + ff_rows, D)
    cot = cotangent.reshape(mine, D)
    w4 = spread([w_query, w_key, w_value, w_gate_out], 0)
    small, w4 = after(small, w4)
    small = share(small, n, cs, 9)
    piece = cs * ff_rows
    units = zs * piece
    middle = (units // LANES + 1) // 2 * 2 * LANES
    parts = ((0, middle), (middle, 2 * units))
    w_gate, small = after(w_gate, small)
    gus = spread_ff(w_gate, w_up, piece, parts, 2)
    pieces = cut(small.reshape(n, -1), sizes + [mine])
    wfd = to_k(pieces[0].reshape(D, rank).T).T
    wfu = pieces[1].reshape(n, rank, fu_cols).transpose(1, 0, 2).reshape(rank, n * fu_cols)
    wfu = lax.dynamic_slice_in_dim(wfu, t_idx * SLOTS, SLOTS, axis=1)
    gain_attn = pieces[2].reshape(-1).astype(F32)
    gain_head = pieces[3].reshape(1, -1).astype(F32)
    gain_mlp = pieces[4].reshape(1, -1).astype(F32)
    all_docs = pieces[5].reshape(zs, TP, cs, mine)
    all_docs = lax.dynamic_index_in_dim(all_docs, lax.axis_index("z"), 0, keepdims=False)
    all_docs = lax.dynamic_index_in_dim(all_docs, lax.axis_index("c"), 1, keepdims=False)
    docs = jnp.concatenate([lax.dynamic_index_in_dim(all_docs, t_idx ^ k, 0) for k in range(TP)], axis=0)
    docs = docs.astype(F32).reshape(TP * seqs, seq_len)

    def by_columns(w):
        return lax.all_gather(w.reshape(TP * rows, -1), ("c", "z"), axis=0, tiled=True)

    w4 = by_columns(w4)
    gus = [by_columns(gu) for gu in gus]
    down = by_rows[:, :, rows:].reshape(-1, D)
    wo = swap_t(by_rows[:, :, :rows].reshape(TP, -1, rows, D)).reshape(TP, zs // TP, cs, rows, D)
    wo = wo.transpose(1, 0, 2, 3, 4).reshape(HEAD, D)

    x = tokens.reshape(mine, D).astype(F32)
    normed_in, norm_in_back = jax.vjp(rms_norm, x, gain_attn)
    h = to_k(normed_in.astype(BF16))
    h = gather_t_end(h, *gather_t_begin(h))
    d_branch = gather_t_end(cot, *gather_t_begin(cot))
    d_hidden = dot_nt(d_branch, down)
    h, d_hidden = after(h, d_hidden)
    h, wo = after(h, wo)
    h_own, h_other = after(core_half(h, c_idx), core_half(h, 1 - c_idx))
    h, h_own = after(h, h_own)
    pre = dot(h, w4)
    f_low = dot(h, wfd).astype(BF16)
    act = slots_forward(pre, f_low, wfu, gain_head, docs)
    terms = dot(act, wo).astype(BF16)
    tokens_flat = tokens.reshape(mine, D)
    hm, resid = relay_forward(terms.reshape(TP, mine, D), tokens_flat, gain_mlp, rows, 6)
    hm = hm.reshape(TP * mine, D)

    hidden, d_gus, g_gus = [], [], []
    for gu, (low, high) in zip(gus, parts):
        part, d_gu = ff_forward(hm, gu, d_hidden, low // (2 * LANES))
        hidden.append(part)
        d_gus.append(d_gu)
        g_gu = other_term(core_half(hm, 1 - c_idx), d_gu)
        if high == 2 * units:
            d_gus[-1], _ = after(d_gu, g_gu)
            d_hm = d_hm_product(d_gus, gus)
            hm, _ = after(hm, d_hm)
        g_gu = own_term(core_half(hm, c_idx), d_gu, g_gu)
        hm, g_gu = after(hm, g_gu)
        g_gus.append(sum_z(g_gu).reshape(TP, rows, -1))
    d_hm, _ = after(d_hm, g_gu)
    d_attn, d_resid, g_norm_mlp, g_down, branch = relay_backward(
        d_hm.reshape(TP, mine, D), resid, cot, gain_mlp, hidden, d_branch, down, rows, zs, cs, 7)
    d_attn = d_attn.reshape(TP * mine, D)
    g_down = sum_z(g_down.reshape(-1, D))

    d_attn, g_gus[0] = after(d_attn, g_gus[0])
    d_attn, g_gus[1] = after(d_attn, g_gus[1])
    first = scatter_t_send(branch)
    d_act = dot_nt(d_attn, wo)
    count = TP * seqs
    *begun, g_norm_head = slots_backward(pre, f_low, wfu, gain_head, docs, d_act, 0, count // 2)
    first, begun = after(first, begun)
    part, passed = scatter_t_middle(branch, first)
    d_act, passed = after(d_act, passed)
    second = scatter_t_pass(passed)
    d_pre, d_f, d_low, g_more = slots_backward(
        pre, f_low, wfu, gain_head, docs, d_act, count // 2, count - count // 2, begun)
    g_norm_head = g_norm_head + g_more
    d_pre, second = after(d_pre, second)
    g4, *g_gus = heads_gradient(h_own, h_other, d_pre, g_gus, 3)
    d_pre, _ = after(d_pre, g4)
    d_pre, g_down = after(d_pre, g_down)
    g4 = sum_z(g4)
    d_h = (dot_nt(d_pre, w4) + dot_nt(d_low, wfd)).astype(BF16)
    tokens_grad, flat, g_out = settle(
        d_h.reshape(TP, mine, D), tokens_flat, d_resid, gain_attn.reshape(1, D), d_low, f_low, d_f, g_norm_head,
        g_norm_mlp, act, d_attn, h, rows, zs, cs, 8)
    g_out = sum_z(g_out.reshape(-1, D))

    second, tokens_grad = after(second, tokens_grad)
    mixed = (resid + part + jnp.concatenate(second, axis=0).astype(F32)).astype(BF16)
    g_gate, g_up = widen(g_gus, ff_moves(piece, units, parts), 2, n * ff_rows)
    g_down = g_down.astype(F32)
    g4, mixed, tokens_grad, g_gate, g_up, g_down = lax.optimization_barrier(
        (g4, mixed, tokens_grad, g_gate, g_up, g_down))
    small, g4 = finish(flat, g4.reshape(TP, rows, -1), n, cs)
    heads = norm_head.shape[0]
    head_moves = [(i, j * HEAD, 0, j, i * HEAD, HEAD) for i in range(4) for j in range(TP)]
    g_heads, g_out = after(widen([g4], head_moves, 4, D), g_out)
    g_query, g_key, g_value, g_gate_out = g_heads
    g_out = g_out.astype(F32)
    return (
        mixed.reshape(tokens.shape),
        tokens_grad.reshape(tokens.shape),
        g_query, g_key, g_value, g_gate_out,
        g_out,
        small[:rank, :rows].T,
        small[:rank, rows:rows + fu_cols],
        small[rank, :rows],
        small[rank, rows:rows + heads],
        small[rank + 1, :rows],
        g_gate, g_up,
        g_down,
    )


def solution(mesh):
    cs = mesh.shape["outer"]
    zs = mesh.shape["dp"] // TP
    grid = Mesh(mesh.devices.reshape(zs, TP, cs), ALL)
    whole, row, vec = P(ALL, None, None), P(ALL, None), P(ALL)
    cols = P(None, ALL)

    def body(*args):
        return per_device(zs, cs, *args)

    return jax.shard_map(
        body,
        mesh=grid,
        in_specs=(whole, row, row, row, row, row, row, row, cols, vec, vec, vec, row, row, row, whole),
        out_specs=(whole, whole, row, row, row, row, row, row, cols, vec, vec, vec, row, row, row),
        check_vma=False,
    )
```

```python
import functools

import jax
import jax.numpy as jnp
from jax import lax
from jax.experimental import pallas as pl
from jax.experimental.pallas import tpu as pltpu
from jax.sharding import Mesh, PartitionSpec as P

HEADS = 4
HEAD = 512
SLOTS = 64
TP = 4
ALL = ("z", "t", "c")
F32 = jnp.float32
BF16 = jnp.bfloat16
SPAN = 80.0


def mm(a, b, dims):
    return lax.dot_general(a, b, (dims, ((), ())), preferred_element_type=F32)


NN, NT, TN = ((1,), (0,)), ((1,), (1,)), ((0,), (0,))


def split(a):
    high = a.astype(BF16)
    return high, (a - high.astype(F32)).astype(BF16)


def mm3(a, b, dims):
    ah, al = split(a)
    bh, bl = split(b)
    return mm(ah, bh, dims) + (mm(ah, bl, dims) + mm(al, bh, dims))


def mm_exact(mask, b, dims):
    b1, rest = split(b)
    b2 = rest
    b3 = (b - b1.astype(F32) - b2.astype(F32)).astype(BF16)
    return mm(mask, b1, dims) + (mm(mask, b2, dims) + mm(mask, b3, dims))


def swish_parts(v):
    sig = 1.0 / (1.0 + jnp.exp(-v))
    return v * sig, sig * (1.0 + v * (1.0 - sig))


def gates(f_low, wfu):
    f_pre = mm(f_low, wfu, NN)
    soft = jnp.log(1.0 + jnp.exp(-jnp.abs(f_pre)))
    log_f = (jnp.minimum(f_pre, 0.0) - soft) * 0.125
    return f_pre, log_f


def lower_tri(n, kind=BF16):
    rows = lax.broadcasted_iota(jnp.int32, (n, n), 0)
    cols = lax.broadcasted_iota(jnp.int32, (n, n), 1)
    return rows >= cols


def column(a, j):
    picked = lax.broadcasted_iota(jnp.int32, a.shape, 1) == j
    return jnp.sum(jnp.where(picked, a, 0.0), axis=1, keepdims=True)


def row(a, j):
    picked = lax.broadcasted_iota(jnp.int32, a.shape, 0) == j
    return jnp.sum(jnp.where(picked, a, 0.0), axis=0, keepdims=True)


def gap(total, j):
    return jnp.exp(jnp.minimum(total - row(total, j), 0.0))


def softmax(scores):
    e = jnp.exp(scores - jnp.max(scores, axis=1, keepdims=True))
    return e / jnp.sum(e, axis=1, keepdims=True)


def far_near(total):
    mid = 0.5 * total[-1:]
    return jnp.exp(total - mid), jnp.exp(mid - total)


def sum_over_j(mats, total, unit, fast, dest):
    n = total.shape[0]

    @pl.when(fast)
    def _():
        near, far = far_near(total)
        got = mm3(jnp.concatenate(mats, axis=0), far * unit, NN)
        for i, d in enumerate(dest):
            d[...] = got[i * n:(i + 1) * n] * near

    @pl.when(jnp.logical_not(fast))
    def _():
        for d in dest:
            d[...] = jnp.zeros_like(total)

        def step(j, _):
            e = gap(total, j) * row(unit, j)
            for d, m in zip(dest, mats):
                d[...] += column(m, j) * e
            return 0

        lax.fori_loop(0, n, step, 0)


def sum_over_m(probs, total, unit, fast, dest):
    n = total.shape[0]

    @pl.when(fast)
    def _():
        near, far = far_near(total)
        got = mm3(jnp.concatenate([p * near for p in probs], axis=0), far * unit, NT)
        for i, d in enumerate(dest):
            d[...] = got[i * n:(i + 1) * n]

    @pl.when(jnp.logical_not(fast))
    def _():
        cols = lax.broadcasted_iota(jnp.int32, (n, n), 1)

        def step(j, _):
            e = gap(total, j) * row(unit, j)
            for d, p in zip(dest, probs):
                d[...] = jnp.where(cols == j, jnp.sum(p * e, axis=1, keepdims=True), d[...])
            return 0

        lax.fori_loop(0, n, step, 0)


def sum_over_t(mats, probs, total, fast, dest):
    n = total.shape[0]

    @pl.when(fast)
    def _():
        near, far = far_near(total)
        got = mm3(jnp.concatenate(mats, axis=0), jnp.concatenate([p * near for p in probs], axis=0), TN)
        dest[...] = got * far

    @pl.when(jnp.logical_not(fast))
    def _():
        rows = lax.broadcasted_iota(jnp.int32, total.shape, 0)

        def step(j, _):
            e = gap(total, j)
            s = sum(column(m, j) * p for m, p in zip(mats, probs))
            dest[...] = jnp.where(rows == j, jnp.sum(s * e, axis=0, keepdims=True), dest[...])
            return 0

        lax.fori_loop(0, n, step, 0)


def mixer_forward(pre_ref, f_low_ref, wfu_ref, doc_col_ref, doc_row_ref, score_ref, mix_ref):
    pre = pre_ref[...]
    q, q_slope = swish_parts(pre[:, :HEAD])
    k, k_slope = swish_parts(pre[:, HEAD:2 * HEAD])
    q, k, v = q.astype(BF16), k.astype(BF16), pre[:, 2 * HEAD:3 * HEAD].astype(BF16)
    n = q.shape[0]
    tri = lower_tri(n)
    keep = tri & (doc_col_ref[0] == doc_row_ref[0])
    inner = jnp.where(keep, mm(q, k, NT) * HEAD ** -0.5, 0.0)
    f_pre, log_f = gates(f_low_ref[...], wfu_ref[...])
    total = mm_exact(tri.astype(BF16), log_f, NN)
    unit = 1.0 - jnp.exp(log_f)
    fast = jnp.min(total[-1:]) > -SPAN
    return q, k, v, q_slope, k_slope, keep, inner, f_pre, log_f, total, unit, fast


def forward_kernel(pre_ref, f_low_ref, wfu_ref, gain_ref, doc_col_ref, doc_row_ref, act_ref, score_ref, mix_ref):
    q, k, v, _, _, keep, inner, _, _, total, unit, fast = mixer_forward(
        pre_ref, f_low_ref, wfu_ref, doc_col_ref, doc_row_ref, score_ref, mix_ref)
    sum_over_j([inner], total, unit, fast, [score_ref])
    probs = softmax(score_ref[...])
    sum_over_m([probs], total, unit, fast, [mix_ref])
    mixing = jnp.where(keep, mix_ref[...], 0.0).astype(BF16)
    out = mm(mixing, v, NN)
    scale = lax.rsqrt(jnp.mean(out * out, axis=1, keepdims=True) + 1e-06)
    gate, _ = swish_parts(pre_ref[:, 3 * HEAD:])
    act_ref[...] = (out * scale * gain_ref[...] * gate).astype(BF16)


def backward_kernel(pre_ref, f_low_ref, wfu_ref, gain_ref, doc_col_ref, doc_row_ref, d_act_ref, *refs):
    d_pre_ref, d_f_ref, d_low_ref, g_gain_ref, score_ref, d_p_ref, mix_ref, d_inner_ref, k_ref = refs[-9:]
    q, k, v, q_slope, k_slope, keep, inner, f_pre, log_f, total, unit, fast = mixer_forward(
        pre_ref, f_low_ref, wfu_ref, doc_col_ref, doc_row_ref, score_ref, mix_ref)
    sum_over_j([inner], total, unit, fast, [score_ref])
    scores = score_ref[...]
    probs = softmax(scores)
    sum_over_m([probs], total, unit, fast, [mix_ref])
    mixing = jnp.where(keep, mix_ref[...], 0.0).astype(BF16)
    out = mm(mixing, v, NN)

    scale = lax.rsqrt(jnp.mean(out * out, axis=1, keepdims=True) + 1e-06)
    gain = gain_ref[...]
    gate, gate_slope = swish_parts(pre_ref[:, 3 * HEAD:])
    d_act = d_act_ref[...].astype(F32)
    d_gate = d_act * out * scale * gain * gate_slope
    d_norm = d_act * gate
    g_gain = jnp.sum(d_norm * out * scale, axis=0, keepdims=True)

    @pl.when(pl.program_id(0) == 0)
    def _():
        g_gain_ref[...] = jnp.zeros_like(g_gain_ref)

    g_gain_ref[...] += g_gain
    d_norm = d_norm * gain
    d_out = scale * (d_norm - out * (scale * scale) * jnp.mean(d_norm * out, axis=1, keepdims=True))
    d_out = d_out.astype(BF16)

    d_mix = jnp.where(keep, mm(d_out, v, NT), 0.0)
    d_v = mm(mixing, d_out, TN)
    sum_over_j([d_mix], total, unit, fast, [d_p_ref])
    d_p = d_p_ref[...]
    d_score = probs * (d_p - jnp.sum(probs * d_p, axis=1, keepdims=True))
    sum_over_m([d_score], total, unit, fast, [d_inner_ref])
    d_inner = jnp.where(keep, d_inner_ref[...], 0.0).astype(BF16)
    sum_over_t([d_mix, inner], [probs, d_score], total, fast, k_ref)
    k_sum = k_ref[...]
    d_total = probs * d_p + d_score * scores - unit * k_sum
    n = q.shape[0]
    tri = lower_tri(n).astype(BF16)
    d_log = mm_exact(tri, d_total, TN) - jnp.exp(log_f) * k_sum
    d_f = (d_log * (0.125 / (1.0 + jnp.exp(f_pre)))).astype(BF16)
    d_f_ref[...] = d_f
    d_low_ref[...] = mm(d_f, wfu_ref[...], NT).astype(BF16)
    d_q = mm(d_inner, k, NN) * HEAD ** -0.5
    d_k = mm(d_inner, q, TN) * HEAD ** -0.5
    d_pre_ref[:, :HEAD] = (d_q * q_slope).astype(BF16)
    d_pre_ref[:, HEAD:2 * HEAD] = (d_k * k_slope).astype(BF16)
    d_pre_ref[:, 2 * HEAD:3 * HEAD] = d_v.astype(BF16)
    d_pre_ref[:, 3 * HEAD:] = d_gate.astype(BF16)


def mixer_specs(length, rank, first=0):
    return [
        pl.BlockSpec((length, 4 * HEAD), lambda i: (i + first, 0)),
        pl.BlockSpec((length, rank), lambda i: (i + first, 0)),
        pl.BlockSpec((rank, SLOTS), lambda i: (0, 0)),
        pl.BlockSpec((1, HEAD), lambda i: (0, 0)),
        pl.BlockSpec((1, length, 1), lambda i: (i + first, 0, 0)),
        pl.BlockSpec((1, 1, length), lambda i: (i + first, 0, 0)),
    ]


def slots_forward(pre, f_low, wfu, gain, docs):
    count, length = docs.shape
    tm = pltpu.VMEM((length, SLOTS), F32)
    tj = pltpu.VMEM((length, length), F32)
    return pl.pallas_call(
        forward_kernel,
        out_shape=jax.ShapeDtypeStruct((count * length, HEAD), BF16),
        grid=(count,),
        in_specs=mixer_specs(length, f_low.shape[1]),
        out_specs=pl.BlockSpec((length, HEAD), lambda i: (i, 0)),
        scratch_shapes=[tm, tj],
        compiler_params=pltpu.CompilerParams(vmem_limit_bytes=32 << 20),
        name="slots_forward",
    )(pre, f_low, wfu, gain, docs[:, :, None], docs[:, None, :])


def slots_backward(pre, f_low, wfu, gain, docs, d_act, first, steps, begun=()):
    count, length = docs.shape
    rank = f_low.shape[1]
    tm = pltpu.VMEM((length, SLOTS), F32)
    tj = pltpu.VMEM((length, length), F32)
    block = lambda width: pl.BlockSpec((length, width), lambda i: (i + first, 0))
    return pl.pallas_call(
        backward_kernel,
        out_shape=(
            jax.ShapeDtypeStruct((count * length, 4 * HEAD), BF16),
            jax.ShapeDtypeStruct((count * length, SLOTS), BF16),
            jax.ShapeDtypeStruct((count * length, rank), BF16),
            jax.ShapeDtypeStruct((1, HEAD), F32),
        ),
        grid=(steps,),
        in_specs=mixer_specs(length, rank, first) + [block(HEAD)] + [pl.BlockSpec(memory_space=pl.ANY)] * len(begun),
        out_specs=(block(4 * HEAD), block(SLOTS), block(rank), pl.BlockSpec((1, HEAD), lambda i: (0, 0))),
        scratch_shapes=[tm, tm, tj, tj, tm],
        input_output_aliases={7 + i: i for i in range(len(begun))},
        compiler_params=pltpu.CompilerParams(vmem_limit_bytes=32 << 20),
        name="slots_backward",
    )(pre, f_low, wfu, gain, docs[:, :, None], docs[:, None, :], d_act, *begun)


def place(index, cs):
    return (index // (TP * cs), (index // cs) % TP, index % cs)


def greet_all(n, cs, me):
    barrier = pltpu.get_barrier_semaphore()

    def greet(step, _):
        pl.semaphore_signal(barrier, inc=1, device_id=place((me + step) % n, cs), device_id_type=pl.DeviceIdType.MESH)
        return 0

    lax.fori_loop(1, n, greet, 0)
    pl.semaphore_wait(barrier, n - 1)


def my_index(cs):
    return (lax.axis_index("z") * TP + lax.axis_index("t")) * cs + lax.axis_index("c")


def chip_peer(t, step):
    high, low = t // 2, t % 2
    return (high + step // 2) % 2 * 2 + (low + step % 2) % 2


def share_kernel(n, cs, x_ref, o_ref, send_sem, recv_sem):
    me = my_index(cs)
    greet_all(n, cs, me)

    def send(step, _):
        pltpu.make_async_remote_copy(
            src_ref=x_ref, dst_ref=o_ref.at[me], send_sem=send_sem, recv_sem=recv_sem,
            device_id=place((me + step) % n, cs), device_id_type=pl.DeviceIdType.MESH).start()
        return 0

    lax.fori_loop(1, n, send, 0)
    o_ref[me] = x_ref[...]
    others = o_ref.at[pl.ds(0, n - 1)]
    pltpu.make_async_copy(others, others, recv_sem).wait()
    pltpu.make_async_copy(others, others, send_sem).wait()


def share(x, n, cs, ident):
    return pl.pallas_call(
        functools.partial(share_kernel, n, cs),
        out_shape=jax.ShapeDtypeStruct((n,) + x.shape, x.dtype),
        in_specs=[pl.BlockSpec(memory_space=pltpu.VMEM)],
        out_specs=pl.BlockSpec(memory_space=pltpu.VMEM),
        scratch_shapes=[pltpu.SemaphoreType.DMA, pltpu.SemaphoreType.DMA],
        compiler_params=pltpu.CompilerParams(collective_id=ident, has_side_effects=True, vmem_limit_bytes=32 << 20),
        name="share_small",
    )(x)


def spread_kernel(count, *refs):
    srcs, (out, own_sem, send_sem, recv_sem) = refs[:count], refs[count:]
    z, t, c = (lax.axis_index(a) for a in ALL)
    greet_plane(z, t, c)
    width = srcs[0].shape[1] // TP

    def block(i, to, at):
        src = srcs[i].at[:, pl.ds(pl.multiple_of(to * width, 128), width)]
        return src, out.at[at, :, pl.ds(i * width, width)]

    copies = []
    for step in (3, 1, 2):
        peer = chip_peer(t, step)
        for i in range(count):
            src, dst = block(i, peer, t)
            copies.append(pltpu.make_async_remote_copy(
                src_ref=src, dst_ref=dst, send_sem=send_sem.at[step - 1, i], recv_sem=recv_sem.at[step - 1, i],
                device_id=(z, peer, c), device_id_type=pl.DeviceIdType.MESH))
            copies[-1].start()
    for i in range(count):
        src, dst = block(i, t, t)
        copies.append(pltpu.make_async_copy(src, dst, own_sem.at[i]))
        copies[-1].start()
    for copy in copies:
        copy.wait()


def spread(weights, ident):
    rows, columns = weights[0].shape
    anywhere = pl.BlockSpec(memory_space=pl.ANY)
    return pl.pallas_call(
        functools.partial(spread_kernel, len(weights)),
        out_shape=jax.ShapeDtypeStruct((TP, rows, len(weights) * columns // TP), weights[0].dtype),
        in_specs=[anywhere] * len(weights),
        out_specs=anywhere,
        scratch_shapes=block_sems(len(weights)),
        compiler_params=pltpu.CompilerParams(collective_id=ident, has_side_effects=True),
        name="spread",
    )(*weights)


def greet_plane(z, t, c):
    barrier = pltpu.get_barrier_semaphore()
    for step in (1, 2, 3):
        pl.semaphore_signal(barrier, inc=1, device_id=(z, chip_peer(t, step), c), device_id_type=pl.DeviceIdType.MESH)
    pl.semaphore_wait(barrier, TP - 1)


LANES = 128


def unit_runs(piece, units):
    cuts = sorted(set(range(0, units, piece)) | set(range(0, units, LANES)) | {units})
    return [(low, high - low) for low, high in zip(cuts, cuts[1:])]


def packed_at(unit, up):
    return unit // LANES * 2 * LANES + up * LANES + unit % LANES


def natural_at(unit, piece, chip):
    return (unit // piece * TP + chip) * piece + unit % piece


def spread_ff_kernel(piece, parts, wg_ref, wu_ref, *refs):
    outs, (packed, own_sem, send_sem, recv_sem) = refs[:len(parts)], refs[len(parts):]
    z, t, c = (lax.axis_index(a) for a in ALL)
    greet_plane(z, t, c)
    for j in range(TP):
        for up, w in enumerate((wg_ref, wu_ref)):
            for unit, count in unit_runs(piece, packed.shape[2] // 2):
                at, source = packed_at(unit, up), natural_at(unit, piece, j)
                packed[j, :, at:at + count] = w[:, source:source + count]
    copies = []
    for step in (3, 1, 2):
        peer = chip_peer(t, step)
        for i, ((low, high), out) in enumerate(zip(parts, outs)):
            copies.append(pltpu.make_async_remote_copy(
                src_ref=packed.at[peer, :, low:high], dst_ref=out.at[t], send_sem=send_sem.at[step - 1, i],
                recv_sem=recv_sem.at[step - 1, i], device_id=(z, peer, c), device_id_type=pl.DeviceIdType.MESH))
            copies[-1].start()
    for i, ((low, high), out) in enumerate(zip(parts, outs)):
        copies.append(pltpu.make_async_copy(packed.at[t, :, low:high], out.at[t], own_sem.at[i]))
        copies[-1].start()
    for copy in copies:
        copy.wait()


def spread_ff(w_gate, w_up, piece, parts, ident):
    rows, units = w_gate.shape
    fast = pl.BlockSpec(memory_space=pltpu.VMEM)
    anywhere = pl.BlockSpec(memory_space=pl.ANY)
    return pl.pallas_call(
        functools.partial(spread_ff_kernel, piece, parts),
        out_shape=tuple(jax.ShapeDtypeStruct((TP, rows, high - low), w_gate.dtype) for low, high in parts),
        in_specs=[fast, fast],
        out_specs=(anywhere,) * len(parts),
        scratch_shapes=[pltpu.VMEM((TP, rows, 2 * units // TP), w_gate.dtype)] + block_sems(len(parts)),
        compiler_params=pltpu.CompilerParams(collective_id=ident, has_side_effects=True, vmem_limit_bytes=32 << 20),
        name="spread_ff",
    )(w_gate, w_up)


def send_blocks(sources, targets, own_sem, send_sem, recv_sem):
    z, t, c = (lax.axis_index(a) for a in ALL)
    copies = []
    for step in (3, 1, 2):
        peer = chip_peer(t, step)
        for i, (source, target) in enumerate(zip(sources, targets)):
            copies.append(pltpu.make_async_remote_copy(
                src_ref=source.at[peer], dst_ref=target.at[t], send_sem=send_sem.at[step - 1, i],
                recv_sem=recv_sem.at[step - 1, i], device_id=(z, peer, c), device_id_type=pl.DeviceIdType.MESH))
            copies[-1].start()
    for i, (source, target) in enumerate(zip(sources, targets)):
        copies.append(pltpu.make_async_copy(source.at[t], target.at[t], own_sem.at[i]))
        copies[-1].start()
    return copies


def block_sems(count):
    return [pltpu.SemaphoreType.DMA((count,))] + [pltpu.SemaphoreType.DMA((TP - 1, count))] * 2


def ff_moves(piece, units, parts):
    moves = []
    for j in range(TP):
        for up in (0, 1):
            for unit, count in unit_runs(piece, units):
                at = packed_at(unit, up)
                source = [i for i, (low, high) in enumerate(parts) if low <= at < high][0]
                moves.append((up, natural_at(unit, piece, j), source, j, at - parts[source][0], count))
    return moves


def widen_kernel(moves, sources, *refs):
    for out, at, source, j, start, width in moves:
        refs[sources + out][:, at:at + width] = refs[source][j, :, start:start + width].astype(F32)


def widen(xs, moves, count, columns):
    fast = pl.BlockSpec(memory_space=pltpu.VMEM)
    return pl.pallas_call(
        functools.partial(widen_kernel, moves, len(xs)),
        out_shape=tuple(jax.ShapeDtypeStruct((xs[0].shape[1], columns), F32) for _ in range(count)),
        in_specs=[fast] * len(xs),
        out_specs=tuple(fast for _ in range(count)),
        compiler_params=pltpu.CompilerParams(vmem_limit_bytes=32 << 20),
        name="widen",
    )(*xs)


def finish_kernel(n, cs, x_ref, blocks_ref, o_ref, back_ref, got_ref, send_sem, recv_sem, *block_sem):
    me = my_index(cs)
    greet_all(n, cs, me)

    def send(step, _):
        peer = (me + step) % n
        pltpu.make_async_remote_copy(
            src_ref=x_ref.at[peer], dst_ref=got_ref.at[me], send_sem=send_sem, recv_sem=recv_sem,
            device_id=place(peer, cs), device_id_type=pl.DeviceIdType.MESH).start()
        return 0

    lax.fori_loop(1, n, send, 0)
    copies = send_blocks([blocks_ref], [back_ref], *block_sem)
    got_ref[me] = x_ref[me]
    others = got_ref.at[pl.ds(0, n - 1)]
    pltpu.make_async_copy(others, others, recv_sem).wait()
    pltpu.make_async_copy(others, others, send_sem).wait()
    o_ref[...] = jnp.sum(got_ref[...], axis=0)
    for copy in copies:
        copy.wait()


def finish(x, blocks, n, cs):
    anywhere = pl.BlockSpec(memory_space=pl.ANY)
    fast = pl.BlockSpec(memory_space=pltpu.VMEM)
    return pl.pallas_call(
        functools.partial(finish_kernel, n, cs),
        out_shape=(jax.ShapeDtypeStruct(x.shape[1:], x.dtype), jax.ShapeDtypeStruct(blocks.shape, blocks.dtype)),
        in_specs=[fast, anywhere],
        out_specs=(fast, anywhere),
        scratch_shapes=[pltpu.VMEM(x.shape, x.dtype), pltpu.SemaphoreType.DMA, pltpu.SemaphoreType.DMA] + block_sems(1),
        compiler_params=pltpu.CompilerParams(collective_id=1, has_side_effects=True, vmem_limit_bytes=32 << 20),
        name="finish",
    )(x, blocks)


def pack_rows(parts, unit):
    flat = jnp.concatenate(parts, axis=-1)
    size = flat.shape[-1]
    padded = -(-size // (unit * 128)) * unit * 128
    flat = jnp.pad(flat, [(0, 0)] * (flat.ndim - 1) + [(0, padded - size)])
    return flat.reshape(flat.shape[:-1] + (padded // 128, 128))


def cut(flat, sizes):
    at, pieces = 0, []
    for size in sizes:
        pieces.append(flat[..., at:at + size])
        at += size
    return pieces


def relay(p_ref, o_ref, got1, pass2, got2, sems, subs, middle, shared=True, beside=None, plane=False, cores=False):
    z, t, c = (lax.axis_index(a) for a in ALL)
    peers = {step: (z, chip_peer(t, step), c) for step in (1, 2)}
    barrier = pltpu.get_barrier_semaphore()
    met = [peers[1], peers[2]] + [(z, chip_peer(t, 3), c)] * plane + [(z, t, 1 - c)] * cores
    for device in met:
        pl.semaphore_signal(barrier, inc=1, device_id=device, device_id_type=pl.DeviceIdType.MESH)
    pl.semaphore_wait(barrier, len(met))
    send_sem, recv_sem = sems
    half = p_ref.shape[1] // 2
    size = half // subs
    ways = ((1, 2), (2, 1))
    copies = []

    def start(src, dst, step, slot, i):
        copy = pltpu.make_async_remote_copy(
            src_ref=src, dst_ref=dst, send_sem=send_sem.at[slot, i], recv_sem=recv_sem.at[slot, i],
            device_id=peers[step], device_id_type=pl.DeviceIdType.MESH)
        copy.start()
        copies.append(copy)
        return copy

    def part(w, i):
        return pl.ds(w * half + i * size, size)

    def local(i):
        return pl.ds(i * size, size)

    first = [[[start(p_ref.at[near if j == 0 else 3, part(w, i)], got1.at[w, j, local(i)], near, 2 * w + j, i)
               for j in (0, 1)] for w, (near, far) in enumerate(ways)] for i in range(subs)]
    second, third, fourth = [None] * subs, [None] * subs, []
    for i in range(subs + 2):
        if i < subs:
            second[i] = []
            for w, (near, far) in enumerate(ways):
                first[i][w][1].wait_recv()
                both = p_ref[far, part(w, i)].astype(F32) + got1[w, 1, local(i)].astype(F32)
                pass2[w, local(i)] = both.astype(BF16)
                second[i].append(start(pass2.at[w, local(i)], got2.at[w, local(i)], far, 4 + w, i))
        if 1 <= i <= subs:
            k = i - 1
            third[k] = []
            for w in (0, 1):
                first[k][w][0].wait_recv()
                second[k][w].wait_recv()
                total = p_ref[0, part(w, k)].astype(F32) + got1[w, 0, local(k)].astype(F32)
                total = total + got2[w, local(k)].astype(F32)
                rows = middle(w * half + k * size, size, total)
                if not shared:
                    o_ref[part(w, k)] = rows
                    continue
                o_ref[0, part(w, k)] = rows
                third[k].append([start(o_ref.at[0, part(w, k)], o_ref.at[step, part(w, k)], step, 5 + 2 * w + step, k)
                                 for step in (1, 2)])
        if beside is not None:
            beside(i)
        if i >= 2 and shared:
            k = i - 2
            for w, (near, far) in enumerate(ways):
                third[k][w][far - 1].wait_recv()
                fourth.append(start(o_ref.at[far, part(w, k)], o_ref.at[3, part(w, k)], near, 10 + w, k))
    for copy in copies:
        copy.wait_send()
    for k in range(subs if shared else 0):
        for w, (near, far) in enumerate(ways):
            third[k][w][near - 1].wait_recv()
    for copy in fourth:
        copy.wait_recv()


def forward_relay_kernel(unit, subs, p_ref, x_ref, gain_ref, o_ref, resid_ref, got1, pass2, got2, ordered, *sems):
    def middle(at, size, total):
        rows = pl.ds(at, size)
        resid = total + x_ref[rows].astype(F32)
        resid_ref[rows] = resid
        normed = resid * lax.rsqrt(jnp.mean(resid * resid, axis=1, keepdims=True) + 1e-06) * gain_ref[...]
        half = normed.shape[1] // 2
        for j in range(half // unit):
            for k in (0, 1):
                ordered[:, k * half + j * unit:k * half + (j + 1) * unit] = normed[:, (2 * j + k) * unit:(2 * j + k + 1) * unit]
        return ordered[...].astype(BF16)

    relay(p_ref, o_ref, got1, pass2, got2, sems, subs, middle)


def norm_backward(unit, resid_ref, gain_ref, g_gain_ref, ordered, finish):
    g_gain_ref[...] = jnp.zeros_like(g_gain_ref)

    def middle(at, size, total):
        rows = pl.ds(at, size)
        half = total.shape[1] // 2
        for j in range(half // unit):
            for k in (0, 1):
                ordered[:, (2 * j + k) * unit:(2 * j + k + 1) * unit] = total[:, k * half + j * unit:k * half + (j + 1) * unit]
        d = ordered[...]
        resid = resid_ref[rows].astype(F32)
        scale = lax.rsqrt(jnp.mean(resid * resid, axis=1, keepdims=True) + 1e-06)
        unit_resid = resid * scale
        g_gain_ref[...] += jnp.sum(d * unit_resid, axis=0, keepdims=True)
        d = d * gain_ref[...]
        d = scale * (d - unit_resid * jnp.mean(d * unit_resid, axis=1, keepdims=True))
        return finish(rows, d)

    return middle


def backward_relay_kernel(unit, subs, parts, p_ref, resid_ref, cot_ref, gain_ref, *refs):
    hidden_hbm, (branch_hbm, down_hbm, o_ref, d_resid_ref, g_gain_ref, g_down_hbm, kept_hbm, one_hbm, two_hbm, *refs) = refs[:parts], refs[parts:]
    (got1, pass2, got2, ordered, send_sem, recv_sem, hidden, branch, down, g_down, g_other, terms,
     in_sem, out_sem, core_send, core_recv) = refs
    z, t, c = (lax.axis_index(a) for a in ALL)
    loads, at = [], 0
    for source in hidden_hbm:
        loads.append((source, hidden.at[:, at:at + source.shape[1]]))
        at += source.shape[1]
    loads += [(branch_hbm, branch), (down_hbm, down)]
    loads = [pltpu.make_async_copy(src, dst, in_sem.at[i]) for i, (src, dst) in enumerate(loads)]
    for copy in loads:
        copy.start()
    width = branch.shape[1] // subs
    _, zs, cs, count, _ = g_down.shape
    stores, crossings = [], []

    def beside(i):
        if i == 0:
            for copy in loads:
                copy.wait()
        cols = slice(i * width, (i + 1) * width)
        if i < subs:
            g = mm(hidden[...], branch[:, cols], TN).astype(BF16)
            for j in range(zs):
                for k in range(cs):
                    at = (j * cs + k) * count
                    g_down[i, j, k] = g[at:at + count]
            crossings.append(pltpu.make_async_remote_copy(
                src_ref=g_down.at[i, :, 1 - c], dst_ref=g_other.at[i], send_sem=core_send.at[i], recv_sem=core_recv.at[i],
                device_id=(z, t, 1 - c), device_id_type=pl.DeviceIdType.MESH))
            crossings[i].start()
            terms[i] = mm(hidden[...], down[:, cols], NN).astype(BF16)
            half = terms.shape[1] // (2 * TP)
            places = ((kept_hbm, 0, 0, 2), (kept_hbm, 2, 4, 1), (kept_hbm, 3, 3, 1),
                      (one_hbm, 0, 2, 1), (one_hbm, 1, 6, 1), (two_hbm, 0, 5, 1), (two_hbm, 1, 7, 1))
            for j, (target, at, low, size) in enumerate(places):
                stores.append(pltpu.make_async_copy(
                    terms.at[i, low * half:(low + size) * half], target.at[at * half:(at + size) * half, cols], out_sem.at[j, i]))
                stores[-1].start()
        if 1 <= i <= subs:
            k = i - 1
            crossings[k].wait()
            g_other[k] = (g_other[k].astype(F32) + g_down[k, :, c].astype(F32)).astype(BF16)
            stores.append(pltpu.make_async_copy(
                g_other.at[k], g_down_hbm.at[:, :, slice(k * width, (k + 1) * width)], out_sem.at[7, k]))
            stores[-1].start()

    def finish(rows, d):
        d = d + cot_ref[rows].astype(F32)
        d_resid_ref[rows] = d
        return d.astype(BF16)

    middle = norm_backward(unit, resid_ref, gain_ref, g_gain_ref, ordered, finish)
    relay(p_ref, o_ref, got1, pass2, got2, (send_sem, recv_sem), subs, middle, beside=beside, cores=True)
    for copy in stores:
        copy.wait()


def settle_kernel(unit, subs, p_ref, x_ref, d_resid_ref, gain_ref, d_low_ref, f_low_ref, d_f_ref, g_head_ref,
                  g_mlp_ref, act_hbm, d_attn_hbm, h_hbm, o_ref, flat_ref, g_out_hbm,
                  got1, pass2, got2, ordered, send_sem, recv_sem,
                  act, d_attn, h, g_out, g_sum, g_gain_ref, in_sem, core_send, core_recv, swap_own, swap_send, swap_recv):
    z, t, c = (lax.axis_index(a) for a in ALL)
    loads = [pltpu.make_async_copy(src, dst, in_sem.at[i])
             for i, (src, dst) in enumerate([(act_hbm, act), (d_attn_hbm, d_attn), (h_hbm, h)])]
    for copy in loads:
        copy.start()
    crossing = pltpu.make_async_remote_copy(
        src_ref=g_out.at[:, :, 1 - c], dst_ref=g_sum, send_sem=core_send, recv_sem=core_recv,
        device_id=(z, t, 1 - c), device_id_type=pl.DeviceIdType.MESH)
    copies = []
    n = flat_ref.shape[0]
    deep, _, cs, rows, D = g_out.shape
    rank = f_low_ref.shape[1]

    def beside(i):
        if i == 0:
            for copy in loads:
                copy.wait()
            for low in range(0, D, D // 4):
                cols = slice(low, low + D // 4)
                g = mm(act[...], d_attn[:, cols], TN).astype(BF16)
                for j in range(deep):
                    for k in range(TP):
                        for m in range(cs):
                            at = ((j * TP + k) * cs + m) * rows
                            g_out[j, k, m, :, cols] = g[at:at + rows]
            crossing.start()
        if i == 1:
            crossing.wait()
            g_sum[...] = (g_sum[...].astype(F32) + g_out[:, :, c].astype(F32)).astype(BF16)
            for step in (3, 1, 2):
                peer = chip_peer(t, step)
                copies.append(pltpu.make_async_remote_copy(
                    src_ref=g_sum.at[:, peer], dst_ref=g_out_hbm.at[t], send_sem=swap_send.at[step - 1],
                    recv_sem=swap_recv.at[step - 1], device_id=(z, peer, c), device_id_type=pl.DeviceIdType.MESH))
                copies[-1].start()
            copies.append(pltpu.make_async_copy(g_sum.at[:, t], g_out_hbm.at[t], swap_own))
            copies[-1].start()
        if i == 2:
            flat_ref[...] = jnp.zeros_like(flat_ref)
            g_fd = mm(d_low_ref[...], h[...], TN)
            g_fu = mm(f_low_ref[...], d_f_ref[...], TN)
            zs = n // (TP * cs)
            each, wide = n // TP, g_fu.shape[1] * TP // n
            heads = g_head_ref.shape[1] // n
            for j in range(n):
                at = ((j % cs) * zs + j // (TP * cs)) * TP + j // cs % TP
                flat_ref[j, :rank, :unit] = g_fd[:, at * unit:(at + 1) * unit]
                flat_ref[j, rank:rank + 1, unit:unit + heads] = g_head_ref[:, j * heads:(j + 1) * heads]
                flat_ref[j, rank + 1:rank + 2, :unit] = g_mlp_ref[:, j * unit:(j + 1) * unit]
            for j in range(each):
                flat_ref[t * each + j, :rank, unit:unit + wide] = g_fu[:, j * wide:(j + 1) * wide]

    def finish(at, d):
        return (d + d_resid_ref[at]).astype(BF16)

    middle = norm_backward(unit, x_ref, gain_ref, g_gain_ref, ordered, finish)
    relay(p_ref, o_ref, got1, pass2, got2, (send_sem, recv_sem), subs, middle, False, beside, True, True)
    for j in range(n):
        flat_ref[j, rank:rank + 1, :unit] = g_gain_ref[:, j * unit:(j + 1) * unit]
    for copy in copies:
        copy.wait()


def relay_scratch(count, D, subs):
    half, size = count // 2, count // 2 // subs
    return [
        pltpu.VMEM((2, 2, half, D), BF16),
        pltpu.VMEM((2, half, D), BF16),
        pltpu.VMEM((2, half, D), BF16),
        pltpu.VMEM((size, D), F32),
        pltpu.SemaphoreType.DMA((12, subs)),
        pltpu.SemaphoreType.DMA((12, subs)),
    ]


SUBS = 4


def relay_forward(p, x, gain, unit, ident):
    _, count, D = p.shape
    fast = pl.BlockSpec(memory_space=pltpu.VMEM)
    return pl.pallas_call(
        functools.partial(forward_relay_kernel, unit, SUBS),
        out_shape=(jax.ShapeDtypeStruct(p.shape, BF16), jax.ShapeDtypeStruct(x.shape, F32)),
        in_specs=[fast] * 3,
        out_specs=(fast,) * 2,
        scratch_shapes=relay_scratch(count, D, SUBS),
        compiler_params=pltpu.CompilerParams(collective_id=ident, has_side_effects=True, vmem_limit_bytes=40 << 20),
        name="relay_forward",
    )(p, x, gain)


def relay_backward(p, resid, cot, gain, hidden, branch, down, unit, zs, cs, ident):
    _, count, D = p.shape
    tokens = hidden[0].shape[0]
    units = down.shape[0]
    width = D // SUBS
    each = units // (zs * cs)
    fast = pl.BlockSpec(memory_space=pltpu.VMEM)
    anywhere = pl.BlockSpec(memory_space=pl.ANY)
    return pl.pallas_call(
        functools.partial(backward_relay_kernel, unit, SUBS, len(hidden)),
        out_shape=(
            jax.ShapeDtypeStruct(p.shape, BF16),
            jax.ShapeDtypeStruct(resid.shape, F32),
            jax.ShapeDtypeStruct((1, D), F32),
            jax.ShapeDtypeStruct((zs, each, D), BF16),
        ) + tuple(jax.ShapeDtypeStruct((rows, D), BF16) for rows in (tokens // 2, tokens // 4, tokens // 4)),
        in_specs=[fast] * 4 + [anywhere] * (len(hidden) + 2),
        out_specs=(fast,) * 3 + (anywhere,) * 4,
        scratch_shapes=relay_scratch(count, D, SUBS) + [
            pltpu.VMEM((tokens, units), BF16),
            pltpu.VMEM(branch.shape, BF16),
            pltpu.VMEM(down.shape, BF16),
            pltpu.VMEM((SUBS, zs, cs, each, width), BF16),
            pltpu.VMEM((SUBS, zs, each, width), BF16),
            pltpu.VMEM((SUBS, tokens, width), BF16),
            pltpu.SemaphoreType.DMA((len(hidden) + 2,)),
            pltpu.SemaphoreType.DMA((8, SUBS)),
            pltpu.SemaphoreType.DMA((SUBS,)),
            pltpu.SemaphoreType.DMA((SUBS,)),
        ],
        compiler_params=pltpu.CompilerParams(collective_id=ident, has_side_effects=True, vmem_limit_bytes=60 << 20),
        name="relay_backward",
    )(p, resid, cot, gain, *hidden, branch, down)


def settle(p, x, d_resid, gain, d_low, f_low, d_f, g_head, g_mlp, act, d_attn, h, unit, zs, cs, ident):
    _, count, D = p.shape
    fast = pl.BlockSpec(memory_space=pltpu.VMEM)
    anywhere = pl.BlockSpec(memory_space=pl.ANY)
    deep = zs // TP
    rank = f_low.shape[1]
    return pl.pallas_call(
        functools.partial(settle_kernel, unit, SUBS),
        out_shape=(
            jax.ShapeDtypeStruct(p.shape[1:], BF16),
            jax.ShapeDtypeStruct((zs * TP * cs, rank + 8, LANES), F32),
            jax.ShapeDtypeStruct((TP, deep, unit, D), BF16),
        ),
        in_specs=[fast] * 9 + [anywhere] * 3,
        out_specs=(fast,) * 2 + (anywhere,),
        scratch_shapes=relay_scratch(count, D, SUBS) + [
            pltpu.VMEM(act.shape, BF16),
            pltpu.VMEM(d_attn.shape, BF16),
            pltpu.VMEM(h.shape, BF16),
            pltpu.VMEM((deep, TP, cs, unit, D), BF16),
            pltpu.VMEM((deep, TP, unit, D), BF16),
            pltpu.VMEM((1, D), F32),
            pltpu.SemaphoreType.DMA((3,)),
            pltpu.SemaphoreType.DMA,
            pltpu.SemaphoreType.DMA,
            pltpu.SemaphoreType.DMA,
            pltpu.SemaphoreType.DMA((TP - 1,)),
            pltpu.SemaphoreType.DMA((TP - 1,)),
        ],
        compiler_params=pltpu.CompilerParams(collective_id=ident, has_side_effects=True, vmem_limit_bytes=56 << 20),
        name="settle",
    )(p, x, d_resid, gain, d_low, f_low, d_f, g_head, g_mlp, act, d_attn, h)


def ff_kernel(tile, hm_ref, gu_ref, d_hidden_ref, hidden_ref, d_gu_ref):
    for at in range(0, hm_ref.shape[0], tile):
        rows = slice(at, at + tile)
        pre = mm(hm_ref[rows, :], gu_ref[...], NN)
        gate, up = pre[:, :LANES], pre[:, LANES:]
        sig = 0.5 * jnp.tanh(0.5 * gate) + 0.5
        act = gate * sig
        d_hidden = d_hidden_ref[rows, :]
        hidden_ref[rows, :] = (act * up).astype(BF16)
        d_gu_ref[rows, :LANES] = (d_hidden * up * (sig + act * (1.0 - sig))).astype(BF16)
        d_gu_ref[rows, LANES:] = (d_hidden * act).astype(BF16)


def ff_forward(hm, gu, d_hidden, first):
    tokens, D = hm.shape
    columns = gu.shape[1]
    wide = pl.BlockSpec((tokens, 2 * LANES), lambda j: (0, j))
    return pl.pallas_call(
        functools.partial(ff_kernel, 256),
        out_shape=(jax.ShapeDtypeStruct((tokens, columns // 2), BF16), jax.ShapeDtypeStruct((tokens, columns), BF16)),
        grid=(columns // (2 * LANES),),
        in_specs=[
            pl.BlockSpec((tokens, D), lambda j: (0, 0)),
            pl.BlockSpec((D, 2 * LANES), lambda j: (0, j)),
            pl.BlockSpec((tokens, LANES), lambda j: (0, j + first)),
        ],
        out_specs=(pl.BlockSpec((tokens, LANES), lambda j: (0, j)), wide),
        compiler_params=pltpu.CompilerParams(vmem_limit_bytes=48 << 20),
        name="feed_forward",
    )(hm, gu, d_hidden)


def d_hm_kernel(tile, count, *refs):
    grads, weights, o_ref = refs[:count], refs[count:2 * count], refs[2 * count]
    for at in range(0, o_ref.shape[0], tile):
        rows = slice(at, at + tile)
        o_ref[rows, :] = sum(mm(g[rows, :], w[...], NT) for g, w in zip(grads, weights)).astype(BF16)


def d_hm_product(grads, weights):
    tokens, D = grads[0].shape[0], weights[0].shape[0]
    width = 256
    return pl.pallas_call(
        functools.partial(d_hm_kernel, 256, len(grads)),
        out_shape=jax.ShapeDtypeStruct((tokens, D), BF16),
        grid=(D // width,),
        in_specs=[pl.BlockSpec(g.shape, lambda j: (0, 0)) for g in grads]
        + [pl.BlockSpec((width, w.shape[1]), lambda j: (j, 0)) for w in weights],
        out_specs=pl.BlockSpec((tokens, width), lambda j: (0, j)),
        compiler_params=pltpu.CompilerParams(vmem_limit_bytes=48 << 20),
        name="d_hm",
    )(*grads, *weights)


def heads_kernel(steps, count, own_hbm, other_hbm, d_pre_hbm, *refs):
    blocks, (o_hbm, *refs) = refs[:count], refs[count:]
    returned, refs = refs[:count], refs[count:]
    (own, other, d_pre, sent, got, own_sem, back_send, back_recv, in_sem, out_sem, core_send, core_recv) = refs
    z, t, c = (lax.axis_index(a) for a in ALL)
    width = d_pre.shape[2]
    cols = [slice(i * width, (i + 1) * width) for i in range(steps)]
    loads = [pltpu.make_async_copy(other_hbm, other, in_sem.at[0])]
    loads += [pltpu.make_async_copy(d_pre_hbm.at[:, cols[i]], d_pre.at[i], in_sem.at[2 + i]) for i in range(steps)]
    loads += [pltpu.make_async_copy(own_hbm, own, in_sem.at[1])]
    for copy in loads:
        copy.start()
    barrier = pltpu.get_barrier_semaphore()
    for device in [(z, chip_peer(t, step), c) for step in (1, 2, 3)] + [(z, t, 1 - c)]:
        pl.semaphore_signal(barrier, inc=1, device_id=device, device_id_type=pl.DeviceIdType.MESH)
    pl.semaphore_wait(barrier, TP)
    copies = send_blocks(blocks, returned, own_sem, back_send, back_recv)
    crossings = []
    loads[0].wait()
    for i in range(steps):
        loads[1 + i].wait()
        sent[i] = mm(other[...], d_pre[i], TN).astype(BF16)
        crossings.append(pltpu.make_async_remote_copy(
            src_ref=sent.at[i], dst_ref=got.at[i], send_sem=core_send.at[i], recv_sem=core_recv.at[i],
            device_id=(z, t, 1 - c), device_id_type=pl.DeviceIdType.MESH))
        crossings[i].start()
    loads[-1].wait()
    for i in range(steps):
        g = mm(own[...], d_pre[i], TN)
        crossings[i].wait_recv()
        got[i] = (g + got[i].astype(F32)).astype(BF16)
        copies.append(pltpu.make_async_copy(got.at[i], o_hbm.at[:, cols[i]], out_sem.at[i]))
        copies[-1].start()
    for copy in crossings:
        copy.wait_send()
    for copy in copies:
        copy.wait()


def heads_gradient(own, other, d_pre, blocks, ident):
    tokens, half = own.shape
    columns = d_pre.shape[1]
    steps = 4
    width = columns // steps
    count = len(blocks)
    anywhere = pl.BlockSpec(memory_space=pl.ANY)
    return pl.pallas_call(
        functools.partial(heads_kernel, steps, count),
        out_shape=(jax.ShapeDtypeStruct((half, columns), BF16),)
        + tuple(jax.ShapeDtypeStruct(b.shape, b.dtype) for b in blocks),
        in_specs=[anywhere] * (3 + count),
        out_specs=(anywhere,) * (1 + count),
        scratch_shapes=[
            pltpu.VMEM((tokens, half), BF16),
            pltpu.VMEM((tokens, half), BF16),
            pltpu.VMEM((steps, tokens, width), BF16),
            pltpu.VMEM((steps, half, width), BF16),
            pltpu.VMEM((steps, half, width), BF16),
        ] + block_sems(count) + [
            pltpu.SemaphoreType.DMA((2 + steps,)),
            pltpu.SemaphoreType.DMA((steps,)),
            pltpu.SemaphoreType.DMA((steps,)),
            pltpu.SemaphoreType.DMA((steps,)),
        ],
        compiler_params=pltpu.CompilerParams(collective_id=ident, has_side_effects=True, vmem_limit_bytes=56 << 20),
        name="heads_gradient",
    )(own, other, d_pre, *blocks)


def send_t(x, step):
    return lax.ppermute(x, "t", [(i, i ^ step) for i in range(TP)])


def send_c(x):
    return lax.ppermute(x, "c", [(0, 1), (1, 0)])


def gather_t_begin(x):
    return send_t(x, 1), send_t(x, 2)


def gather_t_end(x, one, two):
    half = x.shape[0] // 2
    return jnp.concatenate([x, one, two, send_t(two[:half], 1), send_t(one[half:], 2)], axis=0)


def scatter_t_middle(kept, got):
    half = kept.shape[0] // 4
    first, second = got

    def add(low, v):
        return kept[low:low + half].astype(F32) + v.astype(F32)

    part = jnp.concatenate([add(0, first[:half]), add(half, second[:half])], axis=0)
    return part, (add(2 * half, first[half:]).astype(BF16), add(3 * half, second[half:]).astype(BF16))


def scatter_t_pass(passed):
    return send_t(passed[0], 2), send_t(passed[1], 1)


def swap_t(x):
    t = lax.axis_index("t")

    def block(a, j):
        return lax.dynamic_index_in_dim(a, j, 0, keepdims=False)

    got = jnp.stack([block(x, t)] + [send_t(block(x, t ^ k), k) for k in (1, 2, 3)])
    return jnp.stack([block(got, t ^ j) for j in range(TP)])


def dot(left, right):
    return mm(left, right, NN)


def dot_nt(left, right):
    return mm(left, right, NT)


def dot_tn(left, right):
    return mm(left, right, TN)


def after(x, *others):
    return lax.optimization_barrier((x,) + others)[:2]


def rms_norm(v, gain):
    return v * lax.rsqrt(jnp.mean(v * v, axis=-1, keepdims=True) + 1e-06) * gain


def swiglu(gate_val, up_val):
    return jax.nn.silu(gate_val) * up_val


def per_device(zs, cs, tokens, starts, w_query, w_key, w_value, w_gate_out, w_out, w_forget_down,
               w_forget_up, norm_attn, norm_head, norm_mlp, w_gate, w_up, w_down, cotangent):
    seqs, seq_len, D = tokens.shape
    n = zs * TP * cs
    rows = w_query.shape[0]
    ff_rows = w_down.shape[0]
    rank = w_forget_down.shape[1]
    fu_cols = w_forget_up.shape[1]
    mine = seqs * seq_len
    half = D // cs
    t_idx, c_idx = lax.axis_index("t"), lax.axis_index("c")

    def to_k(v):
        return v.reshape(-1, zs, TP, cs, rows).transpose(0, 3, 1, 2, 4).reshape(-1, D)

    def from_k(v):
        return v.reshape(-1, cs, zs, TP, rows).transpose(0, 2, 3, 1, 4).reshape(-1, D)

    def sum_z(v):
        return lax.psum_scatter(v, "z", scatter_dimension=0, tiled=True)

    def core_half(v, core):
        return lax.dynamic_slice_in_dim(v, core * half, half, axis=1)

    def other_term(left, right):
        return dot_tn(left, right).astype(BF16)

    def own_term(left, right, other):
        return (dot_tn(left, right) + send_c(other).astype(F32)).astype(BF16)

    docs = jnp.cumsum(starts, axis=1).astype(BF16)
    small = pack_rows([w_forget_down.reshape(-1), w_forget_up.reshape(-1), norm_attn, norm_head, norm_mlp,
                       docs.reshape(-1)], 16)
    sizes = [rows * rank, rank * fu_cols, norm_attn.shape[0], norm_head.shape[0], norm_mlp.shape[0]]
    by_rows = lax.all_gather(jnp.concatenate([w_out, w_down], axis=0), ("z", "c"), axis=0, tiled=True)
    by_rows = by_rows.reshape(zs, cs, rows + ff_rows, D)
    cot = cotangent.reshape(mine, D)
    w4 = spread([w_query, w_key, w_value, w_gate_out], 0)
    small, w4 = after(small, w4)
    small = share(small, n, cs, 9)
    piece = cs * ff_rows
    units = zs * piece
    middle = (units // LANES + 1) // 2 * 2 * LANES
    parts = ((0, middle), (middle, 2 * units))
    w_gate, small = after(w_gate, small)
    gus = spread_ff(w_gate, w_up, piece, parts, 2)
    pieces = cut(small.reshape(n, -1), sizes + [mine])
    wfd = to_k(pieces[0].reshape(D, rank).T).T
    wfu = pieces[1].reshape(n, rank, fu_cols).transpose(1, 0, 2).reshape(rank, n * fu_cols)
    wfu = lax.dynamic_slice_in_dim(wfu, t_idx * SLOTS, SLOTS, axis=1)
    gain_attn = pieces[2].reshape(-1).astype(F32)
    gain_head = pieces[3].reshape(1, -1).astype(F32)
    gain_mlp = pieces[4].reshape(1, -1).astype(F32)
    all_docs = pieces[5].reshape(zs, TP, cs, mine)
    all_docs = lax.dynamic_index_in_dim(all_docs, lax.axis_index("z"), 0, keepdims=False)
    all_docs = lax.dynamic_index_in_dim(all_docs, lax.axis_index("c"), 1, keepdims=False)
    docs = jnp.concatenate([lax.dynamic_index_in_dim(all_docs, t_idx ^ k, 0) for k in range(TP)], axis=0)
    docs = docs.astype(F32).reshape(TP * seqs, seq_len)

    def by_columns(w):
        return lax.all_gather(w.reshape(TP * rows, -1), ("c", "z"), axis=0, tiled=True)

    w4 = by_columns(w4)
    gus = [by_columns(gu) for gu in gus]
    down = by_rows[:, :, rows:].reshape(-1, D)
    wo = swap_t(by_rows[:, :, :rows].reshape(TP, -1, rows, D)).reshape(TP, zs // TP, cs, rows, D)
    wo = wo.transpose(1, 0, 2, 3, 4).reshape(HEAD, D)

    x = tokens.reshape(mine, D).astype(F32)
    normed_in, norm_in_back = jax.vjp(rms_norm, x, gain_attn)
    h = to_k(normed_in.astype(BF16))
    h = gather_t_end(h, *gather_t_begin(h))
    d_branch = gather_t_end(cot, *gather_t_begin(cot))
    d_hidden = dot_nt(d_branch, down)
    h, d_hidden = after(h, d_hidden)
    h, wo = after(h, wo)
    h_own, h_other = after(core_half(h, c_idx), core_half(h, 1 - c_idx))
    h, h_own = after(h, h_own)
    pre = dot(h, w4)
    f_low = dot(h, wfd).astype(BF16)
    act = slots_forward(pre, f_low, wfu, gain_head, docs)
    terms = dot(act, wo).astype(BF16)
    tokens_flat = tokens.reshape(mine, D)
    hm, resid = relay_forward(terms.reshape(TP, mine, D), tokens_flat, gain_mlp, rows, 6)
    hm = hm.reshape(TP * mine, D)

    hidden, d_gus, g_gus = [], [], []
    for gu, (low, high) in zip(gus, parts):
        part, d_gu = ff_forward(hm, gu, d_hidden, low // (2 * LANES))
        hidden.append(part)
        d_gus.append(d_gu)
        g_gu = other_term(core_half(hm, 1 - c_idx), d_gu)
        if high == 2 * units:
            d_gus[-1], _ = after(d_gu, g_gu)
            d_hm = d_hm_product(d_gus, gus)
            hm, _ = after(hm, d_hm)
        g_gu = own_term(core_half(hm, c_idx), d_gu, g_gu)
        hm, g_gu = after(hm, g_gu)
        g_gus.append(sum_z(g_gu).reshape(TP, rows, -1))
    d_hm, _ = after(d_hm, g_gu)
    d_attn, d_resid, g_norm_mlp, g_down, *branch = relay_backward(
        d_hm.reshape(TP, mine, D), resid, cot, gain_mlp, hidden, d_branch, down, rows, zs, cs, 7)
    d_attn = d_attn.reshape(TP * mine, D)
    g_down = sum_z(g_down.reshape(-1, D))

    d_attn, g_gus[0] = after(d_attn, g_gus[0])
    d_attn, g_gus[1] = after(d_attn, g_gus[1])
    first = send_t(branch[1], 1), send_t(branch[2], 2)
    d_act = dot_nt(d_attn, wo)
    count = TP * seqs
    ahead = count * 5 // 8
    *begun, g_norm_head = slots_backward(pre, f_low, wfu, gain_head, docs, d_act, 0, ahead)
    first, begun = after(first, begun)
    part, passed = scatter_t_middle(branch[0], first)
    d_act, passed = after(d_act, passed)
    second = scatter_t_pass(passed)
    d_pre, d_f, d_low, g_more = slots_backward(
        pre, f_low, wfu, gain_head, docs, d_act, ahead, count - ahead, begun)
    g_norm_head = g_norm_head + g_more
    d_pre, second = after(d_pre, second)
    g4, *g_gus = heads_gradient(h_own, h_other, d_pre, g_gus, 3)
    d_pre, _ = after(d_pre, g4)
    d_pre, g_down = after(d_pre, g_down)
    g4 = sum_z(g4)
    d_h = (dot_nt(d_pre, w4) + dot_nt(d_low, wfd)).astype(BF16)
    tokens_grad, flat, g_out = settle(
        d_h.reshape(TP, mine, D), tokens_flat, d_resid, gain_attn.reshape(1, D), d_low, f_low, d_f, g_norm_head,
        g_norm_mlp, act, d_attn, h, rows, zs, cs, 8)
    g_out = sum_z(g_out.reshape(-1, D))

    second, tokens_grad = after(second, tokens_grad)
    mixed = (resid + part + jnp.concatenate(second, axis=0).astype(F32)).astype(BF16)
    g_gate, g_up = widen(g_gus, ff_moves(piece, units, parts), 2, n * ff_rows)
    g_down = g_down.astype(F32)
    g4, mixed, tokens_grad, g_gate, g_up, g_down = lax.optimization_barrier(
        (g4, mixed, tokens_grad, g_gate, g_up, g_down))
    small, g4 = finish(flat, g4.reshape(TP, rows, -1), n, cs)
    heads = norm_head.shape[0]
    head_moves = [(i, j * HEAD, 0, j, i * HEAD, HEAD) for i in range(4) for j in range(TP)]
    g_heads, g_out = after(widen([g4], head_moves, 4, D), g_out)
    g_query, g_key, g_value, g_gate_out = g_heads
    g_out = g_out.astype(F32)
    return (
        mixed.reshape(tokens.shape),
        tokens_grad.reshape(tokens.shape),
        g_query, g_key, g_value, g_gate_out,
        g_out,
        small[:rank, :rows].T,
        small[:rank, rows:rows + fu_cols],
        small[rank, :rows],
        small[rank, rows:rows + heads],
        small[rank + 1, :rows],
        g_gate, g_up,
        g_down,
    )


def solution(mesh):
    cs = mesh.shape["outer"]
    zs = mesh.shape["dp"] // TP
    grid = Mesh(mesh.devices.reshape(zs, TP, cs), ALL)
    whole, row, vec = P(ALL, None, None), P(ALL, None), P(ALL)
    cols = P(None, ALL)

    def body(*args):
        return per_device(zs, cs, *args)

    return jax.shard_map(
        body,
        mesh=grid,
        in_specs=(whole, row, row, row, row, row, row, row, cols, vec, vec, vec, row, row, row, whole),
        out_specs=(whole, whole, row, row, row, row, row, row, cols, vec, vec, vec, row, row, row),
        check_vma=False,
    )
```

```python
import functools

import jax
import jax.numpy as jnp
from jax import lax
from jax.experimental import pallas as pl
from jax.experimental.pallas import tpu as pltpu
from jax.sharding import Mesh, PartitionSpec as P

HEADS = 4
HEAD = 512
SLOTS = 64
TP = 4
ALL = ("z", "t", "c")
F32 = jnp.float32
BF16 = jnp.bfloat16
SPAN = 80.0


def mm(a, b, dims):
    return lax.dot_general(a, b, (dims, ((), ())), preferred_element_type=F32)


NN, NT, TN = ((1,), (0,)), ((1,), (1,)), ((0,), (0,))


def split(a):
    high = a.astype(BF16)
    return high, (a - high.astype(F32)).astype(BF16)


def mm3(a, b, dims):
    ah, al = split(a)
    bh, bl = split(b)
    return mm(ah, bh, dims) + (mm(ah, bl, dims) + mm(al, bh, dims))


def mm_exact(mask, b, dims):
    b1, rest = split(b)
    b2 = rest
    b3 = (b - b1.astype(F32) - b2.astype(F32)).astype(BF16)
    return mm(mask, b1, dims) + (mm(mask, b2, dims) + mm(mask, b3, dims))


def swish_parts(v):
    sig = 1.0 / (1.0 + jnp.exp(-v))
    return v * sig, sig * (1.0 + v * (1.0 - sig))


def gates(f_low, wfu):
    f_pre = mm(f_low, wfu, NN)
    soft = jnp.log(1.0 + jnp.exp(-jnp.abs(f_pre)))
    log_f = (jnp.minimum(f_pre, 0.0) - soft) * 0.125
    return f_pre, log_f


def lower_tri(n, kind=BF16):
    rows = lax.broadcasted_iota(jnp.int32, (n, n), 0)
    cols = lax.broadcasted_iota(jnp.int32, (n, n), 1)
    return rows >= cols


def column(a, j):
    picked = lax.broadcasted_iota(jnp.int32, a.shape, 1) == j
    return jnp.sum(jnp.where(picked, a, 0.0), axis=1, keepdims=True)


def row(a, j):
    picked = lax.broadcasted_iota(jnp.int32, a.shape, 0) == j
    return jnp.sum(jnp.where(picked, a, 0.0), axis=0, keepdims=True)


def gap(total, j):
    return jnp.exp(jnp.minimum(total - row(total, j), 0.0))


def softmax(scores):
    e = jnp.exp(scores - jnp.max(scores, axis=1, keepdims=True))
    return e / jnp.sum(e, axis=1, keepdims=True)


def far_near(total):
    mid = 0.5 * total[-1:]
    return jnp.exp(total - mid), jnp.exp(mid - total)


def sum_over_j(mats, total, unit, fast, dest):
    n = total.shape[0]

    @pl.when(fast)
    def _():
        near, far = far_near(total)
        got = mm3(jnp.concatenate(mats, axis=0), far * unit, NN)
        for i, d in enumerate(dest):
            d[...] = got[i * n:(i + 1) * n] * near

    @pl.when(jnp.logical_not(fast))
    def _():
        for d in dest:
            d[...] = jnp.zeros_like(total)

        def step(j, _):
            e = gap(total, j) * row(unit, j)
            for d, m in zip(dest, mats):
                d[...] += column(m, j) * e
            return 0

        lax.fori_loop(0, n, step, 0)


def sum_over_m(probs, total, unit, fast, dest):
    n = total.shape[0]

    @pl.when(fast)
    def _():
        near, far = far_near(total)
        got = mm3(jnp.concatenate([p * near for p in probs], axis=0), far * unit, NT)
        for i, d in enumerate(dest):
            d[...] = got[i * n:(i + 1) * n]

    @pl.when(jnp.logical_not(fast))
    def _():
        cols = lax.broadcasted_iota(jnp.int32, (n, n), 1)

        def step(j, _):
            e = gap(total, j) * row(unit, j)
            for d, p in zip(dest, probs):
                d[...] = jnp.where(cols == j, jnp.sum(p * e, axis=1, keepdims=True), d[...])
            return 0

        lax.fori_loop(0, n, step, 0)


def sum_over_t(mats, probs, total, fast, dest):
    n = total.shape[0]

    @pl.when(fast)
    def _():
        near, far = far_near(total)
        got = mm3(jnp.concatenate(mats, axis=0), jnp.concatenate([p * near for p in probs], axis=0), TN)
        dest[...] = got * far

    @pl.when(jnp.logical_not(fast))
    def _():
        rows = lax.broadcasted_iota(jnp.int32, total.shape, 0)

        def step(j, _):
            e = gap(total, j)
            s = sum(column(m, j) * p for m, p in zip(mats, probs))
            dest[...] = jnp.where(rows == j, jnp.sum(s * e, axis=0, keepdims=True), dest[...])
            return 0

        lax.fori_loop(0, n, step, 0)


def mixer_forward(pre_ref, f_low_ref, wfu_ref, doc_col_ref, doc_row_ref, score_ref, mix_ref):
    pre = pre_ref[...]
    q, q_slope = swish_parts(pre[:, :HEAD])
    k, k_slope = swish_parts(pre[:, HEAD:2 * HEAD])
    q, k, v = q.astype(BF16), k.astype(BF16), pre[:, 2 * HEAD:3 * HEAD].astype(BF16)
    n = q.shape[0]
    tri = lower_tri(n)
    keep = tri & (doc_col_ref[0] == doc_row_ref[0])
    inner = jnp.where(keep, mm(q, k, NT) * HEAD ** -0.5, 0.0)
    f_pre, log_f = gates(f_low_ref[...], wfu_ref[...])
    total = mm_exact(tri.astype(BF16), log_f, NN)
    unit = 1.0 - jnp.exp(log_f)
    fast = jnp.min(total[-1:]) > -SPAN
    return q, k, v, q_slope, k_slope, keep, inner, f_pre, log_f, total, unit, fast


def forward_kernel(pre_ref, f_low_ref, wfu_ref, gain_ref, doc_col_ref, doc_row_ref, act_ref, score_ref, mix_ref):
    q, k, v, _, _, keep, inner, _, _, total, unit, fast = mixer_forward(
        pre_ref, f_low_ref, wfu_ref, doc_col_ref, doc_row_ref, score_ref, mix_ref)
    sum_over_j([inner], total, unit, fast, [score_ref])
    probs = softmax(score_ref[...])
    sum_over_m([probs], total, unit, fast, [mix_ref])
    mixing = jnp.where(keep, mix_ref[...], 0.0).astype(BF16)
    out = mm(mixing, v, NN)
    scale = lax.rsqrt(jnp.mean(out * out, axis=1, keepdims=True) + 1e-06)
    gate, _ = swish_parts(pre_ref[:, 3 * HEAD:])
    act_ref[...] = (out * scale * gain_ref[...] * gate).astype(BF16)


def backward_kernel(pre_ref, f_low_ref, wfu_ref, gain_ref, doc_col_ref, doc_row_ref, d_act_ref, *refs):
    d_pre_ref, d_f_ref, d_low_ref, g_gain_ref, score_ref, d_p_ref, mix_ref, d_inner_ref, k_ref = refs[-9:]
    q, k, v, q_slope, k_slope, keep, inner, f_pre, log_f, total, unit, fast = mixer_forward(
        pre_ref, f_low_ref, wfu_ref, doc_col_ref, doc_row_ref, score_ref, mix_ref)
    sum_over_j([inner], total, unit, fast, [score_ref])
    scores = score_ref[...]
    probs = softmax(scores)
    sum_over_m([probs], total, unit, fast, [mix_ref])
    mixing = jnp.where(keep, mix_ref[...], 0.0).astype(BF16)
    out = mm(mixing, v, NN)

    scale = lax.rsqrt(jnp.mean(out * out, axis=1, keepdims=True) + 1e-06)
    gain = gain_ref[...]
    gate, gate_slope = swish_parts(pre_ref[:, 3 * HEAD:])
    d_act = d_act_ref[...].astype(F32)
    d_gate = d_act * out * scale * gain * gate_slope
    d_norm = d_act * gate
    g_gain = jnp.sum(d_norm * out * scale, axis=0, keepdims=True)

    @pl.when(pl.program_id(0) == 0)
    def _():
        g_gain_ref[...] = jnp.zeros_like(g_gain_ref)

    g_gain_ref[...] += g_gain
    d_norm = d_norm * gain
    d_out = scale * (d_norm - out * (scale * scale) * jnp.mean(d_norm * out, axis=1, keepdims=True))
    d_out = d_out.astype(BF16)

    d_mix = jnp.where(keep, mm(d_out, v, NT), 0.0)
    d_v = mm(mixing, d_out, TN)
    sum_over_j([d_mix], total, unit, fast, [d_p_ref])
    d_p = d_p_ref[...]
    d_score = probs * (d_p - jnp.sum(probs * d_p, axis=1, keepdims=True))
    sum_over_m([d_score], total, unit, fast, [d_inner_ref])
    d_inner = jnp.where(keep, d_inner_ref[...], 0.0).astype(BF16)
    sum_over_t([d_mix, inner], [probs, d_score], total, fast, k_ref)
    k_sum = k_ref[...]
    d_total = probs * d_p + d_score * scores - unit * k_sum
    n = q.shape[0]
    tri = lower_tri(n).astype(BF16)
    d_log = mm_exact(tri, d_total, TN) - jnp.exp(log_f) * k_sum
    d_f = (d_log * (0.125 / (1.0 + jnp.exp(f_pre)))).astype(BF16)
    d_f_ref[...] = d_f
    d_low_ref[...] = mm(d_f, wfu_ref[...], NT).astype(BF16)
    d_q = mm(d_inner, k, NN) * HEAD ** -0.5
    d_k = mm(d_inner, q, TN) * HEAD ** -0.5
    d_pre_ref[:, :HEAD] = (d_q * q_slope).astype(BF16)
    d_pre_ref[:, HEAD:2 * HEAD] = (d_k * k_slope).astype(BF16)
    d_pre_ref[:, 2 * HEAD:3 * HEAD] = d_v.astype(BF16)
    d_pre_ref[:, 3 * HEAD:] = d_gate.astype(BF16)


def mixer_specs(length, rank, first=0):
    return [
        pl.BlockSpec((length, 4 * HEAD), lambda i: (i + first, 0)),
        pl.BlockSpec((length, rank), lambda i: (i + first, 0)),
        pl.BlockSpec((rank, SLOTS), lambda i: (0, 0)),
        pl.BlockSpec((1, HEAD), lambda i: (0, 0)),
        pl.BlockSpec((1, length, 1), lambda i: (i + first, 0, 0)),
        pl.BlockSpec((1, 1, length), lambda i: (i + first, 0, 0)),
    ]


def slots_forward(pre, f_low, wfu, gain, docs):
    count, length = docs.shape
    tm = pltpu.VMEM((length, SLOTS), F32)
    tj = pltpu.VMEM((length, length), F32)
    return pl.pallas_call(
        forward_kernel,
        out_shape=jax.ShapeDtypeStruct((count * length, HEAD), BF16),
        grid=(count,),
        in_specs=mixer_specs(length, f_low.shape[1]),
        out_specs=pl.BlockSpec((length, HEAD), lambda i: (i, 0)),
        scratch_shapes=[tm, tj],
        compiler_params=pltpu.CompilerParams(vmem_limit_bytes=32 << 20),
        name="slots_forward",
    )(pre, f_low, wfu, gain, docs[:, :, None], docs[:, None, :])


def slots_backward(pre, f_low, wfu, gain, docs, d_act, first, steps, begun=()):
    count, length = docs.shape
    rank = f_low.shape[1]
    tm = pltpu.VMEM((length, SLOTS), F32)
    tj = pltpu.VMEM((length, length), F32)
    block = lambda width: pl.BlockSpec((length, width), lambda i: (i + first, 0))
    return pl.pallas_call(
        backward_kernel,
        out_shape=(
            jax.ShapeDtypeStruct((count * length, 4 * HEAD), BF16),
            jax.ShapeDtypeStruct((count * length, SLOTS), BF16),
            jax.ShapeDtypeStruct((count * length, rank), BF16),
            jax.ShapeDtypeStruct((1, HEAD), F32),
        ),
        grid=(steps,),
        in_specs=mixer_specs(length, rank, first) + [block(HEAD)] + [pl.BlockSpec(memory_space=pl.ANY)] * len(begun),
        out_specs=(block(4 * HEAD), block(SLOTS), block(rank), pl.BlockSpec((1, HEAD), lambda i: (0, 0))),
        scratch_shapes=[tm, tm, tj, tj, tm],
        input_output_aliases={7 + i: i for i in range(len(begun))},
        compiler_params=pltpu.CompilerParams(vmem_limit_bytes=32 << 20),
        name="slots_backward",
    )(pre, f_low, wfu, gain, docs[:, :, None], docs[:, None, :], d_act, *begun)


def place(index, cs):
    return (index // (TP * cs), (index // cs) % TP, index % cs)


def greet_all(n, cs, me):
    barrier = pltpu.get_barrier_semaphore()

    def greet(step, _):
        pl.semaphore_signal(barrier, inc=1, device_id=place((me + step) % n, cs), device_id_type=pl.DeviceIdType.MESH)
        return 0

    lax.fori_loop(1, n, greet, 0)
    pl.semaphore_wait(barrier, n - 1)


def my_index(cs):
    return (lax.axis_index("z") * TP + lax.axis_index("t")) * cs + lax.axis_index("c")


def chip_peer(t, step):
    high, low = t // 2, t % 2
    return (high + step // 2) % 2 * 2 + (low + step % 2) % 2


def share_kernel(n, cs, x_ref, o_ref, send_sem, recv_sem):
    me = my_index(cs)
    greet_all(n, cs, me)

    def send(step, _):
        pltpu.make_async_remote_copy(
            src_ref=x_ref, dst_ref=o_ref.at[me], send_sem=send_sem, recv_sem=recv_sem,
            device_id=place((me + step) % n, cs), device_id_type=pl.DeviceIdType.MESH).start()
        return 0

    lax.fori_loop(1, n, send, 0)
    o_ref[me] = x_ref[...]
    others = o_ref.at[pl.ds(0, n - 1)]
    pltpu.make_async_copy(others, others, recv_sem).wait()
    pltpu.make_async_copy(others, others, send_sem).wait()


def share(x, n, cs, ident):
    return pl.pallas_call(
        functools.partial(share_kernel, n, cs),
        out_shape=jax.ShapeDtypeStruct((n,) + x.shape, x.dtype),
        in_specs=[pl.BlockSpec(memory_space=pltpu.VMEM)],
        out_specs=pl.BlockSpec(memory_space=pltpu.VMEM),
        scratch_shapes=[pltpu.SemaphoreType.DMA, pltpu.SemaphoreType.DMA],
        compiler_params=pltpu.CompilerParams(collective_id=ident, has_side_effects=True, vmem_limit_bytes=32 << 20),
        name="share_small",
    )(x)


def spread_kernel(count, *refs):
    srcs, (out, own_sem, send_sem, recv_sem) = refs[:count], refs[count:]
    z, t, c = (lax.axis_index(a) for a in ALL)
    greet_plane(z, t, c)
    width = srcs[0].shape[1] // TP

    def block(i, to, at):
        src = srcs[i].at[:, pl.ds(pl.multiple_of(to * width, 128), width)]
        return src, out.at[at, :, pl.ds(i * width, width)]

    copies = []
    for step in (3, 1, 2):
        peer = chip_peer(t, step)
        for i in range(count):
            src, dst = block(i, peer, t)
            copies.append(pltpu.make_async_remote_copy(
                src_ref=src, dst_ref=dst, send_sem=send_sem.at[step - 1, i], recv_sem=recv_sem.at[step - 1, i],
                device_id=(z, peer, c), device_id_type=pl.DeviceIdType.MESH))
            copies[-1].start()
    for i in range(count):
        src, dst = block(i, t, t)
        copies.append(pltpu.make_async_copy(src, dst, own_sem.at[i]))
        copies[-1].start()
    for copy in copies:
        copy.wait()


def spread(weights, ident):
    rows, columns = weights[0].shape
    anywhere = pl.BlockSpec(memory_space=pl.ANY)
    return pl.pallas_call(
        functools.partial(spread_kernel, len(weights)),
        out_shape=jax.ShapeDtypeStruct((TP, rows, len(weights) * columns // TP), weights[0].dtype),
        in_specs=[anywhere] * len(weights),
        out_specs=anywhere,
        scratch_shapes=block_sems(len(weights)),
        compiler_params=pltpu.CompilerParams(collective_id=ident, has_side_effects=True),
        name="spread",
    )(*weights)


def greet_plane(z, t, c):
    barrier = pltpu.get_barrier_semaphore()
    for step in (1, 2, 3):
        pl.semaphore_signal(barrier, inc=1, device_id=(z, chip_peer(t, step), c), device_id_type=pl.DeviceIdType.MESH)
    pl.semaphore_wait(barrier, TP - 1)


LANES = 128


def unit_runs(piece, units):
    cuts = sorted(set(range(0, units, piece)) | set(range(0, units, LANES)) | {units})
    return [(low, high - low) for low, high in zip(cuts, cuts[1:])]


def packed_at(unit, up):
    return unit // LANES * 2 * LANES + up * LANES + unit % LANES


def natural_at(unit, piece, chip):
    return (unit // piece * TP + chip) * piece + unit % piece


def spread_ff_kernel(piece, parts, wg_ref, wu_ref, *refs):
    outs, (packed, own_sem, send_sem, recv_sem) = refs[:len(parts)], refs[len(parts):]
    z, t, c = (lax.axis_index(a) for a in ALL)
    greet_plane(z, t, c)
    for j in range(TP):
        for up, w in enumerate((wg_ref, wu_ref)):
            for unit, count in unit_runs(piece, packed.shape[2] // 2):
                at, source = packed_at(unit, up), natural_at(unit, piece, j)
                packed[j, :, at:at + count] = w[:, source:source + count]
    copies = []
    for step in (3, 1, 2):
        peer = chip_peer(t, step)
        for i, ((low, high), out) in enumerate(zip(parts, outs)):
            copies.append(pltpu.make_async_remote_copy(
                src_ref=packed.at[peer, :, low:high], dst_ref=out.at[t], send_sem=send_sem.at[step - 1, i],
                recv_sem=recv_sem.at[step - 1, i], device_id=(z, peer, c), device_id_type=pl.DeviceIdType.MESH))
            copies[-1].start()
    for i, ((low, high), out) in enumerate(zip(parts, outs)):
        copies.append(pltpu.make_async_copy(packed.at[t, :, low:high], out.at[t], own_sem.at[i]))
        copies[-1].start()
    for copy in copies:
        copy.wait()


def spread_ff(w_gate, w_up, piece, parts, ident):
    rows, units = w_gate.shape
    fast = pl.BlockSpec(memory_space=pltpu.VMEM)
    anywhere = pl.BlockSpec(memory_space=pl.ANY)
    return pl.pallas_call(
        functools.partial(spread_ff_kernel, piece, parts),
        out_shape=tuple(jax.ShapeDtypeStruct((TP, rows, high - low), w_gate.dtype) for low, high in parts),
        in_specs=[fast, fast],
        out_specs=(anywhere,) * len(parts),
        scratch_shapes=[pltpu.VMEM((TP, rows, 2 * units // TP), w_gate.dtype)] + block_sems(len(parts)),
        compiler_params=pltpu.CompilerParams(collective_id=ident, has_side_effects=True, vmem_limit_bytes=32 << 20),
        name="spread_ff",
    )(w_gate, w_up)


def send_blocks(sources, targets, own_sem, send_sem, recv_sem):
    z, t, c = (lax.axis_index(a) for a in ALL)
    copies = []
    for step in (3, 1, 2):
        peer = chip_peer(t, step)
        for i, (source, target) in enumerate(zip(sources, targets)):
            copies.append(pltpu.make_async_remote_copy(
                src_ref=source.at[peer], dst_ref=target.at[t], send_sem=send_sem.at[step - 1, i],
                recv_sem=recv_sem.at[step - 1, i], device_id=(z, peer, c), device_id_type=pl.DeviceIdType.MESH))
            copies[-1].start()
    for i, (source, target) in enumerate(zip(sources, targets)):
        copies.append(pltpu.make_async_copy(source.at[t], target.at[t], own_sem.at[i]))
        copies[-1].start()
    return copies


def block_sems(count):
    return [pltpu.SemaphoreType.DMA((count,))] + [pltpu.SemaphoreType.DMA((TP - 1, count))] * 2


def ff_moves(piece, units, parts):
    moves = []
    for j in range(TP):
        for up in (0, 1):
            for unit, count in unit_runs(piece, units):
                at = packed_at(unit, up)
                source = [i for i, (low, high) in enumerate(parts) if low <= at < high][0]
                moves.append((up, natural_at(unit, piece, j), source, j, at - parts[source][0], count))
    return moves


def widen_kernel(moves, sources, *refs):
    for out, at, source, j, start, width in moves:
        refs[sources + out][:, at:at + width] = refs[source][j, :, start:start + width].astype(F32)


def widen(xs, moves, count, columns):
    fast = pl.BlockSpec(memory_space=pltpu.VMEM)
    return pl.pallas_call(
        functools.partial(widen_kernel, moves, len(xs)),
        out_shape=tuple(jax.ShapeDtypeStruct((xs[0].shape[1], columns), F32) for _ in range(count)),
        in_specs=[fast] * len(xs),
        out_specs=tuple(fast for _ in range(count)),
        compiler_params=pltpu.CompilerParams(vmem_limit_bytes=32 << 20),
        name="widen",
    )(*xs)


def finish_kernel(n, cs, x_ref, blocks_ref, o_ref, back_ref, got_ref, send_sem, recv_sem, *block_sem):
    me = my_index(cs)
    greet_all(n, cs, me)

    def send(step, _):
        peer = (me + step) % n
        pltpu.make_async_remote_copy(
            src_ref=x_ref.at[peer], dst_ref=got_ref.at[me], send_sem=send_sem, recv_sem=recv_sem,
            device_id=place(peer, cs), device_id_type=pl.DeviceIdType.MESH).start()
        return 0

    lax.fori_loop(1, n, send, 0)
    copies = send_blocks([blocks_ref], [back_ref], *block_sem)
    got_ref[me] = x_ref[me]
    others = got_ref.at[pl.ds(0, n - 1)]
    pltpu.make_async_copy(others, others, recv_sem).wait()
    pltpu.make_async_copy(others, others, send_sem).wait()
    o_ref[...] = jnp.sum(got_ref[...], axis=0)
    for copy in copies:
        copy.wait()


def finish(x, blocks, n, cs):
    anywhere = pl.BlockSpec(memory_space=pl.ANY)
    fast = pl.BlockSpec(memory_space=pltpu.VMEM)
    return pl.pallas_call(
        functools.partial(finish_kernel, n, cs),
        out_shape=(jax.ShapeDtypeStruct(x.shape[1:], x.dtype), jax.ShapeDtypeStruct(blocks.shape, blocks.dtype)),
        in_specs=[fast, anywhere],
        out_specs=(fast, anywhere),
        scratch_shapes=[pltpu.VMEM(x.shape, x.dtype), pltpu.SemaphoreType.DMA, pltpu.SemaphoreType.DMA] + block_sems(1),
        compiler_params=pltpu.CompilerParams(collective_id=1, has_side_effects=True, vmem_limit_bytes=32 << 20),
        name="finish",
    )(x, blocks)


def pack_rows(parts, unit):
    flat = jnp.concatenate(parts, axis=-1)
    size = flat.shape[-1]
    padded = -(-size // (unit * 128)) * unit * 128
    flat = jnp.pad(flat, [(0, 0)] * (flat.ndim - 1) + [(0, padded - size)])
    return flat.reshape(flat.shape[:-1] + (padded // 128, 128))


def cut(flat, sizes):
    at, pieces = 0, []
    for size in sizes:
        pieces.append(flat[..., at:at + size])
        at += size
    return pieces


def relay(p_ref, o_ref, got1, pass2, got2, sems, subs, middle, shared=True, beside=None, plane=False, cores=False,
          source=None, ready=None, landed=None):
    z, t, c = (lax.axis_index(a) for a in ALL)
    peers = {step: (z, chip_peer(t, step), c) for step in (1, 2)}
    barrier = pltpu.get_barrier_semaphore()
    met = [peers[1], peers[2]] + [(z, chip_peer(t, 3), c)] * plane + [(z, t, 1 - c)] * cores
    for device in met:
        pl.semaphore_signal(barrier, inc=1, device_id=device, device_id_type=pl.DeviceIdType.MESH)
    pl.semaphore_wait(barrier, len(met))
    send_sem, recv_sem = sems
    half = p_ref.shape[1] // 2
    size = half // subs
    ways = ((1, 2), (2, 1))
    copies = []

    def start(src, dst, step, slot, i):
        copy = pltpu.make_async_remote_copy(
            src_ref=src, dst_ref=dst, send_sem=send_sem.at[slot, i], recv_sem=recv_sem.at[slot, i],
            device_id=peers[step], device_id_type=pl.DeviceIdType.MESH)
        copy.start()
        copies.append(copy)
        return copy

    def part(w, i):
        return pl.ds(w * half + i * size, size)

    def local(i):
        return pl.ds(i * size, size)

    source = p_ref if source is None else source
    landed = landed or (lambda block, w, i: None)
    first = [[[start(source.at[near if j == 0 else 3, part(w, i)], got1.at[w, j, local(i)], near, 2 * w + j, i)
               for j in (0, 1)] for w, (near, far) in enumerate(ways)] for i in range(subs)]
    second, third, fourth = [None] * subs, [None] * subs, []
    if ready is not None:
        ready()
    for i in range(subs + 2):
        if i < subs:
            second[i] = []
            for w, (near, far) in enumerate(ways):
                first[i][w][1].wait_recv()
                both = p_ref[far, part(w, i)].astype(F32) + got1[w, 1, local(i)].astype(F32)
                pass2[w, local(i)] = both.astype(BF16)
                second[i].append(start(pass2.at[w, local(i)], got2.at[w, local(i)], far, 4 + w, i))
        if 1 <= i <= subs:
            k = i - 1
            third[k] = []
            for w in (0, 1):
                first[k][w][0].wait_recv()
                second[k][w].wait_recv()
                total = p_ref[0, part(w, k)].astype(F32) + got1[w, 0, local(k)].astype(F32)
                total = total + got2[w, local(k)].astype(F32)
                rows = middle(w * half + k * size, size, total)
                if not shared:
                    o_ref[part(w, k)] = rows
                    continue
                o_ref[0, part(w, k)] = rows
                third[k].append([start(o_ref.at[0, part(w, k)], o_ref.at[step, part(w, k)], step, 5 + 2 * w + step, k)
                                 for step in (1, 2)])
                landed(0, w, k)
        if i >= 2 and shared:
            k = i - 2
            for w, (near, far) in enumerate(ways):
                third[k][w][far - 1].wait_recv()
                fourth.append(start(o_ref.at[far, part(w, k)], o_ref.at[3, part(w, k)], near, 10 + w, k))
                landed(far, w, k)
        if beside is not None:
            beside(i)
    for copy in copies:
        copy.wait_send()
    for k in range(subs if shared else 0):
        for w, (near, far) in enumerate(ways):
            third[k][w][near - 1].wait_recv()
            landed(near, w, k)
    for at, copy in enumerate(fourth):
        copy.wait_recv()
        landed(3, at % 2, at // 2)


def forward_relay_kernel(unit, subs, p_ref, x_ref, gain_ref, o_ref, resid_ref, got1, pass2, got2, ordered, *sems):
    def middle(at, size, total):
        rows = pl.ds(at, size)
        resid = total + x_ref[rows].astype(F32)
        resid_ref[rows] = resid
        normed = resid * lax.rsqrt(jnp.mean(resid * resid, axis=1, keepdims=True) + 1e-06) * gain_ref[...]
        half = normed.shape[1] // 2
        for j in range(half // unit):
            for k in (0, 1):
                ordered[:, k * half + j * unit:k * half + (j + 1) * unit] = normed[:, (2 * j + k) * unit:(2 * j + k + 1) * unit]
        return ordered[...].astype(BF16)

    relay(p_ref, o_ref, got1, pass2, got2, sems, subs, middle)


def norm_backward(unit, resid_ref, gain_ref, g_gain_ref, ordered, finish):
    g_gain_ref[...] = jnp.zeros_like(g_gain_ref)

    def middle(at, size, total):
        rows = pl.ds(at, size)
        half = total.shape[1] // 2
        for j in range(half // unit):
            for k in (0, 1):
                ordered[:, (2 * j + k) * unit:(2 * j + k + 1) * unit] = total[:, k * half + j * unit:k * half + (j + 1) * unit]
        d = ordered[...]
        resid = resid_ref[rows].astype(F32)
        scale = lax.rsqrt(jnp.mean(resid * resid, axis=1, keepdims=True) + 1e-06)
        unit_resid = resid * scale
        g_gain_ref[...] += jnp.sum(d * unit_resid, axis=0, keepdims=True)
        d = d * gain_ref[...]
        d = scale * (d - unit_resid * jnp.mean(d * unit_resid, axis=1, keepdims=True))
        return finish(rows, d)

    return middle


def backward_relay_kernel(unit, subs, parts, p_hbm, resid_hbm, cot_hbm, gain_ref, *refs):
    hidden_hbm, (branch_hbm, down_hbm, o_hbm, d_resid_hbm, g_gain_ref, g_down_hbm, kept_hbm, one_hbm, two_hbm, *refs) = refs[:parts], refs[parts:]
    (got1, pass2, got2, ordered, send_sem, recv_sem, hidden, branch, down, g_down, g_other, terms,
     in_sem, out_sem, core_send, core_recv, p_ref, resid_ref, cot_ref, o_ref, d_resid_ref, block_sem, resid_sem) = refs
    z, t, c = (lax.axis_index(a) for a in ALL)
    loads, at = [(p_hbm, p_ref), (resid_hbm, resid_ref), (cot_hbm, cot_ref)], 0
    for source in hidden_hbm:
        loads.append((source, hidden.at[:, at:at + source.shape[1]]))
        at += source.shape[1]
    loads += [(branch_hbm, branch), (down_hbm, down)]
    loads = [pltpu.make_async_copy(src, dst, in_sem.at[i]) for i, (src, dst) in enumerate(loads)]
    for copy in loads:
        copy.start()
    width = branch.shape[1] // subs
    _, zs, cs, count, _ = g_down.shape
    stores, crossings = [], []

    def beside(i):
        if i == 0:
            for copy in loads[1:]:
                copy.wait()
        cols = slice(i * width, (i + 1) * width)
        if i < subs:
            g = mm(hidden[...], branch[:, cols], TN).astype(BF16)
            for j in range(zs):
                for k in range(cs):
                    at = (j * cs + k) * count
                    g_down[i, j, k] = g[at:at + count]
            crossings.append(pltpu.make_async_remote_copy(
                src_ref=g_down.at[i, :, 1 - c], dst_ref=g_other.at[i], send_sem=core_send.at[i], recv_sem=core_recv.at[i],
                device_id=(z, t, 1 - c), device_id_type=pl.DeviceIdType.MESH))
            crossings[i].start()
            terms[i] = mm(hidden[...], down[:, cols], NN).astype(BF16)
            half = terms.shape[1] // (2 * TP)
            places = ((kept_hbm, 0, 0, 2), (kept_hbm, 2, 4, 1), (kept_hbm, 3, 3, 1),
                      (one_hbm, 0, 2, 1), (one_hbm, 1, 6, 1), (two_hbm, 0, 5, 1), (two_hbm, 1, 7, 1))
            for j, (target, at, low, size) in enumerate(places):
                stores.append(pltpu.make_async_copy(
                    terms.at[i, low * half:(low + size) * half], target.at[at * half:(at + size) * half, cols], out_sem.at[j, i]))
                stores[-1].start()
        if 1 <= i <= subs:
            k = i - 1
            crossings[k].wait()
            g_other[k] = (g_other[k].astype(F32) + g_down[k, :, c].astype(F32)).astype(BF16)
            stores.append(pltpu.make_async_copy(
                g_other.at[k], g_down_hbm.at[:, :, slice(k * width, (k + 1) * width)], out_sem.at[7, k]))
            stores[-1].start()

    def finish(rows, d):
        d = d + cot_ref[rows].astype(F32)
        d_resid_ref[rows] = d
        return d.astype(BF16)

    middle = norm_backward(unit, resid_ref, gain_ref, g_gain_ref, ordered, finish)
    part = o_ref.shape[1] // (2 * subs)

    def landed(block, w, i):
        rows = pl.ds((w * subs + i) * part, part)
        stores.append(pltpu.make_async_copy(o_ref.at[block, rows], o_hbm.at[block, rows], block_sem.at[block, w, i]))
        stores[-1].start()
        if block == 0:
            stores.append(pltpu.make_async_copy(d_resid_ref.at[rows], d_resid_hbm.at[rows], resid_sem.at[w, i]))
            stores[-1].start()

    relay(p_ref, o_ref, got1, pass2, got2, (send_sem, recv_sem), subs, middle, beside=beside, cores=True,
          source=p_hbm, ready=loads[0].wait, landed=landed)
    for copy in stores:
        copy.wait()


def settle_kernel(unit, subs, p_ref, x_ref, d_resid_ref, gain_ref, d_low_ref, f_low_ref, d_f_ref, g_head_ref,
                  g_mlp_ref, act_hbm, d_attn_hbm, h_hbm, o_ref, flat_ref, g_out_hbm,
                  got1, pass2, got2, ordered, send_sem, recv_sem,
                  act, d_attn, h, g_out, g_sum, g_gain_ref, in_sem, core_send, core_recv, swap_own, swap_send, swap_recv):
    z, t, c = (lax.axis_index(a) for a in ALL)
    loads = [pltpu.make_async_copy(src, dst, in_sem.at[i])
             for i, (src, dst) in enumerate([(act_hbm, act), (d_attn_hbm, d_attn), (h_hbm, h)])]
    for copy in loads:
        copy.start()
    crossing = pltpu.make_async_remote_copy(
        src_ref=g_out.at[:, :, 1 - c], dst_ref=g_sum, send_sem=core_send, recv_sem=core_recv,
        device_id=(z, t, 1 - c), device_id_type=pl.DeviceIdType.MESH)
    copies = []
    n = flat_ref.shape[0]
    deep, _, cs, rows, D = g_out.shape
    rank = f_low_ref.shape[1]

    def beside(i):
        if i == 0:
            for copy in loads:
                copy.wait()
            for low in range(0, D, D // 4):
                cols = slice(low, low + D // 4)
                g = mm(act[...], d_attn[:, cols], TN).astype(BF16)
                for j in range(deep):
                    for k in range(TP):
                        for m in range(cs):
                            at = ((j * TP + k) * cs + m) * rows
                            g_out[j, k, m, :, cols] = g[at:at + rows]
            crossing.start()
        if i == 1:
            crossing.wait()
            g_sum[...] = (g_sum[...].astype(F32) + g_out[:, :, c].astype(F32)).astype(BF16)
            for step in (3, 1, 2):
                peer = chip_peer(t, step)
                copies.append(pltpu.make_async_remote_copy(
                    src_ref=g_sum.at[:, peer], dst_ref=g_out_hbm.at[t], send_sem=swap_send.at[step - 1],
                    recv_sem=swap_recv.at[step - 1], device_id=(z, peer, c), device_id_type=pl.DeviceIdType.MESH))
                copies[-1].start()
            copies.append(pltpu.make_async_copy(g_sum.at[:, t], g_out_hbm.at[t], swap_own))
            copies[-1].start()
        if i == 2:
            flat_ref[...] = jnp.zeros_like(flat_ref)
            g_fd = mm(d_low_ref[...], h[...], TN)
            g_fu = mm(f_low_ref[...], d_f_ref[...], TN)
            zs = n // (TP * cs)
            each, wide = n // TP, g_fu.shape[1] * TP // n
            heads = g_head_ref.shape[1] // n
            for j in range(n):
                at = ((j % cs) * zs + j // (TP * cs)) * TP + j // cs % TP
                flat_ref[j, :rank, :unit] = g_fd[:, at * unit:(at + 1) * unit]
                flat_ref[j, rank:rank + 1, unit:unit + heads] = g_head_ref[:, j * heads:(j + 1) * heads]
                flat_ref[j, rank + 1:rank + 2, :unit] = g_mlp_ref[:, j * unit:(j + 1) * unit]
            for j in range(each):
                flat_ref[t * each + j, :rank, unit:unit + wide] = g_fu[:, j * wide:(j + 1) * wide]

    def finish(at, d):
        return (d + d_resid_ref[at]).astype(BF16)

    middle = norm_backward(unit, x_ref, gain_ref, g_gain_ref, ordered, finish)
    relay(p_ref, o_ref, got1, pass2, got2, (send_sem, recv_sem), subs, middle, False, beside, True, True)
    for j in range(n):
        flat_ref[j, rank:rank + 1, :unit] = g_gain_ref[:, j * unit:(j + 1) * unit]
    for copy in copies:
        copy.wait()


def relay_scratch(count, D, subs):
    half, size = count // 2, count // 2 // subs
    return [
        pltpu.VMEM((2, 2, half, D), BF16),
        pltpu.VMEM((2, half, D), BF16),
        pltpu.VMEM((2, half, D), BF16),
        pltpu.VMEM((size, D), F32),
        pltpu.SemaphoreType.DMA((12, subs)),
        pltpu.SemaphoreType.DMA((12, subs)),
    ]


SUBS = 4


def relay_forward(p, x, gain, unit, ident):
    _, count, D = p.shape
    fast = pl.BlockSpec(memory_space=pltpu.VMEM)
    return pl.pallas_call(
        functools.partial(forward_relay_kernel, unit, SUBS),
        out_shape=(jax.ShapeDtypeStruct(p.shape, BF16), jax.ShapeDtypeStruct(x.shape, F32)),
        in_specs=[fast] * 3,
        out_specs=(fast,) * 2,
        scratch_shapes=relay_scratch(count, D, SUBS),
        compiler_params=pltpu.CompilerParams(collective_id=ident, has_side_effects=True, vmem_limit_bytes=40 << 20),
        name="relay_forward",
    )(p, x, gain)


def relay_backward(p, resid, cot, gain, hidden, branch, down, unit, zs, cs, ident):
    _, count, D = p.shape
    tokens = hidden[0].shape[0]
    units = down.shape[0]
    width = D // SUBS
    each = units // (zs * cs)
    fast = pl.BlockSpec(memory_space=pltpu.VMEM)
    anywhere = pl.BlockSpec(memory_space=pl.ANY)
    return pl.pallas_call(
        functools.partial(backward_relay_kernel, unit, SUBS, len(hidden)),
        out_shape=(
            jax.ShapeDtypeStruct(p.shape, BF16),
            jax.ShapeDtypeStruct(resid.shape, F32),
            jax.ShapeDtypeStruct((1, D), F32),
            jax.ShapeDtypeStruct((zs, each, D), BF16),
        ) + tuple(jax.ShapeDtypeStruct((rows, D), BF16) for rows in (tokens // 2, tokens // 4, tokens // 4)),
        in_specs=[anywhere] * 3 + [fast] + [anywhere] * (len(hidden) + 2),
        out_specs=(anywhere,) * 2 + (fast,) + (anywhere,) * 4,
        scratch_shapes=relay_scratch(count, D, SUBS) + [
            pltpu.VMEM((tokens, units), BF16),
            pltpu.VMEM(branch.shape, BF16),
            pltpu.VMEM(down.shape, BF16),
            pltpu.VMEM((SUBS, zs, cs, each, width), BF16),
            pltpu.VMEM((SUBS, zs, each, width), BF16),
            pltpu.VMEM((SUBS, tokens, width), BF16),
            pltpu.SemaphoreType.DMA((len(hidden) + 5,)),
            pltpu.SemaphoreType.DMA((8, SUBS)),
            pltpu.SemaphoreType.DMA((SUBS,)),
            pltpu.SemaphoreType.DMA((SUBS,)),
            pltpu.VMEM(p.shape, BF16),
            pltpu.VMEM(resid.shape, F32),
            pltpu.VMEM(cot.shape, BF16),
            pltpu.VMEM(p.shape, BF16),
            pltpu.VMEM(resid.shape, F32),
            pltpu.SemaphoreType.DMA((TP, 2, SUBS)),
            pltpu.SemaphoreType.DMA((2, SUBS)),
        ],
        compiler_params=pltpu.CompilerParams(collective_id=ident, has_side_effects=True, vmem_limit_bytes=60 << 20),
        name="relay_backward",
    )(p, resid, cot, gain, *hidden, branch, down)


def settle(p, x, d_resid, gain, d_low, f_low, d_f, g_head, g_mlp, act, d_attn, h, unit, zs, cs, ident):
    _, count, D = p.shape
    fast = pl.BlockSpec(memory_space=pltpu.VMEM)
    anywhere = pl.BlockSpec(memory_space=pl.ANY)
    deep = zs // TP
    rank = f_low.shape[1]
    return pl.pallas_call(
        functools.partial(settle_kernel, unit, SUBS),
        out_shape=(
            jax.ShapeDtypeStruct(p.shape[1:], BF16),
            jax.ShapeDtypeStruct((zs * TP * cs, rank + 8, LANES), F32),
            jax.ShapeDtypeStruct((TP, deep, unit, D), BF16),
        ),
        in_specs=[fast] * 9 + [anywhere] * 3,
        out_specs=(fast,) * 2 + (anywhere,),
        scratch_shapes=relay_scratch(count, D, SUBS) + [
            pltpu.VMEM(act.shape, BF16),
            pltpu.VMEM(d_attn.shape, BF16),
            pltpu.VMEM(h.shape, BF16),
            pltpu.VMEM((deep, TP, cs, unit, D), BF16),
            pltpu.VMEM((deep, TP, unit, D), BF16),
            pltpu.VMEM((1, D), F32),
            pltpu.SemaphoreType.DMA((3,)),
            pltpu.SemaphoreType.DMA,
            pltpu.SemaphoreType.DMA,
            pltpu.SemaphoreType.DMA,
            pltpu.SemaphoreType.DMA((TP - 1,)),
            pltpu.SemaphoreType.DMA((TP - 1,)),
        ],
        compiler_params=pltpu.CompilerParams(collective_id=ident, has_side_effects=True, vmem_limit_bytes=56 << 20),
        name="settle",
    )(p, x, d_resid, gain, d_low, f_low, d_f, g_head, g_mlp, act, d_attn, h)


def ff_kernel(tile, hm_ref, gu_ref, d_hidden_ref, hidden_ref, d_gu_ref):
    for at in range(0, hm_ref.shape[0], tile):
        rows = slice(at, at + tile)
        pre = mm(hm_ref[rows, :], gu_ref[...], NN)
        gate, up = pre[:, :LANES], pre[:, LANES:]
        sig = 0.5 * jnp.tanh(0.5 * gate) + 0.5
        act = gate * sig
        d_hidden = d_hidden_ref[rows, :]
        hidden_ref[rows, :] = (act * up).astype(BF16)
        d_gu_ref[rows, :LANES] = (d_hidden * up * (sig + act * (1.0 - sig))).astype(BF16)
        d_gu_ref[rows, LANES:] = (d_hidden * act).astype(BF16)


def ff_forward(hm, gu, d_hidden, first):
    tokens, D = hm.shape
    columns = gu.shape[1]
    wide = pl.BlockSpec((tokens, 2 * LANES), lambda j: (0, j))
    return pl.pallas_call(
        functools.partial(ff_kernel, 256),
        out_shape=(jax.ShapeDtypeStruct((tokens, columns // 2), BF16), jax.ShapeDtypeStruct((tokens, columns), BF16)),
        grid=(columns // (2 * LANES),),
        in_specs=[
            pl.BlockSpec((tokens, D), lambda j: (0, 0)),
            pl.BlockSpec((D, 2 * LANES), lambda j: (0, j)),
            pl.BlockSpec((tokens, LANES), lambda j: (0, j + first)),
        ],
        out_specs=(pl.BlockSpec((tokens, LANES), lambda j: (0, j)), wide),
        compiler_params=pltpu.CompilerParams(vmem_limit_bytes=48 << 20),
        name="feed_forward",
    )(hm, gu, d_hidden)


def d_hm_kernel(tile, count, *refs):
    grads, weights, o_ref = refs[:count], refs[count:2 * count], refs[2 * count]
    for at in range(0, o_ref.shape[0], tile):
        rows = slice(at, at + tile)
        o_ref[rows, :] = sum(mm(g[rows, :], w[...], NT) for g, w in zip(grads, weights)).astype(BF16)


def d_hm_product(grads, weights):
    tokens, D = grads[0].shape[0], weights[0].shape[0]
    width = 256
    return pl.pallas_call(
        functools.partial(d_hm_kernel, 256, len(grads)),
        out_shape=jax.ShapeDtypeStruct((tokens, D), BF16),
        grid=(D // width,),
        in_specs=[pl.BlockSpec(g.shape, lambda j: (0, 0)) for g in grads]
        + [pl.BlockSpec((width, w.shape[1]), lambda j: (j, 0)) for w in weights],
        out_specs=pl.BlockSpec((tokens, width), lambda j: (0, j)),
        compiler_params=pltpu.CompilerParams(vmem_limit_bytes=48 << 20),
        name="d_hm",
    )(*grads, *weights)


def heads_kernel(steps, count, own_hbm, other_hbm, d_pre_hbm, *refs):
    blocks, (o_hbm, *refs) = refs[:count], refs[count:]
    returned, refs = refs[:count], refs[count:]
    (own, other, d_pre, sent, got, own_sem, back_send, back_recv, in_sem, out_sem, core_send, core_recv) = refs
    z, t, c = (lax.axis_index(a) for a in ALL)
    width = d_pre.shape[2]
    cols = [slice(i * width, (i + 1) * width) for i in range(steps)]
    loads = [pltpu.make_async_copy(other_hbm, other, in_sem.at[0])]
    loads += [pltpu.make_async_copy(d_pre_hbm.at[:, cols[i]], d_pre.at[i], in_sem.at[2 + i]) for i in range(steps)]
    loads += [pltpu.make_async_copy(own_hbm, own, in_sem.at[1])]
    for copy in loads:
        copy.start()
    barrier = pltpu.get_barrier_semaphore()
    for device in [(z, chip_peer(t, step), c) for step in (1, 2, 3)] + [(z, t, 1 - c)]:
        pl.semaphore_signal(barrier, inc=1, device_id=device, device_id_type=pl.DeviceIdType.MESH)
    pl.semaphore_wait(barrier, TP)
    copies = send_blocks(blocks, returned, own_sem, back_send, back_recv)
    crossings = []
    loads[0].wait()
    for i in range(steps):
        loads[1 + i].wait()
        sent[i] = mm(other[...], d_pre[i], TN).astype(BF16)
        crossings.append(pltpu.make_async_remote_copy(
            src_ref=sent.at[i], dst_ref=got.at[i], send_sem=core_send.at[i], recv_sem=core_recv.at[i],
            device_id=(z, t, 1 - c), device_id_type=pl.DeviceIdType.MESH))
        crossings[i].start()
    loads[-1].wait()
    for i in range(steps):
        g = mm(own[...], d_pre[i], TN)
        crossings[i].wait_recv()
        got[i] = (g + got[i].astype(F32)).astype(BF16)
        copies.append(pltpu.make_async_copy(got.at[i], o_hbm.at[:, cols[i]], out_sem.at[i]))
        copies[-1].start()
    for copy in crossings:
        copy.wait_send()
    for copy in copies:
        copy.wait()


def heads_gradient(own, other, d_pre, blocks, ident):
    tokens, half = own.shape
    columns = d_pre.shape[1]
    steps = 4
    width = columns // steps
    count = len(blocks)
    anywhere = pl.BlockSpec(memory_space=pl.ANY)
    return pl.pallas_call(
        functools.partial(heads_kernel, steps, count),
        out_shape=(jax.ShapeDtypeStruct((half, columns), BF16),)
        + tuple(jax.ShapeDtypeStruct(b.shape, b.dtype) for b in blocks),
        in_specs=[anywhere] * (3 + count),
        out_specs=(anywhere,) * (1 + count),
        scratch_shapes=[
            pltpu.VMEM((tokens, half), BF16),
            pltpu.VMEM((tokens, half), BF16),
            pltpu.VMEM((steps, tokens, width), BF16),
            pltpu.VMEM((steps, half, width), BF16),
            pltpu.VMEM((steps, half, width), BF16),
        ] + block_sems(count) + [
            pltpu.SemaphoreType.DMA((2 + steps,)),
            pltpu.SemaphoreType.DMA((steps,)),
            pltpu.SemaphoreType.DMA((steps,)),
            pltpu.SemaphoreType.DMA((steps,)),
        ],
        compiler_params=pltpu.CompilerParams(collective_id=ident, has_side_effects=True, vmem_limit_bytes=56 << 20),
        name="heads_gradient",
    )(own, other, d_pre, *blocks)


def send_t(x, step):
    return lax.ppermute(x, "t", [(i, i ^ step) for i in range(TP)])


def send_c(x):
    return lax.ppermute(x, "c", [(0, 1), (1, 0)])


def gather_t_begin(x):
    return send_t(x, 1), send_t(x, 2)


def gather_t_end(x, one, two):
    half = x.shape[0] // 2
    return jnp.concatenate([x, one, two, send_t(two[:half], 1), send_t(one[half:], 2)], axis=0)


def scatter_t_middle(kept, got):
    half = kept.shape[0] // 4
    first, second = got

    def add(low, v):
        return kept[low:low + half].astype(F32) + v.astype(F32)

    part = jnp.concatenate([add(0, first[:half]), add(half, second[:half])], axis=0)
    return part, (add(2 * half, first[half:]).astype(BF16), add(3 * half, second[half:]).astype(BF16))


def scatter_t_pass(passed):
    return send_t(passed[0], 2), send_t(passed[1], 1)


def swap_t(x):
    t = lax.axis_index("t")

    def block(a, j):
        return lax.dynamic_index_in_dim(a, j, 0, keepdims=False)

    got = jnp.stack([block(x, t)] + [send_t(block(x, t ^ k), k) for k in (1, 2, 3)])
    return jnp.stack([block(got, t ^ j) for j in range(TP)])


def dot(left, right):
    return mm(left, right, NN)


def dot_nt(left, right):
    return mm(left, right, NT)


def dot_tn(left, right):
    return mm(left, right, TN)


def after(x, *others):
    return lax.optimization_barrier((x,) + others)[:2]


def rms_norm(v, gain):
    return v * lax.rsqrt(jnp.mean(v * v, axis=-1, keepdims=True) + 1e-06) * gain


def swiglu(gate_val, up_val):
    return jax.nn.silu(gate_val) * up_val


def per_device(zs, cs, tokens, starts, w_query, w_key, w_value, w_gate_out, w_out, w_forget_down,
               w_forget_up, norm_attn, norm_head, norm_mlp, w_gate, w_up, w_down, cotangent):
    seqs, seq_len, D = tokens.shape
    n = zs * TP * cs
    rows = w_query.shape[0]
    ff_rows = w_down.shape[0]
    rank = w_forget_down.shape[1]
    fu_cols = w_forget_up.shape[1]
    mine = seqs * seq_len
    half = D // cs
    t_idx, c_idx = lax.axis_index("t"), lax.axis_index("c")

    def to_k(v):
        return v.reshape(-1, zs, TP, cs, rows).transpose(0, 3, 1, 2, 4).reshape(-1, D)

    def from_k(v):
        return v.reshape(-1, cs, zs, TP, rows).transpose(0, 2, 3, 1, 4).reshape(-1, D)

    def sum_z(v):
        return lax.psum_scatter(v, "z", scatter_dimension=0, tiled=True)

    def core_half(v, core):
        return lax.dynamic_slice_in_dim(v, core * half, half, axis=1)

    def other_term(left, right):
        return dot_tn(left, right).astype(BF16)

    def own_term(left, right, other):
        return (dot_tn(left, right) + send_c(other).astype(F32)).astype(BF16)

    docs = jnp.cumsum(starts, axis=1).astype(BF16)
    small = pack_rows([w_forget_down.reshape(-1), w_forget_up.reshape(-1), norm_attn, norm_head, norm_mlp,
                       docs.reshape(-1)], 16)
    sizes = [rows * rank, rank * fu_cols, norm_attn.shape[0], norm_head.shape[0], norm_mlp.shape[0]]
    by_rows = lax.all_gather(jnp.concatenate([w_out, w_down], axis=0), ("z", "c"), axis=0, tiled=True)
    by_rows = by_rows.reshape(zs, cs, rows + ff_rows, D)
    cot = cotangent.reshape(mine, D)
    w4 = spread([w_query, w_key, w_value, w_gate_out], 0)
    small, w4 = after(small, w4)
    small = share(small, n, cs, 9)
    piece = cs * ff_rows
    units = zs * piece
    middle = units // LANES // 2 * 2 * LANES
    parts = ((0, middle), (middle, 2 * units))
    w_gate, small = after(w_gate, small)
    gus = spread_ff(w_gate, w_up, piece, parts, 2)
    pieces = cut(small.reshape(n, -1), sizes + [mine])
    wfd = to_k(pieces[0].reshape(D, rank).T).T
    wfu = pieces[1].reshape(n, rank, fu_cols).transpose(1, 0, 2).reshape(rank, n * fu_cols)
    wfu = lax.dynamic_slice_in_dim(wfu, t_idx * SLOTS, SLOTS, axis=1)
    gain_attn = pieces[2].reshape(-1).astype(F32)
    gain_head = pieces[3].reshape(1, -1).astype(F32)
    gain_mlp = pieces[4].reshape(1, -1).astype(F32)
    all_docs = pieces[5].reshape(zs, TP, cs, mine)
    all_docs = lax.dynamic_index_in_dim(all_docs, lax.axis_index("z"), 0, keepdims=False)
    all_docs = lax.dynamic_index_in_dim(all_docs, lax.axis_index("c"), 1, keepdims=False)
    docs = jnp.concatenate([lax.dynamic_index_in_dim(all_docs, t_idx ^ k, 0) for k in range(TP)], axis=0)
    docs = docs.astype(F32).reshape(TP * seqs, seq_len)

    def by_columns(w):
        return lax.all_gather(w.reshape(TP * rows, -1), ("c", "z"), axis=0, tiled=True)

    w4 = by_columns(w4)
    gus = [by_columns(gu) for gu in gus]
    down = by_rows[:, :, rows:].reshape(-1, D)
    wo = swap_t(by_rows[:, :, :rows].reshape(TP, -1, rows, D)).reshape(TP, zs // TP, cs, rows, D)
    wo = wo.transpose(1, 0, 2, 3, 4).reshape(HEAD, D)

    x = tokens.reshape(mine, D).astype(F32)
    normed_in, norm_in_back = jax.vjp(rms_norm, x, gain_attn)
    h = to_k(normed_in.astype(BF16))
    h = gather_t_end(h, *gather_t_begin(h))
    d_branch = gather_t_end(cot, *gather_t_begin(cot))
    d_hidden = dot_nt(d_branch, down)
    h, d_hidden = after(h, d_hidden)
    h, wo = after(h, wo)
    h_own, h_other = after(core_half(h, c_idx), core_half(h, 1 - c_idx))
    h, h_own = after(h, h_own)
    pre = dot(h, w4)
    f_low = dot(h, wfd).astype(BF16)
    act = slots_forward(pre, f_low, wfu, gain_head, docs)
    terms = dot(act, wo).astype(BF16)
    tokens_flat = tokens.reshape(mine, D)
    hm, resid = relay_forward(terms.reshape(TP, mine, D), tokens_flat, gain_mlp, rows, 6)
    hm = hm.reshape(TP * mine, D)

    hidden, d_gus, g_gus = [], [], []
    for gu, (low, high) in zip(gus, parts):
        part, d_gu = ff_forward(hm, gu, d_hidden, low // (2 * LANES))
        hidden.append(part)
        d_gus.append(d_gu)
        g_gu = other_term(core_half(hm, 1 - c_idx), d_gu)
        if high == 2 * units:
            d_gus[-1], _ = after(d_gu, g_gu)
            d_hm = d_hm_product(d_gus, gus)
            hm, _ = after(hm, d_hm)
        g_gu = own_term(core_half(hm, c_idx), d_gu, g_gu)
        hm, g_gu = after(hm, g_gu)
        g_gus.append(sum_z(g_gu).reshape(TP, rows, -1))
    d_hm, _ = after(d_hm, g_gu)
    d_attn, d_resid, g_norm_mlp, g_down, *branch = relay_backward(
        d_hm.reshape(TP, mine, D), resid, cot, gain_mlp, hidden, d_branch, down, rows, zs, cs, 7)
    d_attn = d_attn.reshape(TP * mine, D)
    g_down = sum_z(g_down.reshape(-1, D))

    d_attn, g_gus[0] = after(d_attn, g_gus[0])
    d_attn, g_gus[1] = after(d_attn, g_gus[1])
    first = send_t(branch[1], 1), send_t(branch[2], 2)
    d_act = dot_nt(d_attn, wo).astype(BF16)
    count = TP * seqs
    ahead = count * 5 // 8
    *begun, g_norm_head = slots_backward(pre, f_low, wfu, gain_head, docs, d_act, 0, ahead)
    first, begun = after(first, begun)
    part, passed = scatter_t_middle(branch[0], first)
    d_act, passed = after(d_act, passed)
    second = scatter_t_pass(passed)
    d_pre, d_f, d_low, g_more = slots_backward(
        pre, f_low, wfu, gain_head, docs, d_act, ahead, count - ahead, begun)
    g_norm_head = g_norm_head + g_more
    d_pre, second = after(d_pre, second)
    g4, *g_gus = heads_gradient(h_own, h_other, d_pre, g_gus, 3)
    d_pre, _ = after(d_pre, g4)
    d_pre, g_down = after(d_pre, g_down)
    g4 = sum_z(g4)
    d_h = (dot_nt(d_pre, w4) + dot_nt(d_low, wfd)).astype(BF16)
    tokens_grad, flat, g_out = settle(
        d_h.reshape(TP, mine, D), tokens_flat, d_resid, gain_attn.reshape(1, D), d_low, f_low, d_f, g_norm_head,
        g_norm_mlp, act, d_attn, h, rows, zs, cs, 8)
    g_out = sum_z(g_out.reshape(-1, D))

    second, tokens_grad = after(second, tokens_grad)
    mixed = (resid + part + jnp.concatenate(second, axis=0).astype(F32)).astype(BF16)
    g_gate, g_up = widen(g_gus, ff_moves(piece, units, parts), 2, n * ff_rows)
    g_down = g_down.astype(F32)
    g4, mixed, tokens_grad, g_gate, g_up, g_down = lax.optimization_barrier(
        (g4, mixed, tokens_grad, g_gate, g_up, g_down))
    small, g4 = finish(flat, g4.reshape(TP, rows, -1), n, cs)
    heads = norm_head.shape[0]
    head_moves = [(i, j * HEAD, 0, j, i * HEAD, HEAD) for i in range(4) for j in range(TP)]
    g_heads, g_out = after(widen([g4], head_moves, 4, D), g_out)
    g_query, g_key, g_value, g_gate_out = g_heads
    g_out = g_out.astype(F32)
    return (
        mixed.reshape(tokens.shape),
        tokens_grad.reshape(tokens.shape),
        g_query, g_key, g_value, g_gate_out,
        g_out,
        small[:rank, :rows].T,
        small[:rank, rows:rows + fu_cols],
        small[rank, :rows],
        small[rank, rows:rows + heads],
        small[rank + 1, :rows],
        g_gate, g_up,
        g_down,
    )


def solution(mesh):
    cs = mesh.shape["outer"]
    zs = mesh.shape["dp"] // TP
    grid = Mesh(mesh.devices.reshape(zs, TP, cs), ALL)
    whole, row, vec = P(ALL, None, None), P(ALL, None), P(ALL)
    cols = P(None, ALL)

    def body(*args):
        return per_device(zs, cs, *args)

    return jax.shard_map(
        body,
        mesh=grid,
        in_specs=(whole, row, row, row, row, row, row, row, cols, vec, vec, vec, row, row, row, whole),
        out_specs=(whole, whole, row, row, row, row, row, row, cols, vec, vec, vec, row, row, row),
        check_vma=False,
    )
```

```python
import functools

import jax
import jax.numpy as jnp
from jax import lax
from jax.experimental import pallas as pl
from jax.experimental.pallas import tpu as pltpu
from jax.sharding import Mesh, PartitionSpec as P

HEADS = 4
HEAD = 512
SLOTS = 64
TP = 4
ALL = ("z", "t", "c")
F32 = jnp.float32
BF16 = jnp.bfloat16
SPAN = 80.0


def mm(a, b, dims):
    return lax.dot_general(a, b, (dims, ((), ())), preferred_element_type=F32)


NN, NT, TN = ((1,), (0,)), ((1,), (1,)), ((0,), (0,))


def split(a):
    high = a.astype(BF16)
    return high, (a - high.astype(F32)).astype(BF16)


def mm3(a, b, dims):
    ah, al = split(a)
    bh, bl = split(b)
    return mm(ah, bh, dims) + (mm(ah, bl, dims) + mm(al, bh, dims))


def mm_exact(mask, b, dims):
    b1, rest = split(b)
    b2 = rest
    b3 = (b - b1.astype(F32) - b2.astype(F32)).astype(BF16)
    return mm(mask, b1, dims) + (mm(mask, b2, dims) + mm(mask, b3, dims))


def swish_parts(v):
    sig = 1.0 / (1.0 + jnp.exp(-v))
    return v * sig, sig * (1.0 + v * (1.0 - sig))


def gates(f_low, wfu):
    f_pre = mm(f_low, wfu, NN)
    soft = jnp.log(1.0 + jnp.exp(-jnp.abs(f_pre)))
    log_f = (jnp.minimum(f_pre, 0.0) - soft) * 0.125
    return f_pre, log_f


def lower_tri(n, kind=BF16):
    rows = lax.broadcasted_iota(jnp.int32, (n, n), 0)
    cols = lax.broadcasted_iota(jnp.int32, (n, n), 1)
    return rows >= cols


def column(a, j):
    picked = lax.broadcasted_iota(jnp.int32, a.shape, 1) == j
    return jnp.sum(jnp.where(picked, a, 0.0), axis=1, keepdims=True)


def row(a, j):
    picked = lax.broadcasted_iota(jnp.int32, a.shape, 0) == j
    return jnp.sum(jnp.where(picked, a, 0.0), axis=0, keepdims=True)


def gap(total, j):
    return jnp.exp(jnp.minimum(total - row(total, j), 0.0))


def softmax(scores):
    e = jnp.exp(scores - jnp.max(scores, axis=1, keepdims=True))
    return e / jnp.sum(e, axis=1, keepdims=True)


def far_near(total):
    mid = 0.5 * total[-1:]
    return jnp.exp(total - mid), jnp.exp(mid - total)


def sum_over_j(mats, total, unit, fast, dest):
    n = total.shape[0]

    @pl.when(fast)
    def _():
        near, far = far_near(total)
        got = mm3(jnp.concatenate(mats, axis=0), far * unit, NN)
        for i, d in enumerate(dest):
            d[...] = got[i * n:(i + 1) * n] * near

    @pl.when(jnp.logical_not(fast))
    def _():
        for d in dest:
            d[...] = jnp.zeros_like(total)

        def step(j, _):
            e = gap(total, j) * row(unit, j)
            for d, m in zip(dest, mats):
                d[...] += column(m, j) * e
            return 0

        lax.fori_loop(0, n, step, 0)


def sum_over_m(probs, total, unit, fast, dest):
    n = total.shape[0]

    @pl.when(fast)
    def _():
        near, far = far_near(total)
        got = mm3(jnp.concatenate([p * near for p in probs], axis=0), far * unit, NT)
        for i, d in enumerate(dest):
            d[...] = got[i * n:(i + 1) * n]

    @pl.when(jnp.logical_not(fast))
    def _():
        cols = lax.broadcasted_iota(jnp.int32, (n, n), 1)

        def step(j, _):
            e = gap(total, j) * row(unit, j)
            for d, p in zip(dest, probs):
                d[...] = jnp.where(cols == j, jnp.sum(p * e, axis=1, keepdims=True), d[...])
            return 0

        lax.fori_loop(0, n, step, 0)


def sum_over_t(mats, probs, total, fast, dest):
    n = total.shape[0]

    @pl.when(fast)
    def _():
        near, far = far_near(total)
        got = mm3(jnp.concatenate(mats, axis=0), jnp.concatenate([p * near for p in probs], axis=0), TN)
        dest[...] = got * far

    @pl.when(jnp.logical_not(fast))
    def _():
        rows = lax.broadcasted_iota(jnp.int32, total.shape, 0)

        def step(j, _):
            e = gap(total, j)
            s = sum(column(m, j) * p for m, p in zip(mats, probs))
            dest[...] = jnp.where(rows == j, jnp.sum(s * e, axis=0, keepdims=True), dest[...])
            return 0

        lax.fori_loop(0, n, step, 0)


def mixer_forward(pre_ref, f_low_ref, wfu_ref, doc_col_ref, doc_row_ref, score_ref, mix_ref):
    pre = pre_ref[...]
    q, q_slope = swish_parts(pre[:, :HEAD])
    k, k_slope = swish_parts(pre[:, HEAD:2 * HEAD])
    q, k, v = q.astype(BF16), k.astype(BF16), pre[:, 2 * HEAD:3 * HEAD].astype(BF16)
    n = q.shape[0]
    tri = lower_tri(n)
    keep = tri & (doc_col_ref[0] == doc_row_ref[0])
    inner = jnp.where(keep, mm(q, k, NT) * HEAD ** -0.5, 0.0)
    f_pre, log_f = gates(f_low_ref[...], wfu_ref[...])
    total = mm_exact(tri.astype(BF16), log_f, NN)
    unit = 1.0 - jnp.exp(log_f)
    fast = jnp.min(total[-1:]) > -SPAN
    return q, k, v, q_slope, k_slope, keep, inner, f_pre, log_f, total, unit, fast


def forward_kernel(pre_ref, f_low_ref, wfu_ref, gain_ref, doc_col_ref, doc_row_ref, act_ref, score_ref, mix_ref):
    q, k, v, _, _, keep, inner, _, _, total, unit, fast = mixer_forward(
        pre_ref, f_low_ref, wfu_ref, doc_col_ref, doc_row_ref, score_ref, mix_ref)
    sum_over_j([inner], total, unit, fast, [score_ref])
    probs = softmax(score_ref[...])
    sum_over_m([probs], total, unit, fast, [mix_ref])
    mixing = jnp.where(keep, mix_ref[...], 0.0).astype(BF16)
    out = mm(mixing, v, NN)
    scale = lax.rsqrt(jnp.mean(out * out, axis=1, keepdims=True) + 1e-06)
    gate, _ = swish_parts(pre_ref[:, 3 * HEAD:])
    act_ref[...] = (out * scale * gain_ref[...] * gate).astype(BF16)


def backward_kernel(pre_ref, f_low_ref, wfu_ref, gain_ref, doc_col_ref, doc_row_ref, d_act_ref, *refs):
    d_pre_ref, d_f_ref, d_low_ref, g_gain_ref, score_ref, d_p_ref, mix_ref, d_inner_ref, k_ref = refs[-9:]
    q, k, v, q_slope, k_slope, keep, inner, f_pre, log_f, total, unit, fast = mixer_forward(
        pre_ref, f_low_ref, wfu_ref, doc_col_ref, doc_row_ref, score_ref, mix_ref)
    sum_over_j([inner], total, unit, fast, [score_ref])
    scores = score_ref[...]
    probs = softmax(scores)
    sum_over_m([probs], total, unit, fast, [mix_ref])
    mixing = jnp.where(keep, mix_ref[...], 0.0).astype(BF16)
    out = mm(mixing, v, NN)

    scale = lax.rsqrt(jnp.mean(out * out, axis=1, keepdims=True) + 1e-06)
    gain = gain_ref[...]
    gate, gate_slope = swish_parts(pre_ref[:, 3 * HEAD:])
    d_act = d_act_ref[...].astype(F32)
    d_gate = d_act * out * scale * gain * gate_slope
    d_norm = d_act * gate
    g_gain = jnp.sum(d_norm * out * scale, axis=0, keepdims=True)

    @pl.when(pl.program_id(0) == 0)
    def _():
        g_gain_ref[...] = jnp.zeros_like(g_gain_ref)

    g_gain_ref[...] += g_gain
    d_norm = d_norm * gain
    d_out = scale * (d_norm - out * (scale * scale) * jnp.mean(d_norm * out, axis=1, keepdims=True))
    d_out = d_out.astype(BF16)

    d_mix = jnp.where(keep, mm(d_out, v, NT), 0.0)
    d_v = mm(mixing, d_out, TN)
    sum_over_j([d_mix], total, unit, fast, [d_p_ref])
    d_p = d_p_ref[...]
    d_score = probs * (d_p - jnp.sum(probs * d_p, axis=1, keepdims=True))
    sum_over_m([d_score], total, unit, fast, [d_inner_ref])
    d_inner = jnp.where(keep, d_inner_ref[...], 0.0).astype(BF16)
    sum_over_t([d_mix, inner], [probs, d_score], total, fast, k_ref)
    k_sum = k_ref[...]
    d_total = probs * d_p + d_score * scores - unit * k_sum
    n = q.shape[0]
    tri = lower_tri(n).astype(BF16)
    d_log = mm_exact(tri, d_total, TN) - jnp.exp(log_f) * k_sum
    d_f = (d_log * (0.125 / (1.0 + jnp.exp(f_pre)))).astype(BF16)
    d_f_ref[...] = d_f
    d_low_ref[...] = mm(d_f, wfu_ref[...], NT).astype(BF16)
    d_q = mm(d_inner, k, NN) * HEAD ** -0.5
    d_k = mm(d_inner, q, TN) * HEAD ** -0.5
    d_pre_ref[:, :HEAD] = (d_q * q_slope).astype(BF16)
    d_pre_ref[:, HEAD:2 * HEAD] = (d_k * k_slope).astype(BF16)
    d_pre_ref[:, 2 * HEAD:3 * HEAD] = d_v.astype(BF16)
    d_pre_ref[:, 3 * HEAD:] = d_gate.astype(BF16)


def mixer_specs(length, rank, first=0):
    return [
        pl.BlockSpec((length, 4 * HEAD), lambda i: (i + first, 0)),
        pl.BlockSpec((length, rank), lambda i: (i + first, 0)),
        pl.BlockSpec((rank, SLOTS), lambda i: (0, 0)),
        pl.BlockSpec((1, HEAD), lambda i: (0, 0)),
        pl.BlockSpec((1, length, 1), lambda i: (i + first, 0, 0)),
        pl.BlockSpec((1, 1, length), lambda i: (i + first, 0, 0)),
    ]


def slots_forward(pre, f_low, wfu, gain, docs):
    count, length = docs.shape
    tm = pltpu.VMEM((length, SLOTS), F32)
    tj = pltpu.VMEM((length, length), F32)
    return pl.pallas_call(
        forward_kernel,
        out_shape=jax.ShapeDtypeStruct((count * length, HEAD), BF16),
        grid=(count,),
        in_specs=mixer_specs(length, f_low.shape[1]),
        out_specs=pl.BlockSpec((length, HEAD), lambda i: (i, 0)),
        scratch_shapes=[tm, tj],
        compiler_params=pltpu.CompilerParams(vmem_limit_bytes=32 << 20),
        name="slots_forward",
    )(pre, f_low, wfu, gain, docs[:, :, None], docs[:, None, :])


def slots_backward(pre, f_low, wfu, gain, docs, d_act, first, steps, begun=()):
    count, length = docs.shape
    rank = f_low.shape[1]
    tm = pltpu.VMEM((length, SLOTS), F32)
    tj = pltpu.VMEM((length, length), F32)
    block = lambda width: pl.BlockSpec((length, width), lambda i: (i + first, 0))
    return pl.pallas_call(
        backward_kernel,
        out_shape=(
            jax.ShapeDtypeStruct((count * length, 4 * HEAD), BF16),
            jax.ShapeDtypeStruct((count * length, SLOTS), BF16),
            jax.ShapeDtypeStruct((count * length, rank), BF16),
            jax.ShapeDtypeStruct((1, HEAD), F32),
        ),
        grid=(steps,),
        in_specs=mixer_specs(length, rank, first) + [block(HEAD)] + [pl.BlockSpec(memory_space=pl.ANY)] * len(begun),
        out_specs=(block(4 * HEAD), block(SLOTS), block(rank), pl.BlockSpec((1, HEAD), lambda i: (0, 0))),
        scratch_shapes=[tm, tm, tj, tj, tm],
        input_output_aliases={7 + i: i for i in range(len(begun))},
        compiler_params=pltpu.CompilerParams(vmem_limit_bytes=32 << 20),
        name="slots_backward",
    )(pre, f_low, wfu, gain, docs[:, :, None], docs[:, None, :], d_act, *begun)


def place(index, cs):
    return (index // (TP * cs), (index // cs) % TP, index % cs)


def greet_all(n, cs, me):
    barrier = pltpu.get_barrier_semaphore()

    def greet(step, _):
        pl.semaphore_signal(barrier, inc=1, device_id=place((me + step) % n, cs), device_id_type=pl.DeviceIdType.MESH)
        return 0

    lax.fori_loop(1, n, greet, 0)
    pl.semaphore_wait(barrier, n - 1)


def my_index(cs):
    return (lax.axis_index("z") * TP + lax.axis_index("t")) * cs + lax.axis_index("c")


def chip_peer(t, step):
    high, low = t // 2, t % 2
    return (high + step // 2) % 2 * 2 + (low + step % 2) % 2


def share_kernel(n, cs, x_ref, o_ref, send_sem, recv_sem):
    me = my_index(cs)
    greet_all(n, cs, me)

    def send(step, _):
        pltpu.make_async_remote_copy(
            src_ref=x_ref, dst_ref=o_ref.at[me], send_sem=send_sem, recv_sem=recv_sem,
            device_id=place((me + step) % n, cs), device_id_type=pl.DeviceIdType.MESH).start()
        return 0

    lax.fori_loop(1, n, send, 0)
    o_ref[me] = x_ref[...]
    others = o_ref.at[pl.ds(0, n - 1)]
    pltpu.make_async_copy(others, others, recv_sem).wait()
    pltpu.make_async_copy(others, others, send_sem).wait()


def share(x, n, cs, ident):
    return pl.pallas_call(
        functools.partial(share_kernel, n, cs),
        out_shape=jax.ShapeDtypeStruct((n,) + x.shape, x.dtype),
        in_specs=[pl.BlockSpec(memory_space=pltpu.VMEM)],
        out_specs=pl.BlockSpec(memory_space=pltpu.VMEM),
        scratch_shapes=[pltpu.SemaphoreType.DMA, pltpu.SemaphoreType.DMA],
        compiler_params=pltpu.CompilerParams(collective_id=ident, has_side_effects=True, vmem_limit_bytes=32 << 20),
        name="share_small",
    )(x)


def spread_kernel(count, *refs):
    srcs, (out, own_sem, send_sem, recv_sem) = refs[:count], refs[count:]
    z, t, c = (lax.axis_index(a) for a in ALL)
    greet_plane(z, t, c)
    width = srcs[0].shape[1] // TP

    def block(i, to, at):
        src = srcs[i].at[:, pl.ds(pl.multiple_of(to * width, 128), width)]
        return src, out.at[at, :, pl.ds(i * width, width)]

    copies = []
    for step in (3, 1, 2):
        peer = chip_peer(t, step)
        for i in range(count):
            src, dst = block(i, peer, t)
            copies.append(pltpu.make_async_remote_copy(
                src_ref=src, dst_ref=dst, send_sem=send_sem.at[step - 1, i], recv_sem=recv_sem.at[step - 1, i],
                device_id=(z, peer, c), device_id_type=pl.DeviceIdType.MESH))
            copies[-1].start()
    for i in range(count):
        src, dst = block(i, t, t)
        copies.append(pltpu.make_async_copy(src, dst, own_sem.at[i]))
        copies[-1].start()
    for copy in copies:
        copy.wait()


def spread(weights, ident):
    rows, columns = weights[0].shape
    anywhere = pl.BlockSpec(memory_space=pl.ANY)
    return pl.pallas_call(
        functools.partial(spread_kernel, len(weights)),
        out_shape=jax.ShapeDtypeStruct((TP, rows, len(weights) * columns // TP), weights[0].dtype),
        in_specs=[anywhere] * len(weights),
        out_specs=anywhere,
        scratch_shapes=block_sems(len(weights)),
        compiler_params=pltpu.CompilerParams(collective_id=ident, has_side_effects=True),
        name="spread",
    )(*weights)


def greet_plane(z, t, c):
    barrier = pltpu.get_barrier_semaphore()
    for step in (1, 2, 3):
        pl.semaphore_signal(barrier, inc=1, device_id=(z, chip_peer(t, step), c), device_id_type=pl.DeviceIdType.MESH)
    pl.semaphore_wait(barrier, TP - 1)


LANES = 128


def unit_runs(piece, units):
    cuts = sorted(set(range(0, units, piece)) | set(range(0, units, LANES)) | {units})
    return [(low, high - low) for low, high in zip(cuts, cuts[1:])]


def packed_at(unit, up):
    return unit // LANES * 2 * LANES + up * LANES + unit % LANES


def natural_at(unit, piece, chip):
    return (unit // piece * TP + chip) * piece + unit % piece


def spread_ff_kernel(piece, parts, wg_ref, wu_ref, *refs):
    outs, (packed, own_sem, send_sem, recv_sem) = refs[:len(parts)], refs[len(parts):]
    z, t, c = (lax.axis_index(a) for a in ALL)
    greet_plane(z, t, c)
    for j in range(TP):
        for up, w in enumerate((wg_ref, wu_ref)):
            for unit, count in unit_runs(piece, packed.shape[2] // 2):
                at, source = packed_at(unit, up), natural_at(unit, piece, j)
                packed[j, :, at:at + count] = w[:, source:source + count]
    copies = []
    for step in (3, 1, 2):
        peer = chip_peer(t, step)
        for i, ((low, high), out) in enumerate(zip(parts, outs)):
            copies.append(pltpu.make_async_remote_copy(
                src_ref=packed.at[peer, :, low:high], dst_ref=out.at[t], send_sem=send_sem.at[step - 1, i],
                recv_sem=recv_sem.at[step - 1, i], device_id=(z, peer, c), device_id_type=pl.DeviceIdType.MESH))
            copies[-1].start()
    for i, ((low, high), out) in enumerate(zip(parts, outs)):
        copies.append(pltpu.make_async_copy(packed.at[t, :, low:high], out.at[t], own_sem.at[i]))
        copies[-1].start()
    for copy in copies:
        copy.wait()


def spread_ff(w_gate, w_up, piece, parts, ident):
    rows, units = w_gate.shape
    fast = pl.BlockSpec(memory_space=pltpu.VMEM)
    anywhere = pl.BlockSpec(memory_space=pl.ANY)
    return pl.pallas_call(
        functools.partial(spread_ff_kernel, piece, parts),
        out_shape=tuple(jax.ShapeDtypeStruct((TP, rows, high - low), w_gate.dtype) for low, high in parts),
        in_specs=[fast, fast],
        out_specs=(anywhere,) * len(parts),
        scratch_shapes=[pltpu.VMEM((TP, rows, 2 * units // TP), w_gate.dtype)] + block_sems(len(parts)),
        compiler_params=pltpu.CompilerParams(collective_id=ident, has_side_effects=True, vmem_limit_bytes=32 << 20),
        name="spread_ff",
    )(w_gate, w_up)


def send_blocks(sources, targets, own_sem, send_sem, recv_sem):
    z, t, c = (lax.axis_index(a) for a in ALL)
    copies = []
    for step in (3, 1, 2):
        peer = chip_peer(t, step)
        for i, (source, target) in enumerate(zip(sources, targets)):
            copies.append(pltpu.make_async_remote_copy(
                src_ref=source.at[peer], dst_ref=target.at[t], send_sem=send_sem.at[step - 1, i],
                recv_sem=recv_sem.at[step - 1, i], device_id=(z, peer, c), device_id_type=pl.DeviceIdType.MESH))
            copies[-1].start()
    for i, (source, target) in enumerate(zip(sources, targets)):
        copies.append(pltpu.make_async_copy(source.at[t], target.at[t], own_sem.at[i]))
        copies[-1].start()
    return copies


def block_sems(count):
    return [pltpu.SemaphoreType.DMA((count,))] + [pltpu.SemaphoreType.DMA((TP - 1, count))] * 2


def ff_moves(piece, units, parts):
    moves = []
    for j in range(TP):
        for up in (0, 1):
            for unit, count in unit_runs(piece, units):
                at = packed_at(unit, up)
                source = [i for i, (low, high) in enumerate(parts) if low <= at < high][0]
                moves.append((up, natural_at(unit, piece, j), source, j, at - parts[source][0], count))
    return moves


def widen_kernel(moves, sources, *refs):
    for out, at, source, j, start, width in moves:
        refs[sources + out][:, at:at + width] = refs[source][j, :, start:start + width].astype(F32)


def widen(xs, moves, count, columns):
    fast = pl.BlockSpec(memory_space=pltpu.VMEM)
    return pl.pallas_call(
        functools.partial(widen_kernel, moves, len(xs)),
        out_shape=tuple(jax.ShapeDtypeStruct((xs[0].shape[1], columns), F32) for _ in range(count)),
        in_specs=[fast] * len(xs),
        out_specs=tuple(fast for _ in range(count)),
        compiler_params=pltpu.CompilerParams(vmem_limit_bytes=32 << 20),
        name="widen",
    )(*xs)


def finish_kernel(n, cs, x_ref, blocks_ref, o_ref, back_ref, got_ref, send_sem, recv_sem, *block_sem):
    me = my_index(cs)
    greet_all(n, cs, me)

    def send(step, _):
        peer = (me + step) % n
        pltpu.make_async_remote_copy(
            src_ref=x_ref.at[peer], dst_ref=got_ref.at[me], send_sem=send_sem, recv_sem=recv_sem,
            device_id=place(peer, cs), device_id_type=pl.DeviceIdType.MESH).start()
        return 0

    lax.fori_loop(1, n, send, 0)
    copies = send_blocks([blocks_ref], [back_ref], *block_sem)
    got_ref[me] = x_ref[me]
    others = got_ref.at[pl.ds(0, n - 1)]
    pltpu.make_async_copy(others, others, recv_sem).wait()
    pltpu.make_async_copy(others, others, send_sem).wait()
    o_ref[...] = jnp.sum(got_ref[...], axis=0)
    for copy in copies:
        copy.wait()


def finish(x, blocks, n, cs):
    anywhere = pl.BlockSpec(memory_space=pl.ANY)
    fast = pl.BlockSpec(memory_space=pltpu.VMEM)
    return pl.pallas_call(
        functools.partial(finish_kernel, n, cs),
        out_shape=(jax.ShapeDtypeStruct(x.shape[1:], x.dtype), jax.ShapeDtypeStruct(blocks.shape, blocks.dtype)),
        in_specs=[fast, anywhere],
        out_specs=(fast, anywhere),
        scratch_shapes=[pltpu.VMEM(x.shape, x.dtype), pltpu.SemaphoreType.DMA, pltpu.SemaphoreType.DMA] + block_sems(1),
        compiler_params=pltpu.CompilerParams(collective_id=1, has_side_effects=True, vmem_limit_bytes=32 << 20),
        name="finish",
    )(x, blocks)


def pack_rows(parts, unit):
    flat = jnp.concatenate(parts, axis=-1)
    size = flat.shape[-1]
    padded = -(-size // (unit * 128)) * unit * 128
    flat = jnp.pad(flat, [(0, 0)] * (flat.ndim - 1) + [(0, padded - size)])
    return flat.reshape(flat.shape[:-1] + (padded // 128, 128))


def cut(flat, sizes):
    at, pieces = 0, []
    for size in sizes:
        pieces.append(flat[..., at:at + size])
        at += size
    return pieces


def relay(p_ref, o_ref, got1, pass2, got2, sems, subs, middle, shared=True, beside=None, plane=False, cores=False,
          source=None, ready=None, landed=None):
    z, t, c = (lax.axis_index(a) for a in ALL)
    peers = {step: (z, chip_peer(t, step), c) for step in (1, 2)}
    barrier = pltpu.get_barrier_semaphore()
    met = [peers[1], peers[2]] + [(z, chip_peer(t, 3), c)] * plane + [(z, t, 1 - c)] * cores
    for device in met:
        pl.semaphore_signal(barrier, inc=1, device_id=device, device_id_type=pl.DeviceIdType.MESH)
    pl.semaphore_wait(barrier, len(met))
    send_sem, recv_sem = sems
    half = p_ref.shape[1] // 2
    size = half // subs
    ways = ((1, 2), (2, 1))
    copies = []

    def start(src, dst, step, slot, i):
        copy = pltpu.make_async_remote_copy(
            src_ref=src, dst_ref=dst, send_sem=send_sem.at[slot, i], recv_sem=recv_sem.at[slot, i],
            device_id=peers[step], device_id_type=pl.DeviceIdType.MESH)
        copy.start()
        copies.append(copy)
        return copy

    def part(w, i):
        return pl.ds(w * half + i * size, size)

    def local(i):
        return pl.ds(i * size, size)

    source = p_ref if source is None else source
    landed = landed or (lambda block, w, i: None)
    first = [[[start(source.at[near if j == 0 else 3, part(w, i)], got1.at[w, j, local(i)], near, 2 * w + j, i)
               for j in (0, 1)] for w, (near, far) in enumerate(ways)] for i in range(subs)]
    second, third, fourth = [None] * subs, [None] * subs, []
    if ready is not None:
        ready()
    for i in range(subs + 2):
        if i < subs:
            second[i] = []
            for w, (near, far) in enumerate(ways):
                first[i][w][1].wait_recv()
                both = p_ref[far, part(w, i)].astype(F32) + got1[w, 1, local(i)].astype(F32)
                pass2[w, local(i)] = both.astype(BF16)
                second[i].append(start(pass2.at[w, local(i)], got2.at[w, local(i)], far, 4 + w, i))
        if 1 <= i <= subs:
            k = i - 1
            third[k] = []
            for w in (0, 1):
                first[k][w][0].wait_recv()
                second[k][w].wait_recv()
                total = p_ref[0, part(w, k)].astype(F32) + got1[w, 0, local(k)].astype(F32)
                total = total + got2[w, local(k)].astype(F32)
                rows = middle(w * half + k * size, size, total)
                if not shared:
                    o_ref[part(w, k)] = rows
                    continue
                o_ref[0, part(w, k)] = rows
                third[k].append([start(o_ref.at[0, part(w, k)], o_ref.at[step, part(w, k)], step, 5 + 2 * w + step, k)
                                 for step in (1, 2)])
                landed(0, w, k)
        if i >= 2 and shared:
            k = i - 2
            for w, (near, far) in enumerate(ways):
                third[k][w][far - 1].wait_recv()
                fourth.append(start(o_ref.at[far, part(w, k)], o_ref.at[3, part(w, k)], near, 10 + w, k))
                landed(far, w, k)
        if beside is not None:
            beside(i)
    for copy in copies:
        copy.wait_send()
    for k in range(subs if shared else 0):
        for w, (near, far) in enumerate(ways):
            third[k][w][near - 1].wait_recv()
            landed(near, w, k)
    for at, copy in enumerate(fourth):
        copy.wait_recv()
        landed(3, at % 2, at // 2)


def forward_relay_kernel(unit, subs, p_ref, x_ref, gain_ref, o_ref, resid_ref, got1, pass2, got2, ordered, *sems):
    def middle(at, size, total):
        rows = pl.ds(at, size)
        resid = total + x_ref[rows].astype(F32)
        resid_ref[rows] = resid
        normed = resid * lax.rsqrt(jnp.mean(resid * resid, axis=1, keepdims=True) + 1e-06) * gain_ref[...]
        half = normed.shape[1] // 2
        for j in range(half // unit):
            for k in (0, 1):
                ordered[:, k * half + j * unit:k * half + (j + 1) * unit] = normed[:, (2 * j + k) * unit:(2 * j + k + 1) * unit]
        return ordered[...].astype(BF16)

    relay(p_ref, o_ref, got1, pass2, got2, sems, subs, middle)


def norm_backward(unit, resid_ref, gain_ref, g_gain_ref, ordered, finish):
    g_gain_ref[...] = jnp.zeros_like(g_gain_ref)

    def middle(at, size, total):
        rows = pl.ds(at, size)
        half = total.shape[1] // 2
        for j in range(half // unit):
            for k in (0, 1):
                ordered[:, (2 * j + k) * unit:(2 * j + k + 1) * unit] = total[:, k * half + j * unit:k * half + (j + 1) * unit]
        d = ordered[...]
        resid = resid_ref[rows].astype(F32)
        scale = lax.rsqrt(jnp.mean(resid * resid, axis=1, keepdims=True) + 1e-06)
        unit_resid = resid * scale
        g_gain_ref[...] += jnp.sum(d * unit_resid, axis=0, keepdims=True)
        d = d * gain_ref[...]
        d = scale * (d - unit_resid * jnp.mean(d * unit_resid, axis=1, keepdims=True))
        return finish(rows, d)

    return middle


def backward_relay_kernel(unit, subs, parts, p_hbm, resid_hbm, cot_hbm, gain_ref, *refs):
    hidden_hbm, (branch_hbm, down_hbm, o_hbm, d_resid_hbm, g_gain_ref, g_down_hbm, kept_hbm, one_hbm, two_hbm, *refs) = refs[:parts], refs[parts:]
    (got1, pass2, got2, ordered, send_sem, recv_sem, hidden, branch, down, g_down, g_other, terms,
     in_sem, out_sem, core_send, core_recv, p_ref, resid_ref, cot_ref, o_ref, d_resid_ref, block_sem, resid_sem) = refs
    z, t, c = (lax.axis_index(a) for a in ALL)
    loads, at = [(p_hbm, p_ref), (resid_hbm, resid_ref), (cot_hbm, cot_ref)], 0
    for source in hidden_hbm:
        loads.append((source, hidden.at[:, at:at + source.shape[1]]))
        at += source.shape[1]
    loads += [(branch_hbm, branch), (down_hbm, down)]
    loads = [pltpu.make_async_copy(src, dst, in_sem.at[i]) for i, (src, dst) in enumerate(loads)]
    for copy in loads:
        copy.start()
    width = branch.shape[1] // subs
    _, zs, cs, count, _ = g_down.shape
    stores, crossings = [], []

    def beside(i):
        if i == 0:
            for copy in loads[1:]:
                copy.wait()
        cols = slice(i * width, (i + 1) * width)
        if i < subs:
            g = mm(hidden[...], branch[:, cols], TN).astype(BF16)
            for j in range(zs):
                for k in range(cs):
                    at = (j * cs + k) * count
                    g_down[i, j, k] = g[at:at + count]
            crossings.append(pltpu.make_async_remote_copy(
                src_ref=g_down.at[i, :, 1 - c], dst_ref=g_other.at[i], send_sem=core_send.at[i], recv_sem=core_recv.at[i],
                device_id=(z, t, 1 - c), device_id_type=pl.DeviceIdType.MESH))
            crossings[i].start()
            terms[i] = mm(hidden[...], down[:, cols], NN).astype(BF16)
            half = terms.shape[1] // (2 * TP)
            places = ((kept_hbm, 0, 0, 2), (kept_hbm, 2, 4, 1), (kept_hbm, 3, 3, 1),
                      (one_hbm, 0, 2, 1), (one_hbm, 1, 6, 1), (two_hbm, 0, 5, 1), (two_hbm, 1, 7, 1))
            for j, (target, at, low, size) in enumerate(places):
                stores.append(pltpu.make_async_copy(
                    terms.at[i, low * half:(low + size) * half], target.at[at * half:(at + size) * half, cols], out_sem.at[j, i]))
                stores[-1].start()
        if 1 <= i <= subs:
            k = i - 1
            crossings[k].wait()
            g_other[k] = (g_other[k].astype(F32) + g_down[k, :, c].astype(F32)).astype(BF16)
            stores.append(pltpu.make_async_copy(
                g_other.at[k], g_down_hbm.at[:, :, slice(k * width, (k + 1) * width)], out_sem.at[7, k]))
            stores[-1].start()

    def finish(rows, d):
        d = d + cot_ref[rows].astype(F32)
        d_resid_ref[rows] = d
        return d.astype(BF16)

    middle = norm_backward(unit, resid_ref, gain_ref, g_gain_ref, ordered, finish)
    part = o_ref.shape[1] // (2 * subs)

    def landed(block, w, i):
        rows = pl.ds((w * subs + i) * part, part)
        stores.append(pltpu.make_async_copy(o_ref.at[block, rows], o_hbm.at[block, rows], block_sem.at[block, w, i]))
        stores[-1].start()
        if block == 0:
            stores.append(pltpu.make_async_copy(d_resid_ref.at[rows], d_resid_hbm.at[rows], resid_sem.at[w, i]))
            stores[-1].start()

    relay(p_ref, o_ref, got1, pass2, got2, (send_sem, recv_sem), subs, middle, beside=beside, cores=True,
          source=p_hbm, ready=loads[0].wait, landed=landed)
    for copy in stores:
        copy.wait()


def settle_kernel(unit, subs, p_ref, x_ref, d_resid_ref, gain_ref, d_low_ref, f_low_ref, d_f_ref, g_head_ref,
                  g_mlp_ref, act_hbm, d_attn_hbm, h_hbm, o_ref, flat_ref, g_out_hbm,
                  got1, pass2, got2, ordered, send_sem, recv_sem,
                  act, d_attn, h, g_out, g_sum, g_gain_ref, in_sem, core_send, core_recv, swap_own, swap_send, swap_recv):
    z, t, c = (lax.axis_index(a) for a in ALL)
    loads = [pltpu.make_async_copy(src, dst, in_sem.at[i])
             for i, (src, dst) in enumerate([(act_hbm, act), (d_attn_hbm, d_attn), (h_hbm, h)])]
    for copy in loads:
        copy.start()
    crossing = pltpu.make_async_remote_copy(
        src_ref=g_out.at[:, :, 1 - c], dst_ref=g_sum, send_sem=core_send, recv_sem=core_recv,
        device_id=(z, t, 1 - c), device_id_type=pl.DeviceIdType.MESH)
    copies = []
    n = flat_ref.shape[0]
    deep, _, cs, rows, D = g_out.shape
    rank = f_low_ref.shape[1]

    def beside(i):
        if i == 0:
            for copy in loads:
                copy.wait()
            for low in range(0, D, D // 4):
                cols = slice(low, low + D // 4)
                g = mm(act[...], d_attn[:, cols], TN).astype(BF16)
                for j in range(deep):
                    for k in range(TP):
                        for m in range(cs):
                            at = ((j * TP + k) * cs + m) * rows
                            g_out[j, k, m, :, cols] = g[at:at + rows]
            crossing.start()
        if i == 1:
            crossing.wait()
            g_sum[...] = (g_sum[...].astype(F32) + g_out[:, :, c].astype(F32)).astype(BF16)
            for step in (3, 1, 2):
                peer = chip_peer(t, step)
                copies.append(pltpu.make_async_remote_copy(
                    src_ref=g_sum.at[:, peer], dst_ref=g_out_hbm.at[t], send_sem=swap_send.at[step - 1],
                    recv_sem=swap_recv.at[step - 1], device_id=(z, peer, c), device_id_type=pl.DeviceIdType.MESH))
                copies[-1].start()
            copies.append(pltpu.make_async_copy(g_sum.at[:, t], g_out_hbm.at[t], swap_own))
            copies[-1].start()
        if i == 2:
            flat_ref[...] = jnp.zeros_like(flat_ref)
            g_fd = mm(d_low_ref[...], h[...], TN)
            g_fu = mm(f_low_ref[...], d_f_ref[...], TN)
            zs = n // (TP * cs)
            each, wide = n // TP, g_fu.shape[1] * TP // n
            heads = g_head_ref.shape[1] // n
            for j in range(n):
                at = ((j % cs) * zs + j // (TP * cs)) * TP + j // cs % TP
                flat_ref[j, :rank, :unit] = g_fd[:, at * unit:(at + 1) * unit]
                flat_ref[j, rank:rank + 1, unit:unit + heads] = g_head_ref[:, j * heads:(j + 1) * heads]
                flat_ref[j, rank + 1:rank + 2, :unit] = g_mlp_ref[:, j * unit:(j + 1) * unit]
            for j in range(each):
                flat_ref[t * each + j, :rank, unit:unit + wide] = g_fu[:, j * wide:(j + 1) * wide]

    def finish(at, d):
        return (d + d_resid_ref[at]).astype(BF16)

    middle = norm_backward(unit, x_ref, gain_ref, g_gain_ref, ordered, finish)
    relay(p_ref, o_ref, got1, pass2, got2, (send_sem, recv_sem), subs, middle, False, beside, True, True)
    for j in range(n):
        flat_ref[j, rank:rank + 1, :unit] = g_gain_ref[:, j * unit:(j + 1) * unit]
    for copy in copies:
        copy.wait()


def relay_scratch(count, D, subs):
    half, size = count // 2, count // 2 // subs
    return [
        pltpu.VMEM((2, 2, half, D), BF16),
        pltpu.VMEM((2, half, D), BF16),
        pltpu.VMEM((2, half, D), BF16),
        pltpu.VMEM((size, D), F32),
        pltpu.SemaphoreType.DMA((12, subs)),
        pltpu.SemaphoreType.DMA((12, subs)),
    ]


SUBS = 4


def relay_forward(p, x, gain, unit, ident):
    _, count, D = p.shape
    fast = pl.BlockSpec(memory_space=pltpu.VMEM)
    return pl.pallas_call(
        functools.partial(forward_relay_kernel, unit, SUBS),
        out_shape=(jax.ShapeDtypeStruct(p.shape, BF16), jax.ShapeDtypeStruct(x.shape, F32)),
        in_specs=[fast] * 3,
        out_specs=(fast,) * 2,
        scratch_shapes=relay_scratch(count, D, SUBS),
        compiler_params=pltpu.CompilerParams(collective_id=ident, has_side_effects=True, vmem_limit_bytes=40 << 20),
        name="relay_forward",
    )(p, x, gain)


def relay_backward(p, resid, cot, gain, hidden, branch, down, unit, zs, cs, ident):
    _, count, D = p.shape
    tokens = hidden[0].shape[0]
    units = down.shape[0]
    width = D // SUBS
    each = units // (zs * cs)
    fast = pl.BlockSpec(memory_space=pltpu.VMEM)
    anywhere = pl.BlockSpec(memory_space=pl.ANY)
    return pl.pallas_call(
        functools.partial(backward_relay_kernel, unit, SUBS, len(hidden)),
        out_shape=(
            jax.ShapeDtypeStruct(p.shape, BF16),
            jax.ShapeDtypeStruct(resid.shape, F32),
            jax.ShapeDtypeStruct((1, D), F32),
            jax.ShapeDtypeStruct((zs, each, D), BF16),
        ) + tuple(jax.ShapeDtypeStruct((rows, D), BF16) for rows in (tokens // 2, tokens // 4, tokens // 4)),
        in_specs=[anywhere] * 3 + [fast] + [anywhere] * (len(hidden) + 2),
        out_specs=(anywhere,) * 2 + (fast,) + (anywhere,) * 4,
        scratch_shapes=relay_scratch(count, D, SUBS) + [
            pltpu.VMEM((tokens, units), BF16),
            pltpu.VMEM(branch.shape, BF16),
            pltpu.VMEM(down.shape, BF16),
            pltpu.VMEM((SUBS, zs, cs, each, width), BF16),
            pltpu.VMEM((SUBS, zs, each, width), BF16),
            pltpu.VMEM((SUBS, tokens, width), BF16),
            pltpu.SemaphoreType.DMA((len(hidden) + 5,)),
            pltpu.SemaphoreType.DMA((8, SUBS)),
            pltpu.SemaphoreType.DMA((SUBS,)),
            pltpu.SemaphoreType.DMA((SUBS,)),
            pltpu.VMEM(p.shape, BF16),
            pltpu.VMEM(resid.shape, F32),
            pltpu.VMEM(cot.shape, BF16),
            pltpu.VMEM(p.shape, BF16),
            pltpu.VMEM(resid.shape, F32),
            pltpu.SemaphoreType.DMA((TP, 2, SUBS)),
            pltpu.SemaphoreType.DMA((2, SUBS)),
        ],
        compiler_params=pltpu.CompilerParams(collective_id=ident, has_side_effects=True, vmem_limit_bytes=60 << 20),
        name="relay_backward",
    )(p, resid, cot, gain, *hidden, branch, down)


def settle(p, x, d_resid, gain, d_low, f_low, d_f, g_head, g_mlp, act, d_attn, h, unit, zs, cs, ident):
    _, count, D = p.shape
    fast = pl.BlockSpec(memory_space=pltpu.VMEM)
    anywhere = pl.BlockSpec(memory_space=pl.ANY)
    deep = zs // TP
    rank = f_low.shape[1]
    return pl.pallas_call(
        functools.partial(settle_kernel, unit, SUBS),
        out_shape=(
            jax.ShapeDtypeStruct(p.shape[1:], BF16),
            jax.ShapeDtypeStruct((zs * TP * cs, rank + 8, LANES), F32),
            jax.ShapeDtypeStruct((TP, deep, unit, D), BF16),
        ),
        in_specs=[fast] * 9 + [anywhere] * 3,
        out_specs=(fast,) * 2 + (anywhere,),
        scratch_shapes=relay_scratch(count, D, SUBS) + [
            pltpu.VMEM(act.shape, BF16),
            pltpu.VMEM(d_attn.shape, BF16),
            pltpu.VMEM(h.shape, BF16),
            pltpu.VMEM((deep, TP, cs, unit, D), BF16),
            pltpu.VMEM((deep, TP, unit, D), BF16),
            pltpu.VMEM((1, D), F32),
            pltpu.SemaphoreType.DMA((3,)),
            pltpu.SemaphoreType.DMA,
            pltpu.SemaphoreType.DMA,
            pltpu.SemaphoreType.DMA,
            pltpu.SemaphoreType.DMA((TP - 1,)),
            pltpu.SemaphoreType.DMA((TP - 1,)),
        ],
        compiler_params=pltpu.CompilerParams(collective_id=ident, has_side_effects=True, vmem_limit_bytes=56 << 20),
        name="settle",
    )(p, x, d_resid, gain, d_low, f_low, d_f, g_head, g_mlp, act, d_attn, h)


def ff_kernel(tile, hm_ref, gu_ref, d_hidden_ref, hidden_ref, d_gu_ref):
    for at in range(0, hm_ref.shape[0], tile):
        rows = slice(at, at + tile)
        pre = mm(hm_ref[rows, :], gu_ref[...], NN)
        gate, up = pre[:, :LANES], pre[:, LANES:]
        sig = 0.5 * jnp.tanh(0.5 * gate) + 0.5
        act = gate * sig
        d_hidden = d_hidden_ref[rows, :]
        hidden_ref[rows, :] = (act * up).astype(BF16)
        d_gu_ref[rows, :LANES] = (d_hidden * up * (sig + act * (1.0 - sig))).astype(BF16)
        d_gu_ref[rows, LANES:] = (d_hidden * act).astype(BF16)


def ff_forward(hm, gu, d_hidden, first):
    tokens, D = hm.shape
    columns = gu.shape[1]
    wide = pl.BlockSpec((tokens, 2 * LANES), lambda j: (0, j))
    return pl.pallas_call(
        functools.partial(ff_kernel, 1024),
        out_shape=(jax.ShapeDtypeStruct((tokens, columns // 2), BF16), jax.ShapeDtypeStruct((tokens, columns), BF16)),
        grid=(columns // (2 * LANES),),
        in_specs=[
            pl.BlockSpec((tokens, D), lambda j: (0, 0)),
            pl.BlockSpec((D, 2 * LANES), lambda j: (0, j)),
            pl.BlockSpec((tokens, LANES), lambda j: (0, j + first)),
        ],
        out_specs=(pl.BlockSpec((tokens, LANES), lambda j: (0, j)), wide),
        compiler_params=pltpu.CompilerParams(vmem_limit_bytes=48 << 20),
        name="feed_forward",
    )(hm, gu, d_hidden)


def d_hm_kernel(tile, count, *refs):
    grads, weights, o_ref = refs[:count], refs[count:2 * count], refs[2 * count]
    for at in range(0, o_ref.shape[0], tile):
        rows = slice(at, at + tile)
        o_ref[rows, :] = sum(mm(g[rows, :], w[...], NT) for g, w in zip(grads, weights)).astype(BF16)


def d_hm_product(grads, weights):
    tokens, D = grads[0].shape[0], weights[0].shape[0]
    width = 256
    return pl.pallas_call(
        functools.partial(d_hm_kernel, 1024, len(grads)),
        out_shape=jax.ShapeDtypeStruct((tokens, D), BF16),
        grid=(D // width,),
        in_specs=[pl.BlockSpec(g.shape, lambda j: (0, 0)) for g in grads]
        + [pl.BlockSpec((width, w.shape[1]), lambda j: (j, 0)) for w in weights],
        out_specs=pl.BlockSpec((tokens, width), lambda j: (0, j)),
        compiler_params=pltpu.CompilerParams(vmem_limit_bytes=48 << 20),
        name="d_hm",
    )(*grads, *weights)


def heads_kernel(steps, count, own_hbm, other_hbm, d_pre_hbm, *refs):
    blocks, (o_hbm, *refs) = refs[:count], refs[count:]
    returned, refs = refs[:count], refs[count:]
    (own, other, d_pre, sent, got, own_sem, back_send, back_recv, in_sem, out_sem, core_send, core_recv) = refs
    z, t, c = (lax.axis_index(a) for a in ALL)
    width = d_pre.shape[2]
    cols = [slice(i * width, (i + 1) * width) for i in range(steps)]
    loads = [pltpu.make_async_copy(other_hbm, other, in_sem.at[0])]
    loads += [pltpu.make_async_copy(d_pre_hbm.at[:, cols[i]], d_pre.at[i], in_sem.at[2 + i]) for i in range(steps)]
    loads += [pltpu.make_async_copy(own_hbm, own, in_sem.at[1])]
    for copy in loads:
        copy.start()
    barrier = pltpu.get_barrier_semaphore()
    for device in [(z, chip_peer(t, step), c) for step in (1, 2, 3)] + [(z, t, 1 - c)]:
        pl.semaphore_signal(barrier, inc=1, device_id=device, device_id_type=pl.DeviceIdType.MESH)
    pl.semaphore_wait(barrier, TP)
    copies = send_blocks(blocks, returned, own_sem, back_send, back_recv)
    crossings = []
    loads[0].wait()
    for i in range(steps):
        loads[1 + i].wait()
        sent[i] = mm(other[...], d_pre[i], TN).astype(BF16)
        crossings.append(pltpu.make_async_remote_copy(
            src_ref=sent.at[i], dst_ref=got.at[i], send_sem=core_send.at[i], recv_sem=core_recv.at[i],
            device_id=(z, t, 1 - c), device_id_type=pl.DeviceIdType.MESH))
        crossings[i].start()
    loads[-1].wait()
    for i in range(steps):
        g = mm(own[...], d_pre[i], TN)
        crossings[i].wait_recv()
        got[i] = (g + got[i].astype(F32)).astype(BF16)
        copies.append(pltpu.make_async_copy(got.at[i], o_hbm.at[:, cols[i]], out_sem.at[i]))
        copies[-1].start()
    for copy in crossings:
        copy.wait_send()
    for copy in copies:
        copy.wait()


def heads_gradient(own, other, d_pre, blocks, ident):
    tokens, half = own.shape
    columns = d_pre.shape[1]
    steps = 4
    width = columns // steps
    count = len(blocks)
    anywhere = pl.BlockSpec(memory_space=pl.ANY)
    return pl.pallas_call(
        functools.partial(heads_kernel, steps, count),
        out_shape=(jax.ShapeDtypeStruct((half, columns), BF16),)
        + tuple(jax.ShapeDtypeStruct(b.shape, b.dtype) for b in blocks),
        in_specs=[anywhere] * (3 + count),
        out_specs=(anywhere,) * (1 + count),
        scratch_shapes=[
            pltpu.VMEM((tokens, half), BF16),
            pltpu.VMEM((tokens, half), BF16),
            pltpu.VMEM((steps, tokens, width), BF16),
            pltpu.VMEM((steps, half, width), BF16),
            pltpu.VMEM((steps, half, width), BF16),
        ] + block_sems(count) + [
            pltpu.SemaphoreType.DMA((2 + steps,)),
            pltpu.SemaphoreType.DMA((steps,)),
            pltpu.SemaphoreType.DMA((steps,)),
            pltpu.SemaphoreType.DMA((steps,)),
        ],
        compiler_params=pltpu.CompilerParams(collective_id=ident, has_side_effects=True, vmem_limit_bytes=56 << 20),
        name="heads_gradient",
    )(own, other, d_pre, *blocks)


def send_t(x, step):
    return lax.ppermute(x, "t", [(i, i ^ step) for i in range(TP)])


def send_c(x):
    return lax.ppermute(x, "c", [(0, 1), (1, 0)])


def gather_t_begin(x):
    return send_t(x, 1), send_t(x, 2)


def gather_t_end(x, one, two):
    half = x.shape[0] // 2
    return jnp.concatenate([x, one, two, send_t(two[:half], 1), send_t(one[half:], 2)], axis=0)


def scatter_t_middle(kept, got):
    half = kept.shape[0] // 4
    first, second = got

    def add(low, v):
        return kept[low:low + half].astype(F32) + v.astype(F32)

    part = jnp.concatenate([add(0, first[:half]), add(half, second[:half])], axis=0)
    return part, (add(2 * half, first[half:]).astype(BF16), add(3 * half, second[half:]).astype(BF16))


def scatter_t_pass(passed):
    return send_t(passed[0], 2), send_t(passed[1], 1)


def swap_t(x):
    t = lax.axis_index("t")

    def block(a, j):
        return lax.dynamic_index_in_dim(a, j, 0, keepdims=False)

    got = jnp.stack([block(x, t)] + [send_t(block(x, t ^ k), k) for k in (1, 2, 3)])
    return jnp.stack([block(got, t ^ j) for j in range(TP)])


def dot(left, right):
    return mm(left, right, NN)


def dot_nt(left, right):
    return mm(left, right, NT)


def dot_tn(left, right):
    return mm(left, right, TN)


def after(x, *others):
    return lax.optimization_barrier((x,) + others)[:2]


def rms_norm(v, gain):
    return v * lax.rsqrt(jnp.mean(v * v, axis=-1, keepdims=True) + 1e-06) * gain


def swiglu(gate_val, up_val):
    return jax.nn.silu(gate_val) * up_val


def per_device(zs, cs, tokens, starts, w_query, w_key, w_value, w_gate_out, w_out, w_forget_down,
               w_forget_up, norm_attn, norm_head, norm_mlp, w_gate, w_up, w_down, cotangent):
    seqs, seq_len, D = tokens.shape
    n = zs * TP * cs
    rows = w_query.shape[0]
    ff_rows = w_down.shape[0]
    rank = w_forget_down.shape[1]
    fu_cols = w_forget_up.shape[1]
    mine = seqs * seq_len
    half = D // cs
    t_idx, c_idx = lax.axis_index("t"), lax.axis_index("c")

    def to_k(v):
        return v.reshape(-1, zs, TP, cs, rows).transpose(0, 3, 1, 2, 4).reshape(-1, D)

    def from_k(v):
        return v.reshape(-1, cs, zs, TP, rows).transpose(0, 2, 3, 1, 4).reshape(-1, D)

    def sum_z(v):
        return lax.psum_scatter(v, "z", scatter_dimension=0, tiled=True)

    def core_half(v, core):
        return lax.dynamic_slice_in_dim(v, core * half, half, axis=1)

    def other_term(left, right):
        return dot_tn(left, right).astype(BF16)

    def own_term(left, right, other):
        return (dot_tn(left, right) + send_c(other).astype(F32)).astype(BF16)

    docs = jnp.cumsum(starts, axis=1).astype(BF16)
    small = pack_rows([w_forget_down.reshape(-1), w_forget_up.reshape(-1), norm_attn, norm_head, norm_mlp,
                       docs.reshape(-1)], 16)
    sizes = [rows * rank, rank * fu_cols, norm_attn.shape[0], norm_head.shape[0], norm_mlp.shape[0]]
    by_rows = lax.all_gather(jnp.concatenate([w_out, w_down], axis=0), ("z", "c"), axis=0, tiled=True)
    by_rows = by_rows.reshape(zs, cs, rows + ff_rows, D)
    cot = cotangent.reshape(mine, D)
    w4 = spread([w_query, w_key, w_value, w_gate_out], 0)
    small, w4 = after(small, w4)
    small = share(small, n, cs, 9)
    piece = cs * ff_rows
    units = zs * piece
    middle = units // LANES // 2 * 2 * LANES
    parts = ((0, middle), (middle, 2 * units))
    w_gate, small = after(w_gate, small)
    gus = spread_ff(w_gate, w_up, piece, parts, 2)
    pieces = cut(small.reshape(n, -1), sizes + [mine])
    wfd = to_k(pieces[0].reshape(D, rank).T).T
    wfu = pieces[1].reshape(n, rank, fu_cols).transpose(1, 0, 2).reshape(rank, n * fu_cols)
    wfu = lax.dynamic_slice_in_dim(wfu, t_idx * SLOTS, SLOTS, axis=1)
    gain_attn = pieces[2].reshape(-1).astype(F32)
    gain_head = pieces[3].reshape(1, -1).astype(F32)
    gain_mlp = pieces[4].reshape(1, -1).astype(F32)
    all_docs = pieces[5].reshape(zs, TP, cs, mine)
    all_docs = lax.dynamic_index_in_dim(all_docs, lax.axis_index("z"), 0, keepdims=False)
    all_docs = lax.dynamic_index_in_dim(all_docs, lax.axis_index("c"), 1, keepdims=False)
    docs = jnp.concatenate([lax.dynamic_index_in_dim(all_docs, t_idx ^ k, 0) for k in range(TP)], axis=0)
    docs = docs.astype(F32).reshape(TP * seqs, seq_len)

    def by_columns(w):
        return lax.all_gather(w.reshape(TP * rows, -1), ("c", "z"), axis=0, tiled=True)

    w4 = by_columns(w4)
    gus = [by_columns(gu) for gu in gus]
    down = by_rows[:, :, rows:].reshape(-1, D)
    wo = swap_t(by_rows[:, :, :rows].reshape(TP, -1, rows, D)).reshape(TP, zs // TP, cs, rows, D)
    wo = wo.transpose(1, 0, 2, 3, 4).reshape(HEAD, D)

    x = tokens.reshape(mine, D).astype(F32)
    normed_in, norm_in_back = jax.vjp(rms_norm, x, gain_attn)
    h = to_k(normed_in.astype(BF16))
    h = gather_t_end(h, *gather_t_begin(h))
    d_branch = gather_t_end(cot, *gather_t_begin(cot))
    d_hidden = dot_nt(d_branch, down)
    h, d_hidden = after(h, d_hidden)
    h, wo = after(h, wo)
    h_own, h_other = after(core_half(h, c_idx), core_half(h, 1 - c_idx))
    h, h_own = after(h, h_own)
    pre = dot(h, w4)
    f_low = dot(h, wfd).astype(BF16)
    act = slots_forward(pre, f_low, wfu, gain_head, docs)
    terms = dot(act, wo).astype(BF16)
    tokens_flat = tokens.reshape(mine, D)
    hm, resid = relay_forward(terms.reshape(TP, mine, D), tokens_flat, gain_mlp, rows, 6)
    hm = hm.reshape(TP * mine, D)

    hidden, d_gus, g_gus = [], [], []
    for gu, (low, high) in zip(gus, parts):
        part, d_gu = ff_forward(hm, gu, d_hidden, low // (2 * LANES))
        hidden.append(part)
        d_gus.append(d_gu)
        g_gu = other_term(core_half(hm, 1 - c_idx), d_gu)
        if high == 2 * units:
            d_gus[-1], _ = after(d_gu, g_gu)
            d_hm = d_hm_product(d_gus, gus)
            hm, _ = after(hm, d_hm)
        g_gu = own_term(core_half(hm, c_idx), d_gu, g_gu)
        hm, g_gu = after(hm, g_gu)
        g_gus.append(sum_z(g_gu).reshape(TP, rows, -1))
    d_hm, _ = after(d_hm, g_gu)
    d_attn, d_resid, g_norm_mlp, g_down, *branch = relay_backward(
        d_hm.reshape(TP, mine, D), resid, cot, gain_mlp, hidden, d_branch, down, rows, zs, cs, 7)
    d_attn = d_attn.reshape(TP * mine, D)
    g_down = sum_z(g_down.reshape(-1, D))

    d_attn, g_gus[0] = after(d_attn, g_gus[0])
    d_attn, g_gus[1] = after(d_attn, g_gus[1])
    first = send_t(branch[1], 1), send_t(branch[2], 2)
    d_act = dot_nt(d_attn, wo).astype(BF16)
    count = TP * seqs
    ahead = count * 5 // 8
    *begun, g_norm_head = slots_backward(pre, f_low, wfu, gain_head, docs, d_act, 0, ahead)
    first, begun = after(first, begun)
    part, passed = scatter_t_middle(branch[0], first)
    d_act, passed = after(d_act, passed)
    second = scatter_t_pass(passed)
    d_pre, d_f, d_low, g_more = slots_backward(
        pre, f_low, wfu, gain_head, docs, d_act, ahead, count - ahead, begun)
    g_norm_head = g_norm_head + g_more
    d_pre, second = after(d_pre, second)
    g4, *g_gus = heads_gradient(h_own, h_other, d_pre, g_gus, 3)
    d_pre, _ = after(d_pre, g4)
    d_pre, g_down = after(d_pre, g_down)
    g4 = sum_z(g4)
    d_h = (dot_nt(d_pre, w4) + dot_nt(d_low, wfd)).astype(BF16)
    tokens_grad, flat, g_out = settle(
        d_h.reshape(TP, mine, D), tokens_flat, d_resid, gain_attn.reshape(1, D), d_low, f_low, d_f, g_norm_head,
        g_norm_mlp, act, d_attn, h, rows, zs, cs, 8)
    g_out = sum_z(g_out.reshape(-1, D))

    second, tokens_grad = after(second, tokens_grad)
    mixed = (resid + part + jnp.concatenate(second, axis=0).astype(F32)).astype(BF16)
    g_gate, g_up = widen(g_gus, ff_moves(piece, units, parts), 2, n * ff_rows)
    g_down = g_down.astype(F32)
    g4, mixed, tokens_grad, g_gate, g_up, g_down = lax.optimization_barrier(
        (g4, mixed, tokens_grad, g_gate, g_up, g_down))
    small, g4 = finish(flat, g4.reshape(TP, rows, -1), n, cs)
    heads = norm_head.shape[0]
    head_moves = [(i, j * HEAD, 0, j, i * HEAD, HEAD) for i in range(4) for j in range(TP)]
    g_heads, g_out = after(widen([g4], head_moves, 4, D), g_out)
    g_query, g_key, g_value, g_gate_out = g_heads
    g_out = g_out.astype(F32)
    return (
        mixed.reshape(tokens.shape),
        tokens_grad.reshape(tokens.shape),
        g_query, g_key, g_value, g_gate_out,
        g_out,
        small[:rank, :rows].T,
        small[:rank, rows:rows + fu_cols],
        small[rank, :rows],
        small[rank, rows:rows + heads],
        small[rank + 1, :rows],
        g_gate, g_up,
        g_down,
    )


def solution(mesh):
    cs = mesh.shape["outer"]
    zs = mesh.shape["dp"] // TP
    grid = Mesh(mesh.devices.reshape(zs, TP, cs), ALL)
    whole, row, vec = P(ALL, None, None), P(ALL, None), P(ALL)
    cols = P(None, ALL)

    def body(*args):
        return per_device(zs, cs, *args)

    return jax.shard_map(
        body,
        mesh=grid,
        in_specs=(whole, row, row, row, row, row, row, row, cols, vec, vec, vec, row, row, row, whole),
        out_specs=(whole, whole, row, row, row, row, row, row, cols, vec, vec, vec, row, row, row),
        check_vma=False,
    )
```
